32 devices in a mesh: dp: 16 (over z, x, core), tensor: 2 (over y).
Axes of the slice: x: 2, y: 2, z: 4, core: 2. Of those that a mesh axis runs over, the one named last changes fastest.
Arguments:
- hidden_in: bfloat16 [24576, 1024], P(('dp', 'tensor')), may hold values from -6 to 6
- norm_gain: bfloat16 [1024], P('dp'), may hold values from 0.5 to 1.5
- projection_gate_inner: bfloat16 [1024, 2, 2048], P('dp', None, 'tensor'), may hold values from -0.1875 to 0.1875
- proj_state: bfloat16 [1024, 256], P('dp'), may hold values from -0.1875 to 0.1875
- proj_step: bfloat16 [1024, 32], P('dp', 'tensor'), may hold values from -0.09375 to 0.09375
- conv_inner: bfloat16 [4, 2, 1024], P(None, 'tensor', 'dp'), may hold values from -3 to 3
- conv_inner_bias: bfloat16 [2, 1024], P('tensor', 'dp'), may hold values from -3 to 3
- conv_state: bfloat16 [4, 256], P(None, 'dp'), may hold values from -3 to 3
- conv_state_bias: bfloat16 [256], P('dp'), may hold values from -3 to 3
- decay_log: bfloat16 [32], P('tensor'), may hold values from 0 to 2.75
- skip_gain: bfloat16 [32], P('tensor'), may hold values from 0.5 to 1.5
- step_bias: bfloat16 [32], P('tensor'), may hold values from -4.5 to -1.5
- gate_gain: bfloat16 [2, 1024], P('tensor', 'dp'), may hold values from 0.5 to 1.5
- proj_out: bfloat16 [2048, 1024], P('tensor', 'dp'), may hold values from -0.125 to 0.125
- lengths: int32 [16, 4], P('dp'), may hold values from 0 to 1536, as said below
- cotangent: bfloat16 [24576, 1024], P(('dp', 'tensor')), may hold values from -6 to 6
Outputs:
- block_out: bfloat16 [24576, 1024], P(('dp', 'tensor'))
- grad_hidden: float32 [24576, 1024], P(('dp', 'tensor'))
- grad_norm_gain: float32 [1024], P('dp')
- grad_proj_gate_inner: float32 [1024, 2, 2048], P('dp', None, 'tensor')
- grad_proj_state: float32 [1024, 256], P('dp')
- grad_proj_step: float32 [1024, 32], P('dp', 'tensor')
- grad_conv_inner: float32 [4, 2, 1024], P(None, 'tensor', 'dp')
- grad_conv_inner_bias: float32 [2, 1024], P('tensor', 'dp')
- grad_conv_state: float32 [4, 256], P(None, 'dp')
- grad_conv_state_bias: float32 [256], P('dp')
- grad_decay_log: float32 [32], P('tensor')
- grad_skip_gain: float32 [32], P('tensor')
- grad_step_bias: float32 [32], P('tensor')
- grad_gate_gain: float32 [2, 1024], P('tensor', 'dp')
- grad_proj_out: float32 [2048, 1024], P('tensor', 'dp')
The draws below stay inside these ranges and needn't reach their ends.
Inputs may be any that keep to these rules, and one draw needn't show every extreme that they name: Row d lists the lengths of the sequences packed from the start of block d; each row sums to at most 1536; in every draw some row is one sequence of 1536 tokens.
All inputs are finite; a program needn't handle non-finite values.
Results may differ from the reference program's by a relative error of at most 0.012.
Values may be sent and summed in bfloat16 or wider, within the bound.
No kernel may reach another device: no remote copies, remote signals or barrier semaphores. Data moves between devices by JAX's collectives and lax.ppermute only.
A program may use at most 192 MiB of HBM per device.

```python
import jax
import jax.numpy as jnp
from jax import lax

D = 1024
INNER = 2048
HEADS = 32
HEADDIM = 64
STATE = 128
KCONV = 4
GROUP = 256
SLOTS = 4
TOK_DEV = 1536
TOKENS = 24576
N_DP = 16


def draw_lengths(key, part):
    key = jax.random.fold_in(key, 7)
    first_key, second_key = jax.random.split(key)
    devices = TOKENS // TOK_DEV
    spread_rows = jax.random.randint(first_key, (devices, SLOTS), TOK_DEV // (2 * SLOTS), TOK_DEV // SLOTS + 1, dtype=jnp.int32)
    busiest = jax.random.randint(second_key, (), 0, devices, dtype=jnp.int32)
    single_row = jnp.zeros((SLOTS,), jnp.int32).at[0].set(TOK_DEV)
    device_index = jnp.arange(devices, dtype=jnp.int32)
    return jnp.where((device_index == busiest)[:, None], single_row[None, :], spread_rows)


def steps_of(rng, dims, cuts, least, top_value):
    def one(dim, parts):
        draws = jax.random.uniform(jax.random.fold_in(jax.random.fold_in(rng, 6), dim), (parts,), jnp.float32, least / len(cuts), top_value / len(cuts))
        return jnp.repeat(jnp.exp(draws), dims[dim] // parts).reshape((-1,) + (1,) * (len(dims) - dim - 1))

    factor_of = one(*cuts[0])
    for cut in cuts[1:]:
        factor_of = factor_of * one(*cut)
    return factor_of


def scatter_about(rng, extent, deviation, most, cuts=(), held_as=jnp.bfloat16):
    values = jax.random.normal(rng, extent, jnp.float32) * deviation
    if len(cuts) > 0:
        values = steps_of(rng, extent, cuts, -0.22, 0.18) * values
    return jnp.clip(values, min=-most, max=most).astype(held_as)


def setup_inputs(seed: int = 0) -> dict:
    keys = jax.random.split(jax.random.key(seed), 17)
    hidden_in = scatter_about(keys[0], (TOKENS, D), 1.0, 6.0, ((0, 32),))
    norm_gain = jnp.clip(1.0 + 0.1 * jax.random.normal(keys[1], (D,), jnp.float32), 0.5, 1.5).astype(jnp.bfloat16)
    projection_gate_inner = scatter_about(keys[2], (D, 2, INNER), D ** -0.5, 0.1875, ((0, 16), (2, 2)))
    proj_state = scatter_about(keys[3], (D, 2 * STATE), D ** -0.5, 0.1875, ((0, 16),))
    proj_step = scatter_about(keys[4], (D, HEADS), (4 * D) ** -0.5, 0.09375, ((0, 16), (1, 2)))
    conv_inner = scatter_about(keys[5], (KCONV, 2, INNER // 2), KCONV ** -0.5, 3.0, ((1, 2), (2, 16)))
    conv_inner_bias = scatter_about(keys[6], (2, INNER // 2), 0.5, 3.0, ((0, 2), (1, 16)))
    conv_state = scatter_about(keys[7], (KCONV, 2 * STATE), KCONV ** -0.5, 3.0, ((1, 16),))
    conv_state_bias = scatter_about(keys[8], (2 * STATE,), 0.5, 3.0, ((0, 16),))
    decay_log = jnp.clip(2.75 * jax.random.uniform(keys[9], (HEADS,), jnp.float32) ** steps_of(keys[9], (HEADS,), ((0, 2),), -0.2, 0.2), 0.0, 2.75).astype(jnp.bfloat16)
    skip_gain = jnp.clip(0.5 + 1.0 * jax.random.uniform(keys[10], (HEADS,), jnp.float32) ** steps_of(keys[10], (HEADS,), ((0, 2),), -0.2, 0.2), 0.5, 1.5).astype(jnp.bfloat16)
    step_bias = jnp.clip(-4.5 + 3.0 * jax.random.uniform(keys[11], (HEADS,), jnp.float32) ** steps_of(keys[11], (HEADS,), ((0, 2),), -0.2, 0.2), -4.5, -1.5).astype(jnp.bfloat16)
    gate_gain = jnp.clip(1.0 + 0.1 * jax.random.normal(keys[12], (2, INNER // 2), jnp.float32), 0.5, 1.5).astype(jnp.bfloat16)
    proj_out = scatter_about(keys[13], (INNER, D), INNER ** -0.5, 0.125, ((0, 2), (1, 16)))
    lengths = draw_lengths(jax.random.fold_in(keys[16], 71), 0)
    cotangent = scatter_about(keys[15], (TOKENS, D), 1.0, 6.0, ((0, 32),))
    return dict(hidden_in=hidden_in, norm_gain=norm_gain, projection_gate_inner=projection_gate_inner, proj_state=proj_state, proj_step=proj_step, conv_inner=conv_inner, conv_inner_bias=conv_inner_bias, conv_state=conv_state, conv_state_bias=conv_state_bias, decay_log=decay_log, skip_gain=skip_gain, step_bias=step_bias, gate_gain=gate_gain, proj_out=proj_out, lengths=lengths, cotangent=cotangent)


@jax.custom_vjp
def low(v):
    return lax.optimization_barrier(v.astype(jnp.bfloat16)).astype(jnp.float32)

@jax.custom_vjp
def reduced_backward_input(v):
    return v

def low_keep(v):
    return (low(v), None)

def low_pass(kept, grad):
    return (grad,)

def back_keep(v):
    return (v, None)

def back_low(kept, grad):
    return (low(grad),)
low.defvjp(low_keep, low_pass)
reduced_backward_input.defvjp(back_keep, back_low)
norm_eps = 1e-05
highest_precision_mode = lax.Precision.HIGHEST

def sequence_layout(lengths_row, block_len):
    places = jnp.arange(block_len, dtype=jnp.int32)
    seq_ends = jnp.cumsum(lengths_row).astype(jnp.int32)
    starts = (seq_ends - lengths_row).astype(jnp.int32)
    seq_ids = lax.optimization_barrier(jnp.sum((places[:, None] >= seq_ends[None, :]).astype(jnp.int32), axis=1)).astype(jnp.int32)
    slot_count = lengths_row.shape[0]
    bounds = jnp.concatenate([starts, seq_ends[-1:]])
    labels = jnp.arange(slot_count + 1, dtype=jnp.int32)
    own_start = lax.optimization_barrier(jnp.sum(jnp.where(seq_ids[:, None] == labels[None, :], bounds[None, :], 0), axis=1)).astype(jnp.int32)
    return (seq_ids, places - own_start, seq_ids < slot_count)

def group_masks(seq_ids, group_count, group_len):
    seq_groups = seq_ids.reshape(group_count, group_len)
    tail_ids = seq_groups[:, -1]
    inner_index = jnp.arange(group_len, dtype=jnp.int32)
    intra_mask = (seq_groups[:, :, None] == seq_groups[:, None, :]) & (inner_index[:, None] >= inner_index[None, :])[None]
    tail_mask = seq_groups == tail_ids[:, None]
    prev_tail = jnp.concatenate([jnp.full((1,), -1, jnp.int32), tail_ids[:-1]])
    enter_mask = seq_groups == prev_tail[:, None]
    carry_mask = tail_ids == prev_tail
    return (intra_mask, tail_mask, enter_mask, carry_mask)

def causal_conv(values, kernel, offset_row, position):
    steps_all = kernel.shape[0]
    channels = values.shape[1]
    summed = offset_row[None, :] + kernel[steps_all - 1][None, :] * values
    for offset in range(1, steps_all):
        earlier = jnp.concatenate([jnp.zeros((offset, channels), values.dtype), values[:-offset]], axis=0)
        summed = summed + jnp.where(position[:, None] >= offset, kernel[steps_all - 1 - offset][None, :] * earlier, 0.0)
    return summed

def mixer_block(inner_pre, state_pre, step_pre, lengths_row, kernel_inner, bias_inner, conv_state, conv_state_bias, decay_log, skip_gain, step_bias):
    seq_ids, position, valid_rows = sequence_layout(lengths_row, TOK_DEV)
    inner_act = low(jax.nn.silu(causal_conv(inner_pre, kernel_inner, bias_inner, position)))
    state_act = low(jax.nn.silu(causal_conv(state_pre, conv_state, conv_state_bias, position)))
    group_count = TOK_DEV // GROUP
    keys_c = state_act[:, :STATE].reshape(group_count, GROUP, STATE)
    queries_c = state_act[:, STATE:].reshape(group_count, GROUP, STATE)
    step_size = jax.nn.softplus(step_pre + step_bias[None, :])
    cum_decay = jnp.cumsum(step_size * (-jnp.exp(decay_log))[None, :], axis=0)
    intra_mask, tail_mask, enter_mask, carry_mask = group_masks(seq_ids, group_count, GROUP)
    scores = jnp.einsum('ctn,csn->cts', queries_c, keys_c, precision=highest_precision_mode)
    cum_c = cum_decay.T.reshape(HEADS, group_count, GROUP)
    step_c = step_size.T.reshape(HEADS, group_count, GROUP)
    last_cum = cum_c[:, :, -1]
    prev_cum = jnp.concatenate([jnp.zeros((HEADS, 1), jnp.float32), last_cum[:, :-1]], axis=1)
    log_gap = cum_c[:, :, :, None] - cum_c[:, :, None, :]
    factor = jnp.exp(jnp.where(intra_mask[None], log_gap, 0.0))
    weights = low(jnp.where(intra_mask[None], factor * scores[None] * step_c[:, :, None, :], 0.0))
    values_c = inner_act.reshape(group_count, GROUP, HEADS, HEADDIM)
    intra_part = jnp.einsum('hcts,cshp->cthp', weights, values_c, precision=highest_precision_mode)
    key_factor = jnp.where(tail_mask[None], jnp.exp(last_cum[:, :, None] - cum_c), 0.0)
    decayed = low((key_factor * step_c)[:, :, :, None] * keys_c[None])
    group_state = jnp.einsum('hcsn,cshp->chnp', decayed, values_c, precision=highest_precision_mode)
    state_decay = jnp.where(carry_mask[None], jnp.exp(last_cum - prev_cum), 0.0)

    def advance(state_now, pieces):
        return (pieces[0][:, None, None] * state_now + pieces[1], state_now)
    final_state, prev_states = lax.scan(advance, jnp.zeros((HEADS, STATE, HEADDIM), jnp.float32), (state_decay.T, group_state))
    query_factor = jnp.where(enter_mask[None], jnp.exp(cum_c - prev_cum[:, :, None]), 0.0)
    inter_part = jnp.einsum('ctn,chnp->cthp', queries_c, prev_states, precision=highest_precision_mode) * query_factor.transpose(1, 2, 0)[:, :, :, None]
    mixed = reduced_backward_input(intra_part + inter_part).reshape(TOK_DEV, HEADS, HEADDIM)
    values = inner_act.reshape(TOK_DEV, HEADS, HEADDIM)
    return (mixed + skip_gain[None, :, None] * values).reshape(TOK_DEV, INNER)

def reference(hidden_in, norm_gain, projection_gate_inner, proj_state, proj_step, conv_inner, conv_inner_bias, conv_state, conv_state_bias, decay_log, skip_gain, step_bias, gate_gain, proj_out, lengths, cotangent):
    floats = [item.astype(jnp.float32) for item in (hidden_in, norm_gain, projection_gate_inner, proj_state, proj_step, conv_inner, conv_inner_bias, conv_state, conv_state_bias, decay_log, skip_gain, step_bias, gate_gain, proj_out)]
    seq_valid = jax.vmap(lambda row_lengths: sequence_layout(row_lengths, TOK_DEV)[2])(lengths).reshape(TOKENS)

    def forward(hidden, norm_gain, projection_gate_inner, proj_state, proj_step, conv_inner, conv_inner_bias, conv_state, conv_state_bias, decay_log, skip_gain, step_bias, gate_gain, proj_out):
        inv_rms = lax.rsqrt(lax.optimization_barrier(jnp.mean(hidden * hidden, axis=1, keepdims=True)) + norm_eps)
        normalized_rows = low(hidden * inv_rms * norm_gain[None, :])
        gate_inner_preactivation = reduced_backward_input(jnp.einsum('hk,kyz->hyz', normalized_rows, projection_gate_inner, precision=highest_precision_mode))
        state_pre = reduced_backward_input(jnp.dot(normalized_rows, proj_state, precision=highest_precision_mode))
        step_pre = reduced_backward_input(jnp.dot(normalized_rows, proj_step, precision=highest_precision_mode))
        kernel_inner = conv_inner.reshape(KCONV, INNER)
        bias_inner = conv_inner_bias.reshape(INNER)
        mixer_saved = jax.checkpoint(mixer_block)

        def one_block(pieces):
            return mixer_saved(pieces[0], pieces[1], pieces[2], pieces[3], kernel_inner, bias_inner, conv_state, conv_state_bias, decay_log, skip_gain, step_bias)
        mixed = lax.map(one_block, (gate_inner_preactivation[:, 1].reshape(N_DP, TOK_DEV, INNER), state_pre.reshape(N_DP, TOK_DEV, 2 * STATE), step_pre.reshape(N_DP, TOK_DEV, HEADS), lengths))
        mixed = mixed.reshape(TOKENS, INNER)
        gated = mixed * jax.nn.silu(gate_inner_preactivation[:, 0])
        inv_gate = lax.rsqrt(lax.optimization_barrier(jnp.mean(gated * gated, axis=1, keepdims=True)) + norm_eps)
        out_low = low(gated * inv_gate * gate_gain.reshape(INNER)[None, :])
        return hidden + jnp.where(seq_valid[:, None], jnp.dot(out_low, proj_out, precision=highest_precision_mode), 0.0)
    result, pullback = jax.vjp(forward, *floats)
    gradients = pullback(cotangent.astype(jnp.float32))
    return (result.astype(jnp.bfloat16), gradients[0], gradients[1], gradients[2], gradients[3], gradients[4], gradients[5], gradients[6], gradients[7], gradients[8], gradients[9], gradients[10], gradients[11], gradients[12], gradients[13])
```

```python
import functools

import jax
import jax.numpy as jnp
from jax import lax
from jax.experimental import pallas as pl
from jax.experimental.pallas import tpu as pltpu
from jax.sharding import PartitionSpec as P

GROUP = 256
HALF = GROUP // 2
LANES = 128
PAIR_HEADS = 2
NORM_EPS = 1e-05
LOG2E = 1.4426950408889634
MASKED = -1e30
VMEM_BYTES = 56 * 1024 * 1024

F32 = jnp.float32
BF16 = jnp.bfloat16

ROW_NORM, ROW_TAP, ROW_BIAS, ROW_GATE, ROW_SKIP = 0, 1, 5, 6, 7


def nn(left, right):
    return lax.dot_general(left, right, (((1,), (0,)), ((), ())), preferred_element_type=F32)


def nt(left, right):
    return lax.dot_general(left, right, (((1,), (1,)), ((), ())), preferred_element_type=F32)


def tn(left, right):
    return lax.dot_general(left, right, (((0,), (0,)), ((), ())), preferred_element_type=F32)


def split3(value):
    high = value.astype(BF16)
    rest = value - high.astype(F32)
    mid = rest.astype(BF16)
    low = (rest - mid.astype(F32)).astype(BF16)
    return high, mid, low


def exact_left(ones, value):
    high, mid, low = split3(value)
    return nn(ones, high) + nn(ones, mid) + nn(ones, low)


def three_in_lanes(value, heads):
    high, mid, low = split3(value)
    lane = lax.broadcasted_iota(jnp.int32, value.shape, 1)
    parts = jnp.where(
        lane < heads,
        high.astype(F32),
        jnp.where(lane < 2 * heads, mid.astype(F32), low.astype(F32)),
    )
    return parts.astype(BF16)


def spread_matrix(heads, head_size):
    shape = (LANES, heads * head_size)
    lane = lax.broadcasted_iota(jnp.int32, shape, 0)
    channel = lax.broadcasted_iota(jnp.int32, shape, 1)
    owner = channel // head_size
    hit = (lane == owner) | (lane == owner + heads) | (lane == owner + 2 * heads)
    return hit.astype(F32).astype(BF16)


def collect_matrix(heads, head_size):
    shape = (heads * head_size, LANES)
    lane = lax.broadcasted_iota(jnp.int32, shape, 1)
    owner = lax.broadcasted_iota(jnp.int32, shape, 0) // head_size
    hit = (lane == owner) | (lane == owner + heads) | (lane == owner + 2 * heads)
    return hit.astype(F32).astype(BF16)


def lower_matrix(upper=False):
    row = lax.broadcasted_iota(jnp.int32, (GROUP, GROUP), 0)
    col = lax.broadcasted_iota(jnp.int32, (GROUP, GROUP), 1)
    hit = (col >= row) if upper else (col <= row)
    return hit.astype(F32).astype(BF16)


def sequence_ends(len_ref):
    ends, total = [], jnp.int32(0)
    for slot in range(len_ref.shape[1]):
        total = total + len_ref[0, slot]
        ends.append(total)
    return ends


def sequence_of(ends, token):
    found = (token >= ends[0]).astype(jnp.int32)
    for end in ends[1:]:
        found = found + (token >= end).astype(jnp.int32)
    return found


def scalar_sequence_of(ends, token):
    found = jnp.where(token >= ends[0], 1, 0)
    for end in ends[1:]:
        found = found + jnp.where(token >= end, 1, 0)
    return found


def position_of(ends, token):
    start = jnp.zeros_like(token)
    for end in ends:
        start = jnp.where(token >= end, end, start)
    return token - start


def tokens_column(first, rows=GROUP):
    return first + lax.broadcasted_iota(jnp.int32, (rows, 1), 0)


def additive_mask(ends, first, transposed):
    rows = first + lax.broadcasted_iota(jnp.int32, (GROUP, GROUP), 0)
    cols = first + lax.broadcasted_iota(jnp.int32, (GROUP, GROUP), 1)
    ordered = (cols >= rows) if transposed else (rows >= cols)
    kept = (sequence_of(ends, rows) == sequence_of(ends, cols)) & ordered
    return jnp.where(kept, 0.0, MASKED)


def softplus(value):
    return jnp.maximum(value, 0.0) + jnp.log1p(jnp.exp(-jnp.abs(value)))


def sigmoid(value):
    return 1.0 / (1.0 + jnp.exp(-value))


def decay_terms(ends, first, step_in, rate, lower):
    group = first // GROUP
    step = softplus(step_in)
    cum = exact_left(lower, step * (rate * LOG2E))
    last = cum[GROUP - 1 : GROUP, :]
    sequence = sequence_of(ends, tokens_column(first))
    tail = scalar_sequence_of(ends, first + GROUP - 1)
    before = jnp.where(group > 0, scalar_sequence_of(ends, first - 1), -1)
    in_tail = (sequence == tail).astype(F32)
    entered = (sequence == before).astype(F32)
    carried = jnp.where(tail == before, 1.0, 0.0)
    key_factor = jnp.exp2(last - cum) * in_tail
    entry = jnp.exp2(cum) * entered
    decay = jnp.exp2(last) * carried
    return step, cum, key_factor, entry, decay


def head_masks():
    lane = lax.broadcasted_iota(jnp.int32, (1, LANES), 1)
    first = (lane < LANES // 2).astype(F32)
    return first, 1.0 - first


def forward_kernel(
    rank_ref, len_ref, own_ref, other_ref, w_ref, rows_ref, taps_ref, head_ref,
    normed_ref, ipre_ref, spre_ref, sact_ref, stepin_ref, mixed_ref, sprev_ref,
    ext, state, spread, lower, fac, read, mask, scores, weighted,
):
    inner = rows_ref.shape[1]
    channels = ext.shape[1]
    heads = inner // (LANES // PAIR_HEADS)
    size = sprev_ref.shape[0]
    group = pl.program_id(0)
    first = group * GROUP
    ends = sequence_ends(len_ref)

    @pl.when(group == 0)
    def _():
        ext[0:8, :] = jnp.zeros((8, channels), F32)
        state[...] = jnp.zeros_like(state)
        spread[...] = spread_matrix(heads, LANES // PAIR_HEADS)
        lower[...] = lower_matrix()

    mine = rank_ref[0, 0] == group // (pl.num_programs(0) // 2)
    gain = rows_ref[ROW_NORM : ROW_NORM + 1, :]
    for part in range(4):
        sl = slice(part * 64, part * 64 + 64)
        hidden = jnp.where(mine, own_ref[sl, :].astype(F32), other_ref[sl, :].astype(F32))
        inv = lax.rsqrt(jnp.mean(hidden * hidden, axis=1, keepdims=True) + NORM_EPS)
        normed_ref[sl, :] = (hidden * inv * gain).astype(BF16)

    pre = nn(normed_ref[...], w_ref[...])
    ext[8 : 8 + GROUP, :] = pre[:, :channels]
    ipre_ref[...] = pre[:, :inner]
    spre_ref[...] = pre[:, inner:channels]
    lane = lax.broadcasted_iota(jnp.int32, (1, LANES), 1)
    step_in = jnp.where(lane < 3 * heads, pre[:, channels:], 0.0) + head_ref[0:1, :]
    stepin_ref[...] = step_in

    token = tokens_column(first)
    position = position_of(ends, token)
    keep = [(position >= offset).astype(F32) for offset in (1, 2, 3)]

    def conv(sl, taps, bias):
        total = bias + taps[3:4, :] * ext[8 : 8 + GROUP, sl]
        for offset in (1, 2, 3):
            total = total + keep[offset - 1] * (
                taps[3 - offset : 4 - offset, :] * ext[8 - offset : 8 - offset + GROUP, sl]
            )
        return total

    for part in range(2):
        sl = slice(inner + part * size, inner + (part + 1) * size)
        own = slice(part * size, (part + 1) * size)
        total = conv(sl, taps_ref[0:4, own], taps_ref[4:5, own])
        sact_ref[:, own] = (total * sigmoid(total)).astype(BF16)
    keys = sact_ref[:, :size]
    queries = sact_ref[:, size:]
    scores[...] = nt(queries, keys)
    mask[...] = additive_mask(ends, first, False)

    step, cum, key_factor, entry, decay = decay_terms(
        ends, first, step_in, head_ref[1:2, :], lower[...]
    )
    cum_rows = cum.T
    stacked = jnp.concatenate(
        [step, key_factor * step, entry, jnp.broadcast_to(decay, (16, LANES))], axis=0
    )
    fac[...] = nn(three_in_lanes(stacked, heads), spread[...])
    held = state[...].astype(BF16)
    sprev_ref[...] = held
    read[...] = nn(queries, held)

    masks = head_masks()
    for pair in range(inner // LANES):
        sl = slice(pair * LANES, (pair + 1) * LANES)
        total = conv(sl, rows_ref[ROW_TAP : ROW_TAP + 4, sl], rows_ref[ROW_BIAS : ROW_BIAS + 1, sl])
        values = (total * sigmoid(total)).astype(BF16).astype(F32)
        stepped = values * fac[0:GROUP, sl]
        weighted[:, sl] = (values * fac[GROUP : 2 * GROUP, sl]).astype(BF16)
        top, bottom, low_values, high_values = [], [], [], []
        for which in range(PAIR_HEADS):
            head = pair * PAIR_HEADS + which
            column = cum[:, head : head + 1]
            row = cum_rows[head : head + 1, :]

            def factor(rs, cs):
                gap = column[rs] - row[:, cs] + mask[rs, cs]
                return (jnp.exp2(gap) * scores[rs, cs]).astype(BF16)

            lo, hi = slice(0, HALF), slice(HALF, GROUP)
            top.append(factor(lo, lo))
            bottom.append(factor(hi, lo))
            bottom.append(factor(hi, hi))
            masked = (stepped * masks[which]).astype(BF16)
            low_values.append(masked[:HALF])
            high_values.append(masked)
        upper_part = nn(jnp.concatenate(top, axis=1), jnp.concatenate(low_values, axis=0))
        lower_part = nn(jnp.concatenate(bottom, axis=1), jnp.concatenate(high_values, axis=0))
        rest = fac[2 * GROUP : 3 * GROUP, sl] * read[:, sl] + (
            rows_ref[ROW_SKIP : ROW_SKIP + 1, sl] * values
        )
        mixed_ref[0:HALF, sl] = upper_part + rest[:HALF]
        mixed_ref[HALF:GROUP, sl] = lower_part + rest[HALF:]

    state[...] = fac[3 * GROUP : 3 * GROUP + 1, :] * state[...] + tn(keys, weighted[...])
    ext[0:8, :] = ext[GROUP : GROUP + 8, :]


def gate_kernel(
    rank_ref, len_ref, own_ref, other_ref, normed_ref, mixed_ref, w_ref, proj_ref, rows_ref,
    gate_ref, gol_ref, live_ref, sums_ref,
):
    group = pl.program_id(0)
    first = group * GROUP
    ends = sequence_ends(len_ref)
    mine = rank_ref[0, 0] == group // (pl.num_programs(0) // 2)
    valid = tokens_column(first) < ends[-1]
    cotangent = jnp.where(mine, own_ref[...].astype(F32), other_ref[...].astype(F32))
    live_ref[...] = jnp.where(valid, cotangent, 0.0).astype(BF16)
    gate_ref[...] = nn(normed_ref[...], w_ref[...])
    gol_ref[...] = nn(live_ref[...], proj_ref[...])
    gain = rows_ref[ROW_GATE : ROW_GATE + 1, :]
    lane = lax.broadcasted_iota(jnp.int32, (64, LANES), 1)
    pieces = []
    for part in range(4):
        sl = slice(part * 64, part * 64 + 64)
        gate = gate_ref[sl, :]
        gated = mixed_ref[sl, :] * (gate * sigmoid(gate))
        square = jnp.sum(gated * gated, axis=1, keepdims=True)
        inner = jnp.sum(gol_ref[sl, :] * gain * gated, axis=1, keepdims=True)
        pieces.append(jnp.where(lane < 4, square, inner))
    sums_ref[...] = jnp.concatenate(pieces, axis=0).T[0:8, :]


def gate_grad_kernel(
    own_sums_ref, other_sums_ref, gate_ref, gol_ref, mixed_ref, rows_ref,
    low_ref, first_ref, ggp_ref, gain_ref, *, inner_all,
):
    @pl.when(pl.program_id(0) == 0)
    def _():
        gain_ref[...] = jnp.zeros_like(gain_ref)

    totals = own_sums_ref[...] + other_sums_ref[...]
    columns = jnp.concatenate([totals, jnp.zeros((LANES - 8, GROUP), F32)], axis=0).T
    inv_all = lax.rsqrt(columns[:, 0:1] / inner_all + NORM_EPS)
    slope_all = inv_all * inv_all * inv_all * columns[:, 4:5] / inner_all
    gain = rows_ref[ROW_GATE : ROW_GATE + 1, :]
    total = jnp.zeros((1, gate_ref.shape[1]), F32)
    for part in range(8):
        sl = slice(part * 32, part * 32 + 32)
        inv, slope = inv_all[sl], slope_all[sl]
        gate, gol, mixed = gate_ref[sl, :], gol_ref[sl, :], mixed_ref[sl, :]
        logistic = sigmoid(gate)
        silu = gate * logistic
        gated = mixed * silu
        scaled = gated * inv
        low_ref[sl, :] = (scaled * gain).astype(BF16)
        total = total + jnp.sum(gol * scaled, axis=0, keepdims=True)
        grad = inv * (gol * gain) - gated * slope
        first_ref[sl, :] = (grad * silu).astype(BF16)
        ggp_ref[sl, :] = (grad * mixed * (logistic * (1.0 + gate * (1.0 - logistic)))).astype(BF16)
    gain_ref[0:1, :] += total


def backward_kernel(
    len_ref, ipre_ref, halo_ref, sact_ref, stepin_ref, mixed_ref, first_ref, sprev_ref,
    rows_ref, head_ref,
    gip_ref, gkq_ref, gstep_ref, conv_ref, heads_ref,
    ext, cext, gstate, spread, collect, lower, upper, fac, reads, mask, scores, gscores,
    stepped_all, weighted, entered, sums_high, sums_low,
):
    inner = rows_ref.shape[1]
    heads = inner // (LANES // PAIR_HEADS)
    size = sprev_ref.shape[0]
    turn = pl.program_id(0)
    group = pl.num_programs(0) - 1 - turn
    first = group * GROUP
    ends = sequence_ends(len_ref)

    @pl.when(turn == 0)
    def _():
        cext[GROUP : GROUP + 8, :] = jnp.zeros((8, inner), F32)
        gstate[...] = jnp.zeros_like(gstate)
        spread[...] = spread_matrix(heads, LANES // PAIR_HEADS)
        collect[...] = collect_matrix(heads, LANES // PAIR_HEADS)
        lower[...] = lower_matrix()
        upper[...] = lower_matrix(upper=True)
        conv_ref[...] = jnp.zeros_like(conv_ref)
        heads_ref[...] = jnp.zeros_like(heads_ref)

    ext[0:8, :] = jnp.where(group > 0, halo_ref[...], 0.0)
    ext[8 : 8 + GROUP, :] = ipre_ref[...]
    token = tokens_column(first)
    position = position_of(ends, token)
    keep = [(position >= offset).astype(F32) for offset in (1, 2, 3)]
    ahead = [(position_of(ends, token + offset) >= offset).astype(F32) for offset in (1, 2, 3)]

    step_in = stepin_ref[...]
    rate = head_ref[1:2, :]
    step, cum, key_factor, entry, decay = decay_terms(ends, first, step_in, rate, lower[...])
    cum_rows = cum.T
    key_step = key_factor * step
    stacked = jnp.concatenate(
        [step, key_step, entry, jnp.broadcast_to(decay, (16, LANES))], axis=0
    )
    fac[...] = nn(three_in_lanes(stacked, heads), spread[...])

    keys = sact_ref[:, :size]
    queries = sact_ref[:, size:]
    scores[...] = nt(keys, queries)
    mask[...] = additive_mask(ends, first, True)
    gscores[...] = jnp.zeros_like(gscores)
    held = gstate[...].astype(BF16)
    reads[...] = nn(keys, held)

    masks = head_masks()
    lo, hi = slice(0, HALF), slice(HALF, GROUP)
    for pair in range(inner // LANES):
        sl = slice(pair * LANES, (pair + 1) * LANES)
        taps = rows_ref[ROW_TAP : ROW_TAP + 4, sl]
        shifted = [ext[8 - offset : 8 - offset + GROUP, sl] for offset in range(4)]
        total = rows_ref[ROW_BIAS : ROW_BIAS + 1, sl] + taps[3:4, :] * shifted[0]
        for offset in (1, 2, 3):
            total = total + keep[offset - 1] * (taps[3 - offset : 4 - offset, :] * shifted[offset])
        logistic = sigmoid(total)
        values = (total * logistic).astype(BF16).astype(F32)
        slope = logistic * (1.0 + total * (1.0 - logistic))
        step_wide = fac[0:GROUP, sl]
        key_wide = fac[GROUP : 2 * GROUP, sl]
        stepped = (values * step_wide).astype(BF16)
        stepped_wide = stepped.astype(F32)
        weighted[:, sl] = (values * key_wide).astype(BF16)
        upstream = first_ref[:, sl]
        upstream_wide = upstream.astype(F32)
        entered[:, sl] = (upstream_wide * fac[2 * GROUP : 3 * GROUP, sl]).astype(BF16)

        top, bottom, top_grads, low_grads = [], [], [], []
        g00 = g01 = g11 = None
        for which in range(PAIR_HEADS):
            head = pair * PAIR_HEADS + which
            column = cum[:, head : head + 1]
            row = cum_rows[head : head + 1, :]
            masked = (upstream_wide * masks[which]).astype(BF16)
            grads = nt(stepped, masked)

            def factors(rs, cs):
                gap = row[:, cs] - column[rs] + mask[rs, cs]
                factor = jnp.exp2(gap)
                return (factor * scores[rs, cs]).astype(BF16), factor * grads[rs, cs]

            a00, d00 = factors(lo, lo)
            a01, d01 = factors(lo, hi)
            a11, d11 = factors(hi, hi)
            g00 = d00 if g00 is None else g00 + d00
            g01 = d01 if g01 is None else g01 + d01
            g11 = d11 if g11 is None else g11 + d11
            top.extend([a00, a01])
            bottom.append(a11)
            top_grads.append(masked)
            low_grads.append(masked[HALF:])
        gscores[lo, lo] += g00
        gscores[lo, hi] += g01
        gscores[hi, hi] += g11
        raw = jnp.concatenate(
            [
                nn(jnp.concatenate(top, axis=1), jnp.concatenate(top_grads, axis=0)),
                nn(jnp.concatenate(bottom, axis=1), jnp.concatenate(low_grads, axis=0)),
            ],
            axis=0,
        )
        skip = rows_ref[ROW_SKIP : ROW_SKIP + 1, sl]
        across = reads[:, sl]

        def keep_sum(index, value):
            high = value.astype(BF16)
            sums_high[index * GROUP : (index + 1) * GROUP, sl] = high
            sums_low[index * GROUP : (index + 1) * GROUP, sl] = (
                value - high.astype(F32)
            ).astype(BF16)

        keep_sum(0, upstream_wide * (mixed_ref[:, sl] - skip * values) - stepped_wide * raw)
        keep_sum(1, values * raw)
        keep_sum(2, values * across)
        conv_ref[5:6, sl] += jnp.sum(upstream_wide * values, axis=0, keepdims=True)
        inner_grad = step_wide * raw + key_wide * across + skip * upstream_wide
        grad = inner_grad * slope
        cext[0:GROUP, sl] = grad
        conv_ref[3:4, sl] += jnp.sum(grad * shifted[0], axis=0, keepdims=True)
        conv_ref[4:5, sl] += jnp.sum(grad, axis=0, keepdims=True)
        result = taps[3:4, :] * grad
        for offset in (1, 2, 3):
            conv_ref[3 - offset : 4 - offset, sl] += jnp.sum(
                keep[offset - 1] * grad * shifted[offset], axis=0, keepdims=True
            )
            result = result + ahead[offset - 1] * (
                taps[3 - offset : 4 - offset, :] * cext[offset : offset + GROUP, sl]
            )
        gip_ref[:, sl] = result.astype(BF16)

    cext[GROUP : GROUP + 8, :] = cext[0:8, :]
    state = sprev_ref[...]
    grad_scores = gscores[...].astype(BF16)
    gkq_ref[:, :size] = (nn(grad_scores, queries) + nt(weighted[...], held)).astype(BF16)
    gkq_ref[:, size:] = (tn(grad_scores, keys) + nt(entered[...], state)).astype(BF16)

    collected = nn(sums_high[...], collect[...]) + nn(sums_low[...], collect[...])
    balance = collected[:GROUP]
    direct = collected[GROUP : 2 * GROUP]
    key_dot = collected[2 * GROUP :]
    product = jnp.sum(gstate[...] * state.astype(F32), axis=0, keepdims=True)
    product_high = product.astype(BF16)
    product_low = (product - product_high.astype(F32)).astype(BF16)
    rows16 = jnp.concatenate(
        [jnp.broadcast_to(product_high, (8, inner)), jnp.broadcast_to(product_low, (8, inner))],
        axis=0,
    ).astype(BF16)
    carried = nn(rows16, collect[...])
    carry_term = decay * (carried[0:1, :] + carried[8:9, :])
    moved = key_step * key_dot
    grad_log = (
        exact_left(upper[...], balance) + carry_term + exact_left(lower[...], moved) - moved
    )
    grad_step = direct + key_factor * key_dot + grad_log * rate
    lane = lax.broadcasted_iota(jnp.int32, (1, LANES), 1)
    grad_step_in = jnp.where(lane < heads, grad_step * sigmoid(step_in), 0.0)
    gstep_ref[...] = grad_step_in.astype(BF16)
    heads_ref[0:1, :] += jnp.sum(grad_log * step * rate, axis=0, keepdims=True)
    heads_ref[1:2, :] += jnp.sum(grad_step_in, axis=0, keepdims=True)
    gstate[...] = fac[3 * GROUP : 3 * GROUP + 1, :] * gstate[...] + tn(queries, entered[...])


def state_grad_kernel(
    len_ref, own_ref, other_ref, spre_ref, taps_ref, gsp_ref, conv_ref, ext, cext
):
    rows, channels = spre_ref.shape
    ends = sequence_ends(len_ref)
    ext[0:8, :] = jnp.zeros((8, channels), F32)
    ext[8 : 8 + rows, :] = spre_ref[...]
    cext[rows : rows + 8, :] = jnp.zeros((8, channels), F32)
    conv_ref[...] = jnp.zeros_like(conv_ref)
    for group in range(rows // GROUP):
        base = group * GROUP
        token = tokens_column(base)
        position = position_of(ends, token)
        for part in range(channels // LANES):
            sl = slice(part * LANES, (part + 1) * LANES)
            shifted = [
                ext[base + 8 - offset : base + 8 - offset + GROUP, sl] for offset in range(4)
            ]
            total = taps_ref[4:5, sl] + taps_ref[3:4, sl] * shifted[0]
            for offset in (1, 2, 3):
                keep = (position >= offset).astype(F32)
                total = total + keep * (taps_ref[3 - offset : 4 - offset, sl] * shifted[offset])
            logistic = sigmoid(total)
            slope = logistic * (1.0 + total * (1.0 - logistic))
            upstream = own_ref[base : base + GROUP, sl].astype(F32) + other_ref[
                base : base + GROUP, sl
            ].astype(F32)
            grad = upstream * slope
            cext[base : base + GROUP, sl] = grad
            conv_ref[4:5, sl] += jnp.sum(grad, axis=0, keepdims=True)
            conv_ref[3:4, sl] += jnp.sum(grad * shifted[0], axis=0, keepdims=True)
            for offset in (1, 2, 3):
                keep = (position >= offset).astype(F32)
                conv_ref[3 - offset : 4 - offset, sl] += jnp.sum(
                    keep * grad * shifted[offset], axis=0, keepdims=True
                )
    for group in range(rows // GROUP):
        base = group * GROUP
        token = tokens_column(base)
        for part in range(channels // LANES):
            sl = slice(part * LANES, (part + 1) * LANES)
            result = taps_ref[3:4, sl] * cext[base : base + GROUP, sl]
            for offset in (1, 2, 3):
                ahead = (position_of(ends, token + offset) >= offset).astype(F32)
                result = result + ahead * (
                    taps_ref[3 - offset : 4 - offset, sl]
                    * cext[base + offset : base + offset + GROUP, sl]
                )
            gsp_ref[base : base + GROUP, sl] = result.astype(BF16)


def shape_of(dims, dtype):
    return jax.ShapeDtypeStruct(dims, dtype)


def params(**kwargs):
    return pltpu.CompilerParams(vmem_limit_bytes=VMEM_BYTES, **kwargs)


SMEM_SPEC = pl.BlockSpec(memory_space=pltpu.SMEM)


def whole(*dims):
    return pl.BlockSpec(dims, lambda i: (0,) * len(dims))


def on_device(
    hidden_in,
    norm_gain,
    projection_gate_inner,
    proj_state,
    proj_step,
    conv_inner,
    conv_inner_bias,
    conv_state,
    conv_state_bias,
    decay_log,
    skip_gain,
    step_bias,
    gate_gain,
    proj_out,
    lengths,
    cotangent,
):
    tensor_count = lax.axis_size("tensor")
    tensor_rank = lax.axis_index("tensor")
    shard_rank = lax.axis_index("dp")
    shard_count = lax.axis_size("dp")
    half_rows, width = hidden_in.shape
    tokens = half_rows * tensor_count
    groups = tokens // GROUP
    half_groups = groups // 2
    inner = proj_out.shape[0]
    inner_all = inner * tensor_count
    heads = decay_log.shape[0]
    head_size = inner // heads
    size = proj_state.shape[1] // 2
    taps = conv_inner.shape[0]
    shard = width // shard_count
    channels = inner + 2 * size
    swap = [(0, 1), (1, 0)]

    def exchange(value):
        return lax.ppermute(value, "tensor", swap)

    hidden_other = exchange(hidden_in)
    cotangent_other = exchange(cotangent)

    state_shard = conv_state.shape[1]
    bias_column = jnp.pad(conv_state_bias, (0, shard - state_shard))
    columns = jnp.concatenate(
        [
            proj_step, proj_step, proj_step,
            norm_gain[:, None],
            conv_inner.reshape(taps, shard).T,
            conv_inner_bias.reshape(shard, 1),
            gate_gain.reshape(shard, 1),
            conv_state.reshape(shard, 1),
            bias_column[:, None],
        ],
        axis=1,
    )
    columns = jnp.pad(columns, ((0, 0), (0, LANES - columns.shape[1])))
    first_shard = jnp.concatenate([projection_gate_inner[:, 1], proj_state, columns], axis=1)
    second_shard = jnp.concatenate([projection_gate_inner[:, 0], proj_out.T], axis=1)
    w_first = lax.all_gather(first_shard, "dp", axis=0, tiled=True)
    w_second = lax.all_gather(second_shard, "dp", axis=0, tiled=True)
    w_inner = w_first[:, :inner]
    w_state = w_first[:, inner:channels]
    w_step = w_first[:, channels:]
    w_gate = w_second[:, :inner]
    w_out = w_second[:, inner:]

    base = 3 * heads
    small = w_step[:, base : base + 9].astype(F32).T
    skip_row = jnp.repeat(skip_gain.astype(F32), head_size)[None, :]
    rows = jnp.concatenate([small[0:7], skip_row], axis=0)
    state_taps = small[7].reshape(shard_count, taps, state_shard).transpose(1, 0, 2)
    state_taps = state_taps.reshape(taps, 2 * size)
    state_bias = small[8].reshape(shard_count, shard)[:, :state_shard].reshape(1, 2 * size)
    state_rows = jnp.concatenate(
        [state_taps, state_bias, jnp.zeros((3, 2 * size), F32)], axis=0
    )
    rate = -jnp.exp(decay_log.astype(F32))
    head_rows = jnp.stack([jnp.tile(step_bias.astype(F32), 3), jnp.tile(rate, 3)])
    head_rows = jnp.pad(head_rows, ((0, 6), (0, LANES - base)))
    rank = tensor_rank.astype(jnp.int32).reshape(1, 1)

    def by_group(lanes):
        return pl.BlockSpec((GROUP, lanes), lambda i: (i, 0))

    half_block = pl.BlockSpec((GROUP, width), lambda i: (i % half_groups, 0))
    normed, inner_pre, state_pre, state_act, step_in, mixed, prev_states = pl.pallas_call(
        forward_kernel,
        grid=(groups,),
        in_specs=[
            SMEM_SPEC, SMEM_SPEC, half_block, half_block,
            whole(width, channels + LANES), whole(8, inner), whole(8, 2 * size), whole(8, LANES),
        ],
        out_specs=[
            by_group(width), by_group(inner), by_group(2 * size), by_group(2 * size),
            by_group(LANES), by_group(inner), pl.BlockSpec((size, inner), lambda i: (i, 0)),
        ],
        out_shape=[
            shape_of((tokens, width), BF16),
            shape_of((tokens, inner), F32),
            shape_of((tokens, 2 * size), F32),
            shape_of((tokens, 2 * size), BF16),
            shape_of((tokens, LANES), F32),
            shape_of((tokens, inner), F32),
            shape_of((groups * size, inner), BF16),
        ],
        scratch_shapes=[
            pltpu.VMEM((GROUP + 8, channels), F32),
            pltpu.VMEM((size, inner), F32),
            pltpu.VMEM((LANES, inner), BF16),
            pltpu.VMEM((GROUP, GROUP), BF16),
            pltpu.VMEM((3 * GROUP + 16, inner), F32),
            pltpu.VMEM((GROUP, inner), F32),
            pltpu.VMEM((GROUP, GROUP), F32),
            pltpu.VMEM((GROUP, GROUP), F32),
            pltpu.VMEM((GROUP, inner), BF16),
        ],
        compiler_params=params(),
        name="mixer_forward",
    )(rank, lengths, hidden_in, hidden_other, w_first, rows, state_rows, head_rows)

    gate_pre, grad_out_low, live, sums = pl.pallas_call(
        gate_kernel,
        grid=(groups,),
        in_specs=[
            SMEM_SPEC, SMEM_SPEC, half_block, half_block, by_group(width), by_group(inner),
            pl.BlockSpec((width, inner), lambda i: (0, 0)),
            pl.BlockSpec((width, inner), lambda i: (0, 1)),
            whole(8, inner),
        ],
        out_specs=[
            by_group(inner), by_group(inner), by_group(width),
            pl.BlockSpec((8, GROUP), lambda i: (0, i)),
        ],
        out_shape=[
            shape_of((tokens, inner), F32),
            shape_of((tokens, inner), F32),
            shape_of((tokens, width), BF16),
            shape_of((8, tokens), F32),
        ],
        compiler_params=params(),
        name="gate_forward",
    )(rank, lengths, cotangent, cotangent_other, normed, mixed, w_second, w_second, rows)

    sums_other = exchange(sums)
    sum_block = pl.BlockSpec((8, GROUP), lambda i: (0, i))
    out_low, grad_first, grad_gate_low, gain_rows = pl.pallas_call(
        functools.partial(gate_grad_kernel, inner_all=inner_all),
        grid=(groups,),
        in_specs=[
            sum_block, sum_block, by_group(inner), by_group(inner), by_group(inner),
            whole(8, inner),
        ],
        out_specs=[by_group(inner), by_group(inner), by_group(inner), whole(8, inner)],
        out_shape=[
            shape_of((tokens, inner), BF16),
            shape_of((tokens, inner), BF16),
            shape_of((tokens, inner), BF16),
            shape_of((8, inner), F32),
        ],
        compiler_params=params(),
        name="gate_backward",
    )(sums, sums_other, gate_pre, grad_out_low, mixed, rows)

    first_grads = jnp.concatenate(
        [tn(live, out_low).astype(BF16), tn(normed, grad_gate_low).astype(BF16)], axis=1
    )
    first_sum = lax.psum_scatter(first_grads, "dp", scatter_dimension=0, tiled=True)

    def rows_of(value, which):
        return lax.dynamic_slice_in_dim(value, which * half_rows, half_rows)

    mix_away = nt(rows_of(out_low, 1 - tensor_rank), w_out).astype(BF16)
    mix_here = nt(rows_of(out_low, tensor_rank), w_out)
    mix = mix_here + exchange(mix_away).astype(F32)
    slot = tensor_rank * half_rows + jnp.arange(half_rows, dtype=jnp.int32)
    valid_half = slot < jnp.sum(lengths[0])
    hidden_wide = hidden_in.astype(F32)
    block_out = (hidden_wide + jnp.where(valid_half[:, None], mix, 0.0)).astype(BF16)

    last = groups - 1
    grad_inner_low, grad_kq, grad_step_low, conv_rows, head_sums = pl.pallas_call(
        backward_kernel,
        grid=(groups,),
        in_specs=[
            SMEM_SPEC,
            pl.BlockSpec((GROUP, inner), lambda i: (last - i, 0)),
            pl.BlockSpec(
                (8, inner), lambda i: (jnp.maximum((last - i) * (GROUP // 8) - 1, 0), 0)
            ),
            pl.BlockSpec((GROUP, 2 * size), lambda i: (last - i, 0)),
            pl.BlockSpec((GROUP, LANES), lambda i: (last - i, 0)),
            pl.BlockSpec((GROUP, inner), lambda i: (last - i, 0)),
            pl.BlockSpec((GROUP, inner), lambda i: (last - i, 0)),
            pl.BlockSpec((size, inner), lambda i: (last - i, 0)),
            whole(8, inner), whole(8, LANES),
        ],
        out_specs=[
            pl.BlockSpec((GROUP, inner), lambda i: (last - i, 0)),
            pl.BlockSpec((GROUP, 2 * size), lambda i: (last - i, 0)),
            pl.BlockSpec((GROUP, LANES), lambda i: (last - i, 0)),
            whole(8, inner), whole(8, LANES),
        ],
        out_shape=[
            shape_of((tokens, inner), BF16),
            shape_of((tokens, 2 * size), BF16),
            shape_of((tokens, LANES), BF16),
            shape_of((8, inner), F32),
            shape_of((8, LANES), F32),
        ],
        scratch_shapes=[
            pltpu.VMEM((GROUP + 8, inner), F32),
            pltpu.VMEM((GROUP + 8, inner), F32),
            pltpu.VMEM((size, inner), F32),
            pltpu.VMEM((LANES, inner), BF16),
            pltpu.VMEM((inner, LANES), BF16),
            pltpu.VMEM((GROUP, GROUP), BF16),
            pltpu.VMEM((GROUP, GROUP), BF16),
            pltpu.VMEM((3 * GROUP + 16, inner), F32),
            pltpu.VMEM((GROUP, inner), F32),
            pltpu.VMEM((GROUP, GROUP), F32),
            pltpu.VMEM((GROUP, GROUP), F32),
            pltpu.VMEM((GROUP, GROUP), F32),
            pltpu.VMEM((GROUP, inner), BF16),
            pltpu.VMEM((GROUP, inner), BF16),
            pltpu.VMEM((GROUP, inner), BF16),
            pltpu.VMEM((3 * GROUP, inner), BF16),
            pltpu.VMEM((3 * GROUP, inner), BF16),
        ],
        compiler_params=params(),
        name="mixer_backward",
    )(
        lengths, inner_pre, inner_pre, state_act, step_in, mixed, grad_first, prev_states,
        rows, head_rows,
    )

    grad_kq_other = exchange(grad_kq)

    def partial_normed(which):
        return (
            nt(rows_of(grad_gate_low, which), w_gate)
            + nt(rows_of(grad_inner_low, which), w_inner)
            + nt(rows_of(grad_step_low, which), w_step)
        )

    normed_away = exchange(partial_normed(1 - tensor_rank).astype(BF16))
    normed_here = partial_normed(tensor_rank)
    grad_inner_weight = tn(normed, grad_inner_low).astype(BF16)
    grad_step_weight = tn(normed, grad_step_low).astype(BF16)

    grad_state_low, state_conv_rows = pl.pallas_call(
        state_grad_kernel,
        in_specs=[SMEM_SPEC] + [pl.BlockSpec(memory_space=pltpu.VMEM)] * 4,
        out_specs=[pl.BlockSpec(memory_space=pltpu.VMEM)] * 2,
        out_shape=[shape_of((tokens, 2 * size), BF16), shape_of((8, 2 * size), F32)],
        scratch_shapes=[
            pltpu.VMEM((tokens + 8, 2 * size), F32),
            pltpu.VMEM((tokens + 8, 2 * size), F32),
        ],
        compiler_params=params(),
        name="state_backward",
    )(lengths, grad_kq, grad_kq_other, state_pre, state_rows)

    grad_state_weight = tn(normed, grad_state_low).astype(BF16)
    second_grads = jnp.concatenate(
        [grad_inner_weight, grad_state_weight, grad_step_weight], axis=1
    )
    second_sum = lax.psum_scatter(second_grads, "dp", scatter_dimension=0, tiled=True)

    grad_normed = normed_here + normed_away.astype(F32)
    grad_normed = grad_normed + nt(rows_of(grad_state_low, tensor_rank), w_state)
    gain = rows[ROW_NORM][None, :]
    inv_rms = lax.rsqrt(jnp.mean(hidden_wide * hidden_wide, axis=1, keepdims=True) + NORM_EPS)
    grad_gain_local = jnp.sum(grad_normed * hidden_wide * inv_rms, axis=0)
    scaled_in = grad_normed * gain
    grad_hidden = (
        inv_rms * scaled_in
        - hidden_wide * inv_rms**3 * jnp.mean(scaled_in * hidden_wide, axis=1, keepdims=True)
        + cotangent.astype(F32)
    )

    skip_sums = conv_rows[5].reshape(heads, head_size).sum(axis=1)
    pieces = jnp.concatenate(
        [
            conv_rows[0:5].reshape(-1),
            gain_rows[0],
            state_conv_rows[0:5].reshape(-1),
            head_sums[0:2].reshape(-1),
            jnp.pad(skip_sums, (0, LANES - heads)),
            grad_gain_local,
        ]
    )
    placed = jnp.where(
        jnp.arange(tensor_count, dtype=jnp.int32)[:, None] == tensor_rank, pieces[None, :], 0.0
    )
    small_sum = lax.psum(placed, ("dp", "tensor"))
    mine = lax.dynamic_index_in_dim(small_sum, tensor_rank, 0, keepdims=False)

    def take(value, start, length):
        return value[start : start + length]

    at = 0
    conv_all = take(mine, at, 5 * inner).reshape(5, inner)
    at += 5 * inner
    gate_gain_all = take(mine, at, inner)
    at += inner
    state_conv_all = take(mine, at, 10 * size).reshape(5, 2 * size)
    at += 10 * size
    head_all = take(mine, at, 3 * LANES).reshape(3, LANES)
    at += 3 * LANES
    gain_all = jnp.sum(small_sum[:, at : at + width], axis=0)

    def own_shard(value, length):
        return lax.dynamic_slice_in_dim(value, shard_rank * length, length, value.ndim - 1)

    conv_own = own_shard(conv_all, shard)
    state_own = own_shard(state_conv_all, state_shard)
    gate_grad_own = first_sum[:, width:].astype(F32)
    inner_grad_own = second_sum[:, :inner].astype(F32)
    return (
        block_out,
        grad_hidden,
        own_shard(gain_all, shard),
        jnp.stack([gate_grad_own, inner_grad_own], axis=1),
        second_sum[:, inner:channels].astype(F32),
        second_sum[:, channels : channels + heads].astype(F32),
        conv_own[0:4][:, None, :],
        conv_own[4:5],
        state_own[0:4],
        state_own[4],
        head_all[0, :heads],
        head_all[2, :heads],
        head_all[1, :heads],
        own_shard(gate_gain_all, shard)[None, :],
        first_sum[:, :inner].astype(F32).T,
    )


def solution(mesh):
    placed = (
        P(("dp", "tensor"), None),
        P("dp"),
        P("dp", None, "tensor"),
        P("dp", None),
        P("dp", "tensor"),
        P(None, "tensor", "dp"),
        P("tensor", "dp"),
        P(None, "dp"),
        P("dp"),
        P("tensor"),
        P("tensor"),
        P("tensor"),
        P("tensor", "dp"),
        P("tensor", "dp"),
        P("dp", None),
        P(("dp", "tensor"), None),
    )
    return jax.shard_map(
        on_device,
        mesh=mesh,
        in_specs=placed,
        out_specs=(
            P(("dp", "tensor"), None),
            P(("dp", "tensor"), None),
            P("dp"),
            P("dp", None, "tensor"),
            P("dp", None),
            P("dp", "tensor"),
            P(None, "tensor", "dp"),
            P("tensor", "dp"),
            P(None, "dp"),
            P("dp"),
            P("tensor"),
            P("tensor"),
            P("tensor"),
            P("tensor", "dp"),
            P("tensor", "dp"),
        ),
        check_vma=False,
    )
```

```python
import functools

import jax
import jax.numpy as jnp
from jax import lax
from jax.experimental import pallas as pl
from jax.experimental.pallas import tpu as pltpu
from jax.sharding import PartitionSpec as P

GROUP = 256
HALF = GROUP // 2
LANES = 128
PAIR_HEADS = 2
NORM_EPS = 1e-05
LOG2E = 1.4426950408889634
MASKED = -1e30
VMEM_BYTES = 56 * 1024 * 1024

LANE_CONV, LANE_GATE, LANE_STATE, LANE_HEADS = 16, 21, 24, 32

F32 = jnp.float32
BF16 = jnp.bfloat16

ROW_NORM, ROW_TAP, ROW_BIAS, ROW_GATE, ROW_SKIP = 0, 1, 5, 6, 7


def nn(left, right):
    return lax.dot_general(left, right, (((1,), (0,)), ((), ())), preferred_element_type=F32)


def nt(left, right):
    return lax.dot_general(left, right, (((1,), (1,)), ((), ())), preferred_element_type=F32)


def tn(left, right):
    return lax.dot_general(left, right, (((0,), (0,)), ((), ())), preferred_element_type=F32)


def split3(value):
    high = value.astype(BF16)
    rest = value - high.astype(F32)
    mid = rest.astype(BF16)
    low = (rest - mid.astype(F32)).astype(BF16)
    return high, mid, low


def exact_left(ones, value):
    high, mid, low = split3(value)
    return nn(ones, high) + nn(ones, mid) + nn(ones, low)


def three_in_lanes(value, heads):
    high, mid, low = split3(value)
    lane = lax.broadcasted_iota(jnp.int32, value.shape, 1)
    parts = jnp.where(
        lane < heads,
        high.astype(F32),
        jnp.where(lane < 2 * heads, mid.astype(F32), low.astype(F32)),
    )
    return parts.astype(BF16)


def spread_matrix(heads, head_size):
    shape = (LANES, heads * head_size)
    lane = lax.broadcasted_iota(jnp.int32, shape, 0)
    channel = lax.broadcasted_iota(jnp.int32, shape, 1)
    owner = channel // head_size
    hit = (lane == owner) | (lane == owner + heads) | (lane == owner + 2 * heads)
    return hit.astype(F32).astype(BF16)


def collect_matrix(heads, head_size):
    shape = (heads * head_size, LANES)
    lane = lax.broadcasted_iota(jnp.int32, shape, 1)
    owner = lax.broadcasted_iota(jnp.int32, shape, 0) // head_size
    hit = (lane == owner) | (lane == owner + heads) | (lane == owner + 2 * heads)
    return hit.astype(F32).astype(BF16)


def spaced_matrix(narrow, wide, narrow_shard, wide_shard, compress):
    shape = (wide, narrow) if compress else (narrow, wide)
    at_wide = lax.broadcasted_iota(jnp.int32, shape, 0 if compress else 1)
    at_narrow = lax.broadcasted_iota(jnp.int32, shape, 1 if compress else 0)
    owner, place = at_wide // wide_shard, at_wide % wide_shard
    hit = (place < narrow_shard) & (at_narrow == owner * narrow_shard + place)
    return hit.astype(F32).astype(BF16)


def pack_kernel(
    state_ref, step_ref, norm_ref, conv_ref, bias_ref, gate_ref, taps_ref, taps_bias_ref,
    out_ref, turned, lanes,
):
    shard, heads = step_ref.shape
    states = state_ref.shape[1]
    state_shard = taps_ref.shape[1]
    base = 3 * heads
    turned[...] = jnp.zeros_like(turned)
    turned[base : base + 1, 0:shard] = norm_ref[...].astype(F32)
    turned[base + 1 : base + 5, 0:shard] = conv_ref[...].astype(F32)
    turned[base + 5 : base + 6, 0:shard] = bias_ref[...].astype(F32)
    turned[base + 6 : base + 7, 0:shard] = gate_ref[...].astype(F32)
    turned[base + 8 : base + 12, 0:state_shard] = taps_ref[...].astype(F32)
    turned[base + 12 : base + 13, 0:state_shard] = taps_bias_ref[...].astype(F32)
    lanes[...] = jnp.zeros_like(lanes)
    step = step_ref[...].astype(F32)
    for copy in range(3):
        lanes[:, copy * heads : (copy + 1) * heads] = step
    out_ref[:, :states] = state_ref[...]
    out_ref[:, states:] = (turned[...].T[0:shard, :] + lanes[...]).astype(BF16)


def lower_matrix(upper=False):
    row = lax.broadcasted_iota(jnp.int32, (GROUP, GROUP), 0)
    col = lax.broadcasted_iota(jnp.int32, (GROUP, GROUP), 1)
    hit = (col >= row) if upper else (col <= row)
    return hit.astype(F32).astype(BF16)


def sequence_ends(len_ref):
    ends, total = [], jnp.int32(0)
    for slot in range(len_ref.shape[1]):
        total = total + len_ref[0, slot]
        ends.append(total)
    return ends


def sequence_of(ends, token):
    found = (token >= ends[0]).astype(jnp.int32)
    for end in ends[1:]:
        found = found + (token >= end).astype(jnp.int32)
    return found


def scalar_sequence_of(ends, token):
    found = jnp.where(token >= ends[0], 1, 0)
    for end in ends[1:]:
        found = found + jnp.where(token >= end, 1, 0)
    return found


def position_of(ends, token):
    start = jnp.zeros_like(token)
    for end in ends:
        start = jnp.where(token >= end, end, start)
    return token - start


def tokens_column(first, rows=GROUP):
    return first + lax.broadcasted_iota(jnp.int32, (rows, 1), 0)


def additive_mask(ends, first, transposed):
    rows = first + lax.broadcasted_iota(jnp.int32, (GROUP, GROUP), 0)
    cols = first + lax.broadcasted_iota(jnp.int32, (GROUP, GROUP), 1)
    ordered = (cols >= rows) if transposed else (rows >= cols)
    kept = (sequence_of(ends, rows) == sequence_of(ends, cols)) & ordered
    return jnp.where(kept, 0.0, MASKED)


def softplus(value):
    return jnp.maximum(value, 0.0) + jnp.log1p(jnp.exp(-jnp.abs(value)))


def sigmoid(value):
    return 0.5 * jnp.tanh(0.5 * value) + 0.5


def decay_terms(ends, first, step_in, rate, lower):
    group = first // GROUP
    step = softplus(step_in)
    cum = exact_left(lower, step * (rate * LOG2E))
    last = cum[GROUP - 1 : GROUP, :]
    sequence = sequence_of(ends, tokens_column(first))
    tail = scalar_sequence_of(ends, first + GROUP - 1)
    before = jnp.where(group > 0, scalar_sequence_of(ends, first - 1), -1)
    in_tail = (sequence == tail).astype(F32)
    entered = (sequence == before).astype(F32)
    carried = jnp.where(tail == before, 1.0, 0.0)
    key_factor = jnp.exp2(last - cum) * in_tail
    entry = jnp.exp2(cum) * entered
    decay = jnp.exp2(last) * carried
    return step, cum, key_factor, entry, decay


def head_masks():
    lane = lax.broadcasted_iota(jnp.int32, (1, LANES), 1)
    first = (lane < LANES // 2).astype(F32)
    return first, 1.0 - first


def forward_kernel(
    rank_ref, len_ref, own_ref, other_ref, w_ref, rest_ref, head_ref,
    normed_ref, normed_t_ref, ipre_ref, spre_ref, sact_ref, stepin_ref, mixed_ref, sprev_ref,
    rows_ref, taps_ref,
    ext, state, spread, lower, fac, read, mask, scores, weighted, *, shard, state_shard,
):
    inner = rows_ref.shape[1]
    channels = ext.shape[1]
    heads = inner // (LANES // PAIR_HEADS)
    size = sprev_ref.shape[0]
    group = pl.program_id(0)
    first = group * GROUP
    ends = sequence_ends(len_ref)

    @pl.when(group == 0)
    def _():
        ext[0:8, :] = jnp.zeros((8, channels), F32)
        state[...] = jnp.zeros_like(state)
        spread[...] = spread_matrix(heads, LANES // PAIR_HEADS)
        lower[...] = lower_matrix()
        packed = rest_ref[:, 2 * size :].astype(F32).T
        base = 3 * heads
        rows_ref[0:7, :] = packed[base : base + 7, :]
        once = lax.broadcasted_iota(jnp.int32, (16, LANES), 1) < heads
        skip_row = jnp.where(once, head_ref[2:3, :], 0.0).astype(BF16)
        rows_ref[7:8, :] = nn(skip_row, spread[...])[0:1, :]
        taps_ref[...] = nn(
            packed[base + 8 : base + 16, :].astype(BF16),
            spaced_matrix(2 * size, rest_ref.shape[0], state_shard, shard, True),
        )

    mine = rank_ref[0, 0] == group // (pl.num_programs(0) // 2)
    gain = rows_ref[ROW_NORM : ROW_NORM + 1, :]
    for part in range(4):
        sl = slice(part * 64, part * 64 + 64)
        hidden = jnp.where(mine, own_ref[sl, :].astype(F32), other_ref[sl, :].astype(F32))
        inv = lax.rsqrt(jnp.mean(hidden * hidden, axis=1, keepdims=True) + NORM_EPS)
        normed_ref[sl, :] = (hidden * inv * gain).astype(BF16)

    normed_t_ref[...] = normed_ref[...].T
    pre = nn(normed_ref[...], w_ref[...])
    ext[8 : 8 + GROUP, 0:inner] = pre
    ipre_ref[...] = pre
    rest = nn(normed_ref[...], rest_ref[...])
    ext[8 : 8 + GROUP, inner:channels] = rest[:, : 2 * size]
    spre_ref[...] = rest[:, : 2 * size]
    lane = lax.broadcasted_iota(jnp.int32, (1, LANES), 1)
    step_in = jnp.where(lane < 3 * heads, rest[:, 2 * size :], 0.0) + head_ref[0:1, :]
    stepin_ref[...] = step_in

    token = tokens_column(first)
    position = position_of(ends, token)
    keep = [(position >= offset).astype(F32) for offset in (1, 2, 3)]

    def conv(sl, taps, bias):
        total = bias + taps[3:4, :] * ext[8 : 8 + GROUP, sl]
        for offset in (1, 2, 3):
            total = total + keep[offset - 1] * (
                taps[3 - offset : 4 - offset, :] * ext[8 - offset : 8 - offset + GROUP, sl]
            )
        return total

    for part in range(2):
        sl = slice(inner + part * size, inner + (part + 1) * size)
        own = slice(part * size, (part + 1) * size)
        total = conv(sl, taps_ref[0:4, own], taps_ref[4:5, own])
        sact_ref[:, own] = (total * sigmoid(total)).astype(BF16)
    keys = sact_ref[:, :size]
    queries = sact_ref[:, size:]
    scores[...] = nt(queries, keys)
    mask[...] = additive_mask(ends, first, False)

    step, cum, key_factor, entry, decay = decay_terms(
        ends, first, step_in, head_ref[1:2, :], lower[...]
    )
    cum_rows = cum.T
    stacked = jnp.concatenate(
        [step, key_factor * step, entry, jnp.broadcast_to(decay, (16, LANES))], axis=0
    )
    fac[...] = nn(three_in_lanes(stacked, heads), spread[...])
    held = state[...].astype(BF16)
    sprev_ref[...] = held
    read[...] = nn(queries, held)

    masks = head_masks()
    for pair in range(inner // LANES):
        sl = slice(pair * LANES, (pair + 1) * LANES)
        total = conv(sl, rows_ref[ROW_TAP : ROW_TAP + 4, sl], rows_ref[ROW_BIAS : ROW_BIAS + 1, sl])
        values = (total * sigmoid(total)).astype(BF16).astype(F32)
        stepped = values * fac[0:GROUP, sl]
        weighted[:, sl] = (values * fac[GROUP : 2 * GROUP, sl]).astype(BF16)
        top, bottom, low_values, high_values = [], [], [], []
        for which in range(PAIR_HEADS):
            head = pair * PAIR_HEADS + which
            column = cum[:, head : head + 1]
            row = cum_rows[head : head + 1, :]

            def factor(rs, cs):
                gap = column[rs] - row[:, cs] + mask[rs, cs]
                return (jnp.exp2(gap) * scores[rs, cs]).astype(BF16)

            lo, hi = slice(0, HALF), slice(HALF, GROUP)
            top.append(factor(lo, lo))
            bottom.append(factor(hi, lo))
            bottom.append(factor(hi, hi))
            masked = (stepped * masks[which]).astype(BF16)
            low_values.append(masked[:HALF])
            high_values.append(masked)
        upper_part = nn(jnp.concatenate(top, axis=1), jnp.concatenate(low_values, axis=0))
        lower_part = nn(jnp.concatenate(bottom, axis=1), jnp.concatenate(high_values, axis=0))
        rest = fac[2 * GROUP : 3 * GROUP, sl] * read[:, sl] + (
            rows_ref[ROW_SKIP : ROW_SKIP + 1, sl] * values
        )
        mixed_ref[0:HALF, sl] = upper_part + rest[:HALF]
        mixed_ref[HALF:GROUP, sl] = lower_part + rest[HALF:]

    state[...] = fac[3 * GROUP : 3 * GROUP + 1, :] * state[...] + tn(keys, weighted[...])
    ext[0:8, :] = ext[GROUP : GROUP + 8, :]


def gate_kernel(
    rank_ref, len_ref, own_ref, other_ref, normed_ref, mixed_ref, w_ref, proj_ref, rows_ref,
    gate_ref, gol_ref, live_t_ref, sums_ref,
):
    group = pl.program_id(0)
    first = group * GROUP
    ends = sequence_ends(len_ref)
    mine = rank_ref[0, 0] == group // (pl.num_programs(0) // 2)
    valid = tokens_column(first) < ends[-1]
    cotangent = jnp.where(mine, own_ref[...].astype(F32), other_ref[...].astype(F32))
    live = jnp.where(valid, cotangent, 0.0).astype(BF16)
    live_t_ref[...] = live.T
    gate_ref[...] = nn(normed_ref[...], w_ref[...])
    gol_ref[...] = nn(live, proj_ref[...])
    gain = rows_ref[ROW_GATE : ROW_GATE + 1, :]
    lane = lax.broadcasted_iota(jnp.int32, (64, LANES), 1)
    pieces = []
    for part in range(4):
        sl = slice(part * 64, part * 64 + 64)
        gate = gate_ref[sl, :]
        gated = mixed_ref[sl, :] * (gate * sigmoid(gate))
        square = jnp.sum(gated * gated, axis=1, keepdims=True)
        inner = jnp.sum(gol_ref[sl, :] * gain * gated, axis=1, keepdims=True)
        pieces.append(jnp.where(lane < 4, square, inner))
    sums_ref[...] = jnp.concatenate(pieces, axis=0).T[0:8, :]


def gate_grad_kernel(
    own_sums_ref, other_sums_ref, gate_ref, gol_ref, mixed_ref, rows_ref,
    low_ref, first_ref, ggp_ref, gain_ref, *, inner_all,
):
    @pl.when(pl.program_id(0) == 0)
    def _():
        gain_ref[...] = jnp.zeros_like(gain_ref)

    totals = own_sums_ref[...] + other_sums_ref[...]
    columns = jnp.concatenate([totals, jnp.zeros((LANES - 8, GROUP), F32)], axis=0).T
    inv_all = lax.rsqrt(columns[:, 0:1] / inner_all + NORM_EPS)
    slope_all = inv_all * inv_all * inv_all * columns[:, 4:5] / inner_all
    gain = rows_ref[ROW_GATE : ROW_GATE + 1, :]
    total = jnp.zeros((1, gate_ref.shape[1]), F32)
    for part in range(8):
        sl = slice(part * 32, part * 32 + 32)
        inv, slope = inv_all[sl], slope_all[sl]
        gate, gol, mixed = gate_ref[sl, :], gol_ref[sl, :], mixed_ref[sl, :]
        logistic = sigmoid(gate)
        silu = gate * logistic
        gated = mixed * silu
        scaled = gated * inv
        low_ref[sl, :] = (scaled * gain).astype(BF16)
        total = total + jnp.sum(gol * scaled, axis=0, keepdims=True)
        grad = inv * (gol * gain) - gated * slope
        first_ref[sl, :] = (grad * silu).astype(BF16)
        ggp_ref[sl, :] = (grad * mixed * (logistic * (1.0 + gate * (1.0 - logistic)))).astype(BF16)
    gain_ref[0:1, :] += total


def early_grad_kernel(live_t_ref, low_ref, normed_t_ref, ggp_ref, out_ref):
    half = pl.num_programs(0) // 2

    @pl.when(pl.program_id(0) < half)
    def _():
        out_ref[...] = nn(live_t_ref[...], low_ref[...]).astype(BF16)

    @pl.when(pl.program_id(0) >= half)
    def _():
        out_ref[...] = nn(normed_t_ref[...], ggp_ref[...]).astype(BF16)


def backward_kernel(
    len_ref, ipre_ref, halo_ref, sact_ref, stepin_ref, mixed_ref, first_ref, sprev_ref,
    rows_ref, head_ref,
    gip_ref, gkq_ref, gstep_ref, conv_ref, heads_ref,
    ext, cext, gstate, spread, collect, lower, upper, fac, reads, mask, scores, gscores,
    stepped_all, weighted, entered, sums_high, sums_low,
):
    inner = rows_ref.shape[1]
    heads = inner // (LANES // PAIR_HEADS)
    size = sprev_ref.shape[0]
    turn = pl.program_id(0)
    group = pl.num_programs(0) - 1 - turn
    first = group * GROUP
    ends = sequence_ends(len_ref)

    @pl.when(turn == 0)
    def _():
        cext[GROUP : GROUP + 8, :] = jnp.zeros((8, inner), F32)
        gstate[...] = jnp.zeros_like(gstate)
        spread[...] = spread_matrix(heads, LANES // PAIR_HEADS)
        collect[...] = collect_matrix(heads, LANES // PAIR_HEADS)
        lower[...] = lower_matrix()
        upper[...] = lower_matrix(upper=True)
        conv_ref[...] = jnp.zeros_like(conv_ref)
        heads_ref[...] = jnp.zeros_like(heads_ref)

    ext[0:8, :] = jnp.where(group > 0, halo_ref[...], 0.0)
    ext[8 : 8 + GROUP, :] = ipre_ref[...]
    token = tokens_column(first)
    position = position_of(ends, token)
    keep = [(position >= offset).astype(F32) for offset in (1, 2, 3)]
    ahead = [(position_of(ends, token + offset) >= offset).astype(F32) for offset in (1, 2, 3)]

    step_in = stepin_ref[...]
    rate = head_ref[1:2, :]
    step, cum, key_factor, entry, decay = decay_terms(ends, first, step_in, rate, lower[...])
    cum_rows = cum.T
    key_step = key_factor * step
    stacked = jnp.concatenate(
        [step, key_step, entry, jnp.broadcast_to(decay, (16, LANES))], axis=0
    )
    fac[...] = nn(three_in_lanes(stacked, heads), spread[...])

    keys = sact_ref[:, :size]
    queries = sact_ref[:, size:]
    scores[...] = nt(keys, queries)
    mask[...] = additive_mask(ends, first, True)
    gscores[...] = jnp.zeros_like(gscores)
    held = gstate[...].astype(BF16)
    reads[...] = nn(keys, held)

    masks = head_masks()
    lo, hi = slice(0, HALF), slice(HALF, GROUP)
    for pair in range(inner // LANES):
        sl = slice(pair * LANES, (pair + 1) * LANES)
        taps = rows_ref[ROW_TAP : ROW_TAP + 4, sl]
        shifted = [ext[8 - offset : 8 - offset + GROUP, sl] for offset in range(4)]
        total = rows_ref[ROW_BIAS : ROW_BIAS + 1, sl] + taps[3:4, :] * shifted[0]
        for offset in (1, 2, 3):
            total = total + keep[offset - 1] * (taps[3 - offset : 4 - offset, :] * shifted[offset])
        logistic = sigmoid(total)
        values = (total * logistic).astype(BF16).astype(F32)
        slope = logistic * (1.0 + total * (1.0 - logistic))
        step_wide = fac[0:GROUP, sl]
        key_wide = fac[GROUP : 2 * GROUP, sl]
        stepped = (values * step_wide).astype(BF16)
        stepped_wide = stepped.astype(F32)
        weighted[:, sl] = (values * key_wide).astype(BF16)
        upstream = first_ref[:, sl]
        upstream_wide = upstream.astype(F32)
        entered[:, sl] = (upstream_wide * fac[2 * GROUP : 3 * GROUP, sl]).astype(BF16)

        top, bottom, top_grads, low_grads = [], [], [], []
        g00 = g01 = g11 = None
        for which in range(PAIR_HEADS):
            head = pair * PAIR_HEADS + which
            column = cum[:, head : head + 1]
            row = cum_rows[head : head + 1, :]
            masked = (upstream_wide * masks[which]).astype(BF16)
            grads = nt(stepped, masked)

            def factors(rs, cs):
                gap = row[:, cs] - column[rs] + mask[rs, cs]
                factor = jnp.exp2(gap)
                return (factor * scores[rs, cs]).astype(BF16), factor * grads[rs, cs]

            a00, d00 = factors(lo, lo)
            a01, d01 = factors(lo, hi)
            a11, d11 = factors(hi, hi)
            g00 = d00 if g00 is None else g00 + d00
            g01 = d01 if g01 is None else g01 + d01
            g11 = d11 if g11 is None else g11 + d11
            top.extend([a00, a01])
            bottom.append(a11)
            top_grads.append(masked)
            low_grads.append(masked[HALF:])
        gscores[lo, lo] += g00
        gscores[lo, hi] += g01
        gscores[hi, hi] += g11
        raw = jnp.concatenate(
            [
                nn(jnp.concatenate(top, axis=1), jnp.concatenate(top_grads, axis=0)),
                nn(jnp.concatenate(bottom, axis=1), jnp.concatenate(low_grads, axis=0)),
            ],
            axis=0,
        )
        skip = rows_ref[ROW_SKIP : ROW_SKIP + 1, sl]
        across = reads[:, sl]

        def keep_sum(index, value):
            high = value.astype(BF16)
            sums_high[index * GROUP : (index + 1) * GROUP, sl] = high
            sums_low[index * GROUP : (index + 1) * GROUP, sl] = (
                value - high.astype(F32)
            ).astype(BF16)

        keep_sum(0, upstream_wide * (mixed_ref[:, sl] - skip * values) - stepped_wide * raw)
        keep_sum(1, values * raw)
        keep_sum(2, values * across)
        conv_ref[5:6, sl] += jnp.sum(upstream_wide * values, axis=0, keepdims=True)
        inner_grad = step_wide * raw + key_wide * across + skip * upstream_wide
        grad = inner_grad * slope
        cext[0:GROUP, sl] = grad
        conv_ref[3:4, sl] += jnp.sum(grad * shifted[0], axis=0, keepdims=True)
        conv_ref[4:5, sl] += jnp.sum(grad, axis=0, keepdims=True)
        result = taps[3:4, :] * grad
        for offset in (1, 2, 3):
            conv_ref[3 - offset : 4 - offset, sl] += jnp.sum(
                keep[offset - 1] * grad * shifted[offset], axis=0, keepdims=True
            )
            result = result + ahead[offset - 1] * (
                taps[3 - offset : 4 - offset, :] * cext[offset : offset + GROUP, sl]
            )
        gip_ref[:, sl] = result.astype(BF16)

    cext[GROUP : GROUP + 8, :] = cext[0:8, :]
    state = sprev_ref[...]
    grad_scores = gscores[...].astype(BF16)
    gkq_ref[:, :size] = (nn(grad_scores, queries) + nt(weighted[...], held)).astype(BF16)
    gkq_ref[:, size:] = (tn(grad_scores, keys) + nt(entered[...], state)).astype(BF16)

    collected = nn(sums_high[...], collect[...]) + nn(sums_low[...], collect[...])
    balance = collected[:GROUP]
    direct = collected[GROUP : 2 * GROUP]
    key_dot = collected[2 * GROUP :]

    def row_collect(value):
        high = value.astype(BF16)
        low = (value - high.astype(F32)).astype(BF16)
        rows16 = jnp.concatenate(
            [jnp.broadcast_to(high, (8, inner)), jnp.broadcast_to(low, (8, inner))], axis=0
        )
        found = nn(rows16, collect[...])
        return found[0:1, :] + found[8:9, :]

    carry_term = decay * row_collect(
        jnp.sum(gstate[...] * state.astype(F32), axis=0, keepdims=True)
    )
    moved = key_step * key_dot
    grad_log = (
        exact_left(upper[...], balance) + carry_term + exact_left(lower[...], moved) - moved
    )
    grad_step = direct + key_factor * key_dot + grad_log * rate
    lane = lax.broadcasted_iota(jnp.int32, (1, LANES), 1)
    grad_step_in = jnp.where(lane < heads, grad_step * sigmoid(step_in), 0.0)
    gstep_ref[...] = grad_step_in.astype(BF16)
    heads_ref[0:1, :] += jnp.sum(grad_log * step * rate, axis=0, keepdims=True)
    heads_ref[1:2, :] += jnp.sum(grad_step_in, axis=0, keepdims=True)
    gstate[...] = fac[3 * GROUP : 3 * GROUP + 1, :] * gstate[...] + tn(queries, entered[...])

    @pl.when(turn == pl.num_programs(0) - 1)
    def _():
        heads_ref[2:3, :] = row_collect(conv_ref[5:6, :])


def state_grad_kernel(
    len_ref, own_ref, other_ref, spre_ref, taps_ref, normed_t_ref, gstep_ref, inner_rows_ref,
    gain_ref, heads_ref,
    gsp_ref, rest_ref, conv_ref, ext, cext, turned, *, shard, state_shard, heads,
):
    rows, channels = spre_ref.shape
    width = rest_ref.shape[0]
    ends = sequence_ends(len_ref)
    ext[0:8, :] = jnp.zeros((8, channels), F32)
    ext[8 : 8 + rows, :] = spre_ref[...]
    cext[rows : rows + 8, :] = jnp.zeros((8, channels), F32)
    conv_ref[...] = jnp.zeros_like(conv_ref)
    for group in range(rows // GROUP):
        base = group * GROUP
        token = tokens_column(base)
        position = position_of(ends, token)
        for part in range(channels // LANES):
            sl = slice(part * LANES, (part + 1) * LANES)
            shifted = [
                ext[base + 8 - offset : base + 8 - offset + GROUP, sl] for offset in range(4)
            ]
            total = taps_ref[4:5, sl] + taps_ref[3:4, sl] * shifted[0]
            for offset in (1, 2, 3):
                keep = (position >= offset).astype(F32)
                total = total + keep * (taps_ref[3 - offset : 4 - offset, sl] * shifted[offset])
            logistic = sigmoid(total)
            slope = logistic * (1.0 + total * (1.0 - logistic))
            upstream = own_ref[base : base + GROUP, sl].astype(F32) + other_ref[
                base : base + GROUP, sl
            ].astype(F32)
            grad = upstream * slope
            cext[base : base + GROUP, sl] = grad
            conv_ref[4:5, sl] += jnp.sum(grad, axis=0, keepdims=True)
            conv_ref[3:4, sl] += jnp.sum(grad * shifted[0], axis=0, keepdims=True)
            for offset in (1, 2, 3):
                keep = (position >= offset).astype(F32)
                conv_ref[3 - offset : 4 - offset, sl] += jnp.sum(
                    keep * grad * shifted[offset], axis=0, keepdims=True
                )
    for group in range(rows // GROUP):
        base = group * GROUP
        token = tokens_column(base)
        for part in range(channels // LANES):
            sl = slice(part * LANES, (part + 1) * LANES)
            result = taps_ref[3:4, sl] * cext[base : base + GROUP, sl]
            for offset in (1, 2, 3):
                ahead = (position_of(ends, token + offset) >= offset).astype(F32)
                result = result + ahead * (
                    taps_ref[3 - offset : 4 - offset, sl]
                    * cext[base + offset : base + offset + GROUP, sl]
                )
            gsp_ref[base : base + GROUP, sl] = result.astype(BF16)
    rest_ref[:, :channels] = nn(normed_t_ref[...], gsp_ref[...]).astype(BF16)
    step_part = nn(normed_t_ref[...], gstep_ref[...])
    turned[...] = jnp.zeros_like(turned)
    turned[LANE_CONV : LANE_CONV + 5, :] = inner_rows_ref[0:5, :]
    turned[LANE_GATE : LANE_GATE + 1, :] = gain_ref[0:1, :]
    turned[LANE_STATE : LANE_STATE + 8, :] = nn(
        conv_ref[...].astype(BF16), spaced_matrix(channels, width, state_shard, shard, False)
    )
    columns = jnp.concatenate([heads_ref[...], jnp.zeros((LANES - 8, LANES), F32)], axis=0).T
    for which in range(3):
        start = LANE_HEADS + which * heads
        turned[start : start + heads, :] = jnp.broadcast_to(
            columns[0:heads, which : which + 1], (heads, width)
        )
    rest_ref[:, channels:] = (step_part + turned[...].T).astype(BF16)


def shape_of(dims, dtype):
    return jax.ShapeDtypeStruct(dims, dtype)


def params(**kwargs):
    return pltpu.CompilerParams(vmem_limit_bytes=VMEM_BYTES, **kwargs)


SMEM_SPEC = pl.BlockSpec(memory_space=pltpu.SMEM)


def whole(*dims):
    return pl.BlockSpec(dims, lambda i: (0,) * len(dims))


def bit_order(count, spread_first):
    bits = list(range(count.bit_length() - 1))
    return [0] + bits[2:] + [1] if spread_first and len(bits) > 1 else bits


def flip(value, bit, count):
    return lax.ppermute(value, "dp", [(i, i ^ (1 << bit)) for i in range(count)])


def gather_by_bits(value, rank, count, spread_first):
    held = []
    rows, lanes = value.shape
    for bit in reversed(bit_order(count, spread_first)):
        other = flip(value, bit, count)
        held = sorted(held + [bit], reverse=True)
        low = (rank >> bit) & 1 == 0
        value = jnp.stack(
            [jnp.where(low, value, other), jnp.where(low, other, value)], axis=held.index(bit)
        )
    return value.reshape(count * rows, lanes)


def scatter_by_bits(value, rank, count, spread_first):
    left = list(reversed(range(count.bit_length() - 1)))
    rows, lanes = value.shape[0] // count, value.shape[1]
    value = value.reshape([2] * len(left) + [rows, lanes])
    for bit in bit_order(count, spread_first):
        axis = left.index(bit)
        mine = (rank >> bit) & 1
        away = lax.dynamic_index_in_dim(value, 1 - mine, axis, keepdims=False)
        here = lax.dynamic_index_in_dim(value, mine, axis, keepdims=False)
        left.remove(bit)
        value = here.astype(F32) + flip(away, bit, count).astype(F32)
        if left:
            value = value.astype(BF16)
    return value


def on_device(
    hidden_in,
    norm_gain,
    projection_gate_inner,
    proj_state,
    proj_step,
    conv_inner,
    conv_inner_bias,
    conv_state,
    conv_state_bias,
    decay_log,
    skip_gain,
    step_bias,
    gate_gain,
    proj_out,
    lengths,
    cotangent,
):
    tensor_count = lax.axis_size("tensor")
    tensor_rank = lax.axis_index("tensor")
    shard_rank = lax.axis_index("dp")
    shard_count = lax.axis_size("dp")
    half_rows, width = hidden_in.shape
    tokens = half_rows * tensor_count
    groups = tokens // GROUP
    half_groups = groups // 2
    inner = proj_out.shape[0]
    inner_all = inner * tensor_count
    heads = decay_log.shape[0]
    head_size = inner // heads
    size = proj_state.shape[1] // 2
    taps = conv_inner.shape[0]
    shard = width // shard_count
    channels = inner + 2 * size
    swap = [(0, 1), (1, 0)]

    def exchange(value):
        return lax.ppermute(value, "tensor", swap)

    hidden_other = exchange(hidden_in)
    cotangent_other = exchange(lax.optimization_barrier((cotangent, hidden_other))[0])

    state_shard = conv_state.shape[1]
    rest_shard = pl.pallas_call(
        pack_kernel,
        in_specs=[pl.BlockSpec(memory_space=pltpu.VMEM)] * 8,
        out_specs=pl.BlockSpec(memory_space=pltpu.VMEM),
        out_shape=shape_of((shard, 2 * size + LANES), BF16),
        scratch_shapes=[
            pltpu.VMEM((LANES, max(LANES, shard)), F32),
            pltpu.VMEM((shard, LANES), F32),
        ],
        compiler_params=params(),
        name="pack_small",
    )(
        proj_state, proj_step, norm_gain[None, :], conv_inner.reshape(taps, shard),
        conv_inner_bias, gate_gain, conv_state, conv_state_bias[None, :],
    )
    second_shard = jnp.concatenate([projection_gate_inner[:, 0], proj_out.T], axis=1)
    w_second = lax.all_gather(second_shard, "dp", axis=0, tiled=True)
    w_inner = gather_by_bits(projection_gate_inner[:, 1], shard_rank, shard_count, False)
    w_rest = gather_by_bits(rest_shard, shard_rank, shard_count, True)
    w_state = w_rest[:, : 2 * size]
    w_step = w_rest[:, 2 * size :]
    w_gate = w_second[:, :inner]
    w_out = w_second[:, inner:]

    rate = -jnp.exp(decay_log.astype(F32))
    head_rows = jnp.stack([step_bias.astype(F32), rate, skip_gain.astype(F32)])
    head_rows = jnp.pad(jnp.tile(head_rows, (1, 3)), ((0, 5), (0, LANES - 3 * heads)))
    rank = tensor_rank.astype(jnp.int32).reshape(1, 1)

    def by_group(lanes):
        return pl.BlockSpec((GROUP, lanes), lambda i: (i, 0))

    half_block = pl.BlockSpec((GROUP, width), lambda i: (i % half_groups, 0))
    (
        normed, normed_t, inner_pre, state_pre, state_act, step_in, mixed, prev_states, rows,
        state_rows,
    ) = pl.pallas_call(
        functools.partial(forward_kernel, shard=shard, state_shard=state_shard),
        grid=(groups,),
        in_specs=[
            SMEM_SPEC, SMEM_SPEC, half_block, half_block,
            whole(width, inner), whole(width, 2 * size + LANES), whole(8, LANES),
        ],
        out_specs=[
            by_group(width), pl.BlockSpec((width, GROUP), lambda i: (0, i)), by_group(inner), by_group(2 * size), by_group(2 * size),
            by_group(LANES), by_group(inner), pl.BlockSpec((size, inner), lambda i: (i, 0)),
            whole(8, inner), whole(8, 2 * size),
        ],
        out_shape=[
            shape_of((tokens, width), BF16),
            shape_of((width, tokens), BF16),
            shape_of((tokens, inner), F32),
            shape_of((tokens, 2 * size), F32),
            shape_of((tokens, 2 * size), BF16),
            shape_of((tokens, LANES), F32),
            shape_of((tokens, inner), F32),
            shape_of((groups * size, inner), BF16),
            shape_of((8, inner), F32),
            shape_of((8, 2 * size), F32),
        ],
        scratch_shapes=[
            pltpu.VMEM((GROUP + 8, channels), F32),
            pltpu.VMEM((size, inner), F32),
            pltpu.VMEM((LANES, inner), BF16),
            pltpu.VMEM((GROUP, GROUP), BF16),
            pltpu.VMEM((3 * GROUP + 16, inner), F32),
            pltpu.VMEM((GROUP, inner), F32),
            pltpu.VMEM((GROUP, GROUP), F32),
            pltpu.VMEM((GROUP, GROUP), F32),
            pltpu.VMEM((GROUP, inner), BF16),
        ],
        compiler_params=params(),
        name="mixer_forward",
    )(rank, lengths, hidden_in, hidden_other, w_inner, w_rest, head_rows)

    gate_pre, grad_out_low, live_t, sums = pl.pallas_call(
        gate_kernel,
        grid=(groups,),
        in_specs=[
            SMEM_SPEC, SMEM_SPEC, half_block, half_block, by_group(width), by_group(inner),
            pl.BlockSpec((width, inner), lambda i: (0, 0)),
            pl.BlockSpec((width, inner), lambda i: (0, 1)),
            whole(8, inner),
        ],
        out_specs=[
            by_group(inner), by_group(inner), pl.BlockSpec((width, GROUP), lambda i: (0, i)),
            pl.BlockSpec((8, GROUP), lambda i: (0, i)),
        ],
        out_shape=[
            shape_of((tokens, inner), F32),
            shape_of((tokens, inner), F32),
            shape_of((width, tokens), BF16),
            shape_of((8, tokens), F32),
        ],
        compiler_params=params(),
        name="gate_forward",
    )(rank, lengths, cotangent, cotangent_other, normed, mixed, w_second, w_second, rows)

    sums_other = exchange(sums)
    sum_block = pl.BlockSpec((8, GROUP), lambda i: (0, i))
    out_low, grad_first, grad_gate_low, gain_rows = pl.pallas_call(
        functools.partial(gate_grad_kernel, inner_all=inner_all),
        grid=(groups,),
        in_specs=[
            sum_block, sum_block, by_group(inner), by_group(inner), by_group(inner),
            whole(8, inner),
        ],
        out_specs=[by_group(inner), by_group(inner), by_group(inner), whole(8, inner)],
        out_shape=[
            shape_of((tokens, inner), BF16),
            shape_of((tokens, inner), BF16),
            shape_of((tokens, inner), BF16),
            shape_of((8, inner), F32),
        ],
        compiler_params=params(),
        name="gate_backward",
    )(sums, sums_other, gate_pre, grad_out_low, mixed, rows)

    tiles = 2 * inner // GROUP
    half_tiles = tiles // 2
    first_grads = pl.pallas_call(
        early_grad_kernel,
        grid=(tiles,),
        in_specs=[
            whole(width, tokens),
            pl.BlockSpec((tokens, GROUP), lambda i: (0, jnp.minimum(i, half_tiles - 1))),
            whole(width, tokens),
            pl.BlockSpec((tokens, GROUP), lambda i: (0, jnp.maximum(i - half_tiles, 0))),
        ],
        out_specs=pl.BlockSpec((width, GROUP), lambda i: (0, i)),
        out_shape=shape_of((width, 2 * inner), BF16),
        compiler_params=params(),
        name="early_weight_grads",
    )(live_t, out_low, normed_t, grad_gate_low)

    def rows_of(value, which):
        return lax.dynamic_slice_in_dim(value, which * half_rows, half_rows)

    mix_away = nt(rows_of(out_low, 1 - tensor_rank), w_out).astype(BF16)
    grad_first, first_grads, mix_away = lax.optimization_barrier(
        (grad_first, first_grads, mix_away)
    )
    first_sum = lax.psum_scatter(first_grads, "dp", scatter_dimension=0, tiled=True)
    mix_here = nt(rows_of(out_low, tensor_rank), w_out)
    mix = mix_here + exchange(mix_away).astype(F32)
    slot = tensor_rank * half_rows + jnp.arange(half_rows, dtype=jnp.int32)
    valid_half = slot < jnp.sum(lengths[0])
    hidden_wide = hidden_in.astype(F32)
    block_out = (hidden_wide + jnp.where(valid_half[:, None], mix, 0.0)).astype(BF16)

    last = groups - 1
    grad_inner_low, grad_kq, grad_step_low, conv_rows, head_sums = pl.pallas_call(
        backward_kernel,
        grid=(groups,),
        in_specs=[
            SMEM_SPEC,
            pl.BlockSpec((GROUP, inner), lambda i: (last - i, 0)),
            pl.BlockSpec(
                (8, inner), lambda i: (jnp.maximum((last - i) * (GROUP // 8) - 1, 0), 0)
            ),
            pl.BlockSpec((GROUP, 2 * size), lambda i: (last - i, 0)),
            pl.BlockSpec((GROUP, LANES), lambda i: (last - i, 0)),
            pl.BlockSpec((GROUP, inner), lambda i: (last - i, 0)),
            pl.BlockSpec((GROUP, inner), lambda i: (last - i, 0)),
            pl.BlockSpec((size, inner), lambda i: (last - i, 0)),
            whole(8, inner), whole(8, LANES),
        ],
        out_specs=[
            pl.BlockSpec((GROUP, inner), lambda i: (last - i, 0)),
            pl.BlockSpec((GROUP, 2 * size), lambda i: (last - i, 0)),
            pl.BlockSpec((GROUP, LANES), lambda i: (last - i, 0)),
            whole(8, inner), whole(8, LANES),
        ],
        out_shape=[
            shape_of((tokens, inner), BF16),
            shape_of((tokens, 2 * size), BF16),
            shape_of((tokens, LANES), BF16),
            shape_of((8, inner), F32),
            shape_of((8, LANES), F32),
        ],
        scratch_shapes=[
            pltpu.VMEM((GROUP + 8, inner), F32),
            pltpu.VMEM((GROUP + 8, inner), F32),
            pltpu.VMEM((size, inner), F32),
            pltpu.VMEM((LANES, inner), BF16),
            pltpu.VMEM((inner, LANES), BF16),
            pltpu.VMEM((GROUP, GROUP), BF16),
            pltpu.VMEM((GROUP, GROUP), BF16),
            pltpu.VMEM((3 * GROUP + 16, inner), F32),
            pltpu.VMEM((GROUP, inner), F32),
            pltpu.VMEM((GROUP, GROUP), F32),
            pltpu.VMEM((GROUP, GROUP), F32),
            pltpu.VMEM((GROUP, GROUP), F32),
            pltpu.VMEM((GROUP, inner), BF16),
            pltpu.VMEM((GROUP, inner), BF16),
            pltpu.VMEM((GROUP, inner), BF16),
            pltpu.VMEM((3 * GROUP, inner), BF16),
            pltpu.VMEM((3 * GROUP, inner), BF16),
        ],
        compiler_params=params(),
        name="mixer_backward",
    )(
        lengths, inner_pre, inner_pre, state_act, step_in, mixed, grad_first, prev_states,
        rows, head_rows,
    )

    grad_kq_other = exchange(grad_kq)

    def partial_normed(which):
        return (
            nt(rows_of(grad_gate_low, which), w_gate)
            + nt(rows_of(grad_inner_low, which), w_inner)
            + nt(rows_of(grad_step_low, which), w_step)
        )

    normed_away = exchange(partial_normed(1 - tensor_rank).astype(BF16))
    normed_here = partial_normed(tensor_rank)
    inner_sum = scatter_by_bits(
        nn(normed_t, grad_inner_low).astype(BF16), shard_rank, shard_count, False
    )

    vmem = pl.BlockSpec(memory_space=pltpu.VMEM)
    grad_state_low, rest_grads = pl.pallas_call(
        functools.partial(
            state_grad_kernel, shard=shard, state_shard=state_shard, heads=heads
        ),
        in_specs=[SMEM_SPEC] + [vmem] * 9,
        out_specs=[vmem] * 2,
        out_shape=[shape_of((tokens, 2 * size), BF16), shape_of((width, 2 * size + LANES), BF16)],
        scratch_shapes=[
            pltpu.VMEM((8, 2 * size), F32),
            pltpu.VMEM((tokens + 8, 2 * size), F32),
            pltpu.VMEM((tokens + 8, 2 * size), F32),
            pltpu.VMEM((LANES, width), F32),
        ],
        compiler_params=params(),
        name="state_backward",
    )(
        lengths, grad_kq, grad_kq_other, state_pre, state_rows, normed_t, grad_step_low,
        conv_rows, gain_rows, head_sums,
    )
    rest_sum = scatter_by_bits(rest_grads, shard_rank, shard_count, True)

    grad_normed = normed_here + normed_away.astype(F32)
    grad_normed = grad_normed + nt(rows_of(grad_state_low, tensor_rank), w_state)
    gain = rows[ROW_NORM][None, :]
    inv_rms = lax.rsqrt(jnp.mean(hidden_wide * hidden_wide, axis=1, keepdims=True) + NORM_EPS)
    scaled_in = grad_normed * gain
    grad_hidden = (
        inv_rms * scaled_in
        - hidden_wide * inv_rms**3 * jnp.mean(scaled_in * hidden_wide, axis=1, keepdims=True)
        + cotangent.astype(F32)
    )

    gate_grad_own = first_sum[:, inner:].astype(F32)
    state_grad_own = rest_sum[:, : 2 * size]
    small = rest_sum[:, 2 * size :]
    step_grad_own = small[:, :heads]

    def by_row(grad, weight):
        return jnp.sum(grad * weight.astype(F32), axis=1)

    gain_part = (
        by_row(gate_grad_own, projection_gate_inner[:, 0])
        + by_row(inner_sum, projection_gate_inner[:, 1])
        + by_row(step_grad_own, proj_step)
        + jnp.where(tensor_rank == 0, by_row(state_grad_own, proj_state), 0.0)
    )
    gain_own = (gain_part + exchange(gain_part)) / norm_gain.astype(F32)

    conv_own = small[:, LANE_CONV : LANE_CONV + 5].T
    state_own = small[:state_shard, LANE_STATE : LANE_STATE + 5].T
    head_all = small[0, LANE_HEADS : LANE_HEADS + 3 * heads].reshape(3, heads)
    return (
        block_out,
        grad_hidden,
        gain_own,
        jnp.stack([gate_grad_own, inner_sum], axis=1),
        state_grad_own,
        step_grad_own,
        conv_own[0:4][:, None, :],
        conv_own[4:5],
        state_own[0:4],
        state_own[4],
        head_all[0],
        head_all[2],
        head_all[1],
        small[:, LANE_GATE][None, :],
        first_sum[:, :inner].astype(F32).T,
    )


def solution(mesh):
    placed = (
        P(("dp", "tensor"), None),
        P("dp"),
        P("dp", None, "tensor"),
        P("dp", None),
        P("dp", "tensor"),
        P(None, "tensor", "dp"),
        P("tensor", "dp"),
        P(None, "dp"),
        P("dp"),
        P("tensor"),
        P("tensor"),
        P("tensor"),
        P("tensor", "dp"),
        P("tensor", "dp"),
        P("dp", None),
        P(("dp", "tensor"), None),
    )
    return jax.shard_map(
        on_device,
        mesh=mesh,
        in_specs=placed,
        out_specs=(
            P(("dp", "tensor"), None),
            P(("dp", "tensor"), None),
            P("dp"),
            P("dp", None, "tensor"),
            P("dp", None),
            P("dp", "tensor"),
            P(None, "tensor", "dp"),
            P("tensor", "dp"),
            P(None, "dp"),
            P("dp"),
            P("tensor"),
            P("tensor"),
            P("tensor"),
            P("tensor", "dp"),
            P("tensor", "dp"),
        ),
        check_vma=False,
    )
```

```python
import functools

import jax
import jax.numpy as jnp
from jax import lax
from jax.experimental import pallas as pl
from jax.experimental.pallas import tpu as pltpu
from jax.sharding import PartitionSpec as P

GROUP = 256
HALF = GROUP // 2
LANES = 128
PAIR_HEADS = 2
NORM_EPS = 1e-05
LOG2E = 1.4426950408889634
MASKED = -1e30
VMEM_BYTES = 56 * 1024 * 1024

LANE_CONV, LANE_GATE, LANE_STATE, LANE_HEADS, LANE_GAIN = 16, 21, 24, 32, 127
HALO = 16

F32 = jnp.float32
BF16 = jnp.bfloat16

ROW_NORM, ROW_TAP, ROW_BIAS, ROW_GATE, ROW_SKIP = 0, 1, 5, 6, 7


def nn(left, right):
    return lax.dot_general(left, right, (((1,), (0,)), ((), ())), preferred_element_type=F32)


def nt(left, right):
    return lax.dot_general(left, right, (((1,), (1,)), ((), ())), preferred_element_type=F32)


def tn(left, right):
    return lax.dot_general(left, right, (((0,), (0,)), ((), ())), preferred_element_type=F32)


def split3(value):
    high = value.astype(BF16)
    rest = value - high.astype(F32)
    mid = rest.astype(BF16)
    low = (rest - mid.astype(F32)).astype(BF16)
    return high, mid, low


def exact_left(ones, value):
    lanes = value.shape[1]
    found = nn(ones, jnp.concatenate(split3(value), axis=1))
    return found[:, :lanes] + found[:, lanes : 2 * lanes] + found[:, 2 * lanes :]


def three_in_lanes(value, heads):
    high, mid, low = split3(value)
    lane = lax.broadcasted_iota(jnp.int32, value.shape, 1)
    parts = jnp.where(
        lane < heads,
        high.astype(F32),
        jnp.where(lane < 2 * heads, mid.astype(F32), low.astype(F32)),
    )
    return parts.astype(BF16)


def spread_matrix(heads, head_size):
    shape = (LANES, heads * head_size)
    lane = lax.broadcasted_iota(jnp.int32, shape, 0)
    channel = lax.broadcasted_iota(jnp.int32, shape, 1)
    owner = channel // head_size
    hit = (lane == owner) | (lane == owner + heads) | (lane == owner + 2 * heads)
    return hit.astype(F32).astype(BF16)


def collect_matrix(heads, head_size):
    shape = (heads * head_size, LANES)
    lane = lax.broadcasted_iota(jnp.int32, shape, 1)
    owner = lax.broadcasted_iota(jnp.int32, shape, 0) // head_size
    hit = (lane == owner) | (lane == owner + heads) | (lane == owner + 2 * heads)
    return hit.astype(F32).astype(BF16)


def spaced_matrix(narrow, wide, narrow_shard, wide_shard, compress):
    shape = (wide, narrow) if compress else (narrow, wide)
    at_wide = lax.broadcasted_iota(jnp.int32, shape, 0 if compress else 1)
    at_narrow = lax.broadcasted_iota(jnp.int32, shape, 1 if compress else 0)
    owner, place = at_wide // wide_shard, at_wide % wide_shard
    hit = (place < narrow_shard) & (at_narrow == owner * narrow_shard + place)
    return hit.astype(F32).astype(BF16)


def pack_kernel(
    state_ref, step_ref, norm_ref, conv_ref, bias_ref, gate_ref, taps_ref, taps_bias_ref,
    out_ref, turned, lanes,
):
    shard, heads = step_ref.shape
    states = state_ref.shape[1]
    state_shard = taps_ref.shape[1]
    base = 3 * heads
    turned[...] = jnp.zeros_like(turned)
    turned[base : base + 1, 0:shard] = norm_ref[...].astype(F32)
    turned[base + 1 : base + 5, 0:shard] = conv_ref[...].astype(F32)
    turned[base + 5 : base + 6, 0:shard] = bias_ref[...].astype(F32)
    turned[base + 6 : base + 7, 0:shard] = gate_ref[...].astype(F32)
    turned[base + 8 : base + 12, 0:state_shard] = taps_ref[...].astype(F32)
    turned[base + 12 : base + 13, 0:state_shard] = taps_bias_ref[...].astype(F32)
    lanes[...] = jnp.zeros_like(lanes)
    step = step_ref[...].astype(F32)
    for copy in range(3):
        lanes[:, copy * heads : (copy + 1) * heads] = step
    out_ref[:, :states] = state_ref[...]
    out_ref[:, states:] = (turned[...].T[0:shard, :] + lanes[...]).astype(BF16)


def lower_matrix(upper=False):
    row = lax.broadcasted_iota(jnp.int32, (GROUP, GROUP), 0)
    col = lax.broadcasted_iota(jnp.int32, (GROUP, GROUP), 1)
    hit = (col >= row) if upper else (col <= row)
    return hit.astype(F32).astype(BF16)


def sequence_ends(len_ref):
    ends, total = [], jnp.int32(0)
    for slot in range(len_ref.shape[1]):
        total = total + len_ref[0, slot]
        ends.append(total)
    return ends


def sequence_of(ends, token):
    found = (token >= ends[0]).astype(jnp.int32)
    for end in ends[1:]:
        found = found + (token >= end).astype(jnp.int32)
    return found


def scalar_sequence_of(ends, token):
    found = jnp.where(token >= ends[0], 1, 0)
    for end in ends[1:]:
        found = found + jnp.where(token >= end, 1, 0)
    return found


def position_of(ends, token):
    start = jnp.zeros_like(token)
    for end in ends:
        start = jnp.where(token >= end, end, start)
    return token - start


def tokens_column(first, rows=GROUP):
    return first + lax.broadcasted_iota(jnp.int32, (rows, 1), 0)


def additive_mask(ends, first, transposed):
    rows = first + lax.broadcasted_iota(jnp.int32, (GROUP, GROUP), 0)
    cols = first + lax.broadcasted_iota(jnp.int32, (GROUP, GROUP), 1)
    ordered = (cols >= rows) if transposed else (rows >= cols)
    kept = (sequence_of(ends, rows) == sequence_of(ends, cols)) & ordered
    return jnp.where(kept, 0.0, MASKED)


def softplus(value):
    return jnp.maximum(value, 0.0) + jnp.log1p(jnp.exp(-jnp.abs(value)))


def sigmoid(value):
    return 0.5 * jnp.tanh(0.5 * value) + 0.5


def decay_terms(ends, first, step_in, rate, lower):
    group = first // GROUP
    step = softplus(step_in)
    cum = exact_left(lower, step * (rate * LOG2E))
    last = cum[GROUP - 1 : GROUP, :]
    sequence = sequence_of(ends, tokens_column(first))
    tail = scalar_sequence_of(ends, first + GROUP - 1)
    before = jnp.where(group > 0, scalar_sequence_of(ends, first - 1), -1)
    in_tail = (sequence == tail).astype(F32)
    entered = (sequence == before).astype(F32)
    carried = jnp.where(tail == before, 1.0, 0.0)
    key_factor = jnp.exp2(last - cum) * in_tail
    entry = jnp.exp2(cum) * entered
    decay = jnp.exp2(last) * carried
    return step, cum, key_factor, entry, decay


def head_masks():
    lane = lax.broadcasted_iota(jnp.int32, (1, LANES), 1)
    first = (lane < LANES // 2).astype(F32)
    return first, 1.0 - first


def forward_kernel(
    rank_ref, len_ref, own_ref, other_ref, w_ref, rest_ref, head_ref,
    normed_ref, normed_t_ref, ipre_ref, spre_ref, sact_ref, stepin_ref, mixed_ref, sprev_ref,
    rows_ref, taps_ref,
    ext, state, spread, lower, fac, read, mask, scores, weighted, *, shard, state_shard,
):
    inner = rows_ref.shape[1]
    channels = ext.shape[1]
    heads = inner // (LANES // PAIR_HEADS)
    size = sprev_ref.shape[0]
    group = pl.program_id(0)
    first = group * GROUP
    ends = sequence_ends(len_ref)

    @pl.when(group == 0)
    def _():
        ext[0:8, :] = jnp.zeros((8, channels), F32)
        state[...] = jnp.zeros_like(state)
        spread[...] = spread_matrix(heads, LANES // PAIR_HEADS)
        lower[...] = lower_matrix()
        packed = rest_ref[:, 2 * size :].astype(F32).T
        base = 3 * heads
        rows_ref[0:7, :] = packed[base : base + 7, :]
        once = lax.broadcasted_iota(jnp.int32, (16, LANES), 1) < heads
        skip_row = jnp.where(once, head_ref[2:3, :], 0.0).astype(BF16)
        rows_ref[7:8, :] = nn(skip_row, spread[...])[0:1, :]
        taps_ref[...] = nn(
            packed[base + 8 : base + 16, :].astype(BF16),
            spaced_matrix(2 * size, rest_ref.shape[0], state_shard, shard, True),
        )

    mine = rank_ref[0, 0] == group // (pl.num_programs(0) // 2)
    gain = rows_ref[ROW_NORM : ROW_NORM + 1, :]
    for part in range(4):
        sl = slice(part * 64, part * 64 + 64)
        hidden = jnp.where(mine, own_ref[sl, :].astype(F32), other_ref[sl, :].astype(F32))
        inv = lax.rsqrt(jnp.mean(hidden * hidden, axis=1, keepdims=True) + NORM_EPS)
        normed_ref[sl, :] = (hidden * inv * gain).astype(BF16)

    normed_t_ref[...] = normed_ref[...].T
    pre = nn(normed_ref[...], w_ref[...])
    ext[8 : 8 + GROUP, 0:inner] = pre
    ipre_ref[...] = pre
    rest = nn(normed_ref[...], rest_ref[...])
    ext[8 : 8 + GROUP, inner:channels] = rest[:, : 2 * size]
    spre_ref[...] = rest[:, : 2 * size]
    lane = lax.broadcasted_iota(jnp.int32, (1, LANES), 1)
    step_in = jnp.where(lane < 3 * heads, rest[:, 2 * size :], 0.0) + head_ref[0:1, :]
    stepin_ref[...] = step_in

    token = tokens_column(first)
    position = position_of(ends, token)
    keep = [(position >= offset).astype(F32) for offset in (1, 2, 3)]

    def conv(sl, taps, bias):
        total = bias + taps[3:4, :] * ext[8 : 8 + GROUP, sl]
        for offset in (1, 2, 3):
            total = total + keep[offset - 1] * (
                taps[3 - offset : 4 - offset, :] * ext[8 - offset : 8 - offset + GROUP, sl]
            )
        return total

    for part in range(2):
        sl = slice(inner + part * size, inner + (part + 1) * size)
        own = slice(part * size, (part + 1) * size)
        total = conv(sl, taps_ref[0:4, own], taps_ref[4:5, own])
        sact_ref[:, own] = (total * sigmoid(total)).astype(BF16)
    keys = sact_ref[:, :size]
    queries = sact_ref[:, size:]
    scores[...] = nt(queries, keys)
    mask[...] = additive_mask(ends, first, False)

    step, cum, key_factor, entry, decay = decay_terms(
        ends, first, step_in, head_ref[1:2, :], lower[...]
    )
    cum_rows = cum.T
    stacked = jnp.concatenate(
        [step, key_factor * step, entry, jnp.broadcast_to(decay, (16, LANES))], axis=0
    )
    fac[...] = nn(three_in_lanes(stacked, heads), spread[...])
    held = state[...].astype(BF16)
    sprev_ref[...] = held
    read[...] = nn(queries, held)

    masks = head_masks()
    for pair in range(inner // LANES):
        sl = slice(pair * LANES, (pair + 1) * LANES)
        total = conv(sl, rows_ref[ROW_TAP : ROW_TAP + 4, sl], rows_ref[ROW_BIAS : ROW_BIAS + 1, sl])
        values = (total * sigmoid(total)).astype(BF16).astype(F32)
        stepped = values * fac[0:GROUP, sl]
        weighted[:, sl] = (values * fac[GROUP : 2 * GROUP, sl]).astype(BF16)
        top, bottom, low_values, high_values = [], [], [], []
        for which in range(PAIR_HEADS):
            head = pair * PAIR_HEADS + which
            column = cum[:, head : head + 1]
            row = cum_rows[head : head + 1, :]

            def factor(rs, cs):
                gap = column[rs] - row[:, cs] + mask[rs, cs]
                return (jnp.exp2(gap) * scores[rs, cs]).astype(BF16)

            lo, hi = slice(0, HALF), slice(HALF, GROUP)
            top.append(factor(lo, lo))
            bottom.append(factor(hi, lo))
            bottom.append(factor(hi, hi))
            masked = (stepped * masks[which]).astype(BF16)
            low_values.append(masked[:HALF])
            high_values.append(masked)
        upper_part = nn(jnp.concatenate(top, axis=1), jnp.concatenate(low_values, axis=0))
        lower_part = nn(jnp.concatenate(bottom, axis=1), jnp.concatenate(high_values, axis=0))
        rest = fac[2 * GROUP : 3 * GROUP, sl] * read[:, sl] + (
            rows_ref[ROW_SKIP : ROW_SKIP + 1, sl] * values
        )
        mixed_ref[0:HALF, sl] = upper_part + rest[:HALF]
        mixed_ref[HALF:GROUP, sl] = lower_part + rest[HALF:]

    state[...] = fac[3 * GROUP : 3 * GROUP + 1, :] * state[...] + tn(keys, weighted[...])
    ext[0:8, :] = ext[GROUP : GROUP + 8, :]


def gate_kernel(
    rank_ref, len_ref, own_ref, other_ref, normed_ref, mixed_ref, w_ref, proj_ref, rows_ref,
    gate_ref, gol_ref, live_t_ref, sums_ref,
):
    group = pl.program_id(0)
    first = group * GROUP
    ends = sequence_ends(len_ref)
    mine = rank_ref[0, 0] == group // (pl.num_programs(0) // 2)
    valid = tokens_column(first) < ends[-1]
    cotangent = jnp.where(mine, own_ref[...].astype(F32), other_ref[...].astype(F32))
    live = jnp.where(valid, cotangent, 0.0).astype(BF16)
    live_t_ref[...] = live.T
    square = jnp.zeros((GROUP, LANES), F32)
    inner = jnp.zeros((GROUP, LANES), F32)
    for part in range(gate_ref.shape[1] // GROUP):
        sl = slice(part * GROUP, (part + 1) * GROUP)
        gate = nn(normed_ref[...], w_ref[:, sl])
        gol = nn(live, proj_ref[:, sl])
        gate_ref[:, sl] = gate
        gol_ref[:, sl] = gol
        gated = mixed_ref[:, sl] * (gate * sigmoid(gate))
        squares = gated * gated
        inners = gol * rows_ref[ROW_GATE : ROW_GATE + 1, sl] * gated
        square = square + squares[:, :LANES] + squares[:, LANES:]
        inner = inner + inners[:, :LANES] + inners[:, LANES:]
    lane = lax.broadcasted_iota(jnp.int32, (GROUP, LANES), 1)
    columns = jnp.where(
        lane < 4,
        jnp.sum(square, axis=1, keepdims=True),
        jnp.sum(inner, axis=1, keepdims=True),
    )
    sums_ref[...] = columns.T[0:8, :]


def gate_grad_kernel(
    own_sums_ref, other_sums_ref, gate_ref, gol_ref, mixed_ref, rows_ref,
    low_ref, first_ref, ggp_ref, gain_ref, *, inner_all,
):
    @pl.when(pl.program_id(0) == 0)
    def _():
        gain_ref[...] = jnp.zeros_like(gain_ref)

    totals = own_sums_ref[...] + other_sums_ref[...]
    columns = jnp.concatenate([totals, jnp.zeros((LANES - 8, GROUP), F32)], axis=0).T
    inv_all = lax.rsqrt(columns[:, 0:1] / inner_all + NORM_EPS)
    slope_all = inv_all * inv_all * inv_all * columns[:, 4:5] / inner_all
    gain = rows_ref[ROW_GATE : ROW_GATE + 1, :]
    total = jnp.zeros((1, gate_ref.shape[1]), F32)
    for part in range(8):
        sl = slice(part * 32, part * 32 + 32)
        inv, slope = inv_all[sl], slope_all[sl]
        gate, gol, mixed = gate_ref[sl, :], gol_ref[sl, :], mixed_ref[sl, :]
        logistic = sigmoid(gate)
        silu = gate * logistic
        gated = mixed * silu
        scaled = gated * inv
        low_ref[sl, :] = (scaled * gain).astype(BF16)
        total = total + jnp.sum(gol * scaled, axis=0, keepdims=True)
        grad = inv * (gol * gain) - gated * slope
        first_ref[sl, :] = (grad * silu).astype(BF16)
        ggp_ref[sl, :] = (grad * mixed * (logistic * (1.0 + gate * (1.0 - logistic)))).astype(BF16)
    gain_ref[0:1, :] += total


def early_grad_kernel(live_t_ref, low_ref, normed_t_ref, ggp_ref, out_ref):
    half = pl.num_programs(0) // 2

    @pl.when(pl.program_id(0) < half)
    def _():
        out_ref[...] = nn(live_t_ref[...], low_ref[...]).astype(BF16)

    @pl.when(pl.program_id(0) >= half)
    def _():
        out_ref[...] = nn(normed_t_ref[...], ggp_ref[...]).astype(BF16)


def backward_kernel(
    len_ref, ipre_ref, halo_ref, sact_ref, stepin_ref, mixed_ref, first_ref, sprev_ref,
    rows_ref, head_ref,
    gip_ref, gkq_ref, gstep_ref, conv_ref, heads_ref,
    ext, cext, gstate, spread, collect, lower, upper, fac, reads, mask, scores, gscores,
    weighted, entered, sums,
):
    inner = rows_ref.shape[1]
    heads = inner // (LANES // PAIR_HEADS)
    size = sprev_ref.shape[0]
    turn = pl.program_id(0)
    group = pl.num_programs(0) - 1 - turn
    first = group * GROUP
    ends = sequence_ends(len_ref)

    @pl.when(turn == 0)
    def _():
        cext[GROUP : GROUP + 8, :] = jnp.zeros((8, inner), F32)
        gstate[...] = jnp.zeros_like(gstate)
        spread[...] = spread_matrix(heads, LANES // PAIR_HEADS)
        collect[...] = collect_matrix(heads, LANES // PAIR_HEADS)
        lower[...] = lower_matrix()
        upper[...] = lower_matrix(upper=True)
        conv_ref[...] = jnp.zeros_like(conv_ref)
        heads_ref[...] = jnp.zeros_like(heads_ref)

    ext[0:8, :] = jnp.where(group > 0, halo_ref[...], 0.0)
    ext[8 : 8 + GROUP, :] = ipre_ref[...]
    token = tokens_column(first)
    position = position_of(ends, token)
    keep = [(position >= offset).astype(F32) for offset in (1, 2, 3)]
    ahead = [(position_of(ends, token + offset) >= offset).astype(F32) for offset in (1, 2, 3)]

    step_in = stepin_ref[...]
    rate = head_ref[1:2, :]
    step, cum, key_factor, entry, decay = decay_terms(ends, first, step_in, rate, lower[...])
    cum_rows = cum.T
    key_step = key_factor * step
    stacked = jnp.concatenate(
        [step, key_step, entry, jnp.broadcast_to(decay, (16, LANES))], axis=0
    )
    fac[...] = nn(three_in_lanes(stacked, heads), spread[...])

    keys = sact_ref[:, :size]
    queries = sact_ref[:, size:]
    scores[...] = nt(keys, queries)
    mask[...] = additive_mask(ends, first, True)
    gscores[...] = jnp.zeros_like(gscores)
    held = gstate[...].astype(BF16)
    reads[...] = nn(keys, held)

    masks = head_masks()
    lo, hi = slice(0, HALF), slice(HALF, GROUP)
    for pair in range(inner // LANES):
        sl = slice(pair * LANES, (pair + 1) * LANES)
        taps = rows_ref[ROW_TAP : ROW_TAP + 4, sl]
        shifted = [ext[8 - offset : 8 - offset + GROUP, sl] for offset in range(4)]
        total = rows_ref[ROW_BIAS : ROW_BIAS + 1, sl] + taps[3:4, :] * shifted[0]
        for offset in (1, 2, 3):
            total = total + keep[offset - 1] * (taps[3 - offset : 4 - offset, :] * shifted[offset])
        logistic = sigmoid(total)
        values = (total * logistic).astype(BF16).astype(F32)
        slope = logistic * (1.0 + total * (1.0 - logistic))
        step_wide = fac[0:GROUP, sl]
        key_wide = fac[GROUP : 2 * GROUP, sl]
        stepped = (values * step_wide).astype(BF16)
        stepped_wide = stepped.astype(F32)
        weighted[:, sl] = (values * key_wide).astype(BF16)
        upstream = first_ref[:, sl]
        upstream_wide = upstream.astype(F32)
        entered[:, sl] = (upstream_wide * fac[2 * GROUP : 3 * GROUP, sl]).astype(BF16)

        top, bottom, top_grads, low_grads = [], [], [], []
        g00 = g01 = g11 = None
        split_up = [(upstream_wide * one).astype(BF16) for one in masks]
        grads_low = nt(stepped[HALF:], jnp.concatenate([one[HALF:] for one in split_up], axis=0))
        for which in range(PAIR_HEADS):
            head = pair * PAIR_HEADS + which
            column = cum[:, head : head + 1]
            row = cum_rows[head : head + 1, :]
            masked = split_up[which]
            grads_top = nt(stepped[:HALF], masked)

            def factors(rs, cs, grads):
                gap = row[:, cs] - column[rs] + mask[rs, cs]
                factor = jnp.exp2(gap)
                return (factor * scores[rs, cs]).astype(BF16), factor * grads

            a00, d00 = factors(lo, lo, grads_top[:, lo])
            a01, d01 = factors(lo, hi, grads_top[:, hi])
            a11, d11 = factors(hi, hi, grads_low[:, which * HALF : (which + 1) * HALF])
            g00 = d00 if g00 is None else g00 + d00
            g01 = d01 if g01 is None else g01 + d01
            g11 = d11 if g11 is None else g11 + d11
            top.extend([a00, a01])
            bottom.append(a11)
            top_grads.append(masked)
            low_grads.append(masked[HALF:])
        gscores[lo, lo] += g00
        gscores[lo, hi] += g01
        gscores[hi, hi] += g11
        raw = jnp.concatenate(
            [
                nn(jnp.concatenate(top, axis=1), jnp.concatenate(top_grads, axis=0)),
                nn(jnp.concatenate(bottom, axis=1), jnp.concatenate(low_grads, axis=0)),
            ],
            axis=0,
        )
        skip = rows_ref[ROW_SKIP : ROW_SKIP + 1, sl]
        across = reads[:, sl]

        balance = upstream_wide * (mixed_ref[:, sl] - skip * values) - stepped_wide * raw
        high = balance.astype(BF16)
        sums[0:GROUP, sl] = high
        sums[GROUP : 2 * GROUP, sl] = (balance - high.astype(F32)).astype(BF16)
        sums[2 * GROUP : 3 * GROUP, sl] = (values * raw).astype(BF16)
        sums[3 * GROUP : 4 * GROUP, sl] = (values * across).astype(BF16)
        conv_ref[5:6, sl] += jnp.sum(upstream_wide * values, axis=0, keepdims=True)
        inner_grad = step_wide * raw + key_wide * across + skip * upstream_wide
        grad = inner_grad * slope
        cext[0:GROUP, sl] = grad
        conv_ref[3:4, sl] += jnp.sum(grad * shifted[0], axis=0, keepdims=True)
        conv_ref[4:5, sl] += jnp.sum(grad, axis=0, keepdims=True)
        result = taps[3:4, :] * grad
        for offset in (1, 2, 3):
            conv_ref[3 - offset : 4 - offset, sl] += jnp.sum(
                keep[offset - 1] * grad * shifted[offset], axis=0, keepdims=True
            )
            result = result + ahead[offset - 1] * (
                taps[3 - offset : 4 - offset, :] * cext[offset : offset + GROUP, sl]
            )
        gip_ref[:, sl] = result.astype(BF16)

    cext[GROUP : GROUP + 8, :] = cext[0:8, :]
    state = sprev_ref[...]
    grad_scores = gscores[...].astype(BF16)
    gkq_ref[:, :size] = (nn(grad_scores, queries) + nt(weighted[...], held)).astype(BF16)
    gkq_ref[:, size:] = (tn(grad_scores, keys) + nt(entered[...], state)).astype(BF16)

    collected = nn(sums[...], collect[...])
    balance = collected[:GROUP] + collected[GROUP : 2 * GROUP]
    direct = collected[2 * GROUP : 3 * GROUP]
    key_dot = collected[3 * GROUP :]

    def row_collect(value):
        high = value.astype(BF16)
        low = (value - high.astype(F32)).astype(BF16)
        rows16 = jnp.concatenate(
            [jnp.broadcast_to(high, (8, inner)), jnp.broadcast_to(low, (8, inner))], axis=0
        )
        found = nn(rows16, collect[...])
        return found[0:1, :] + found[8:9, :]

    carry_term = decay * row_collect(
        jnp.sum(gstate[...] * state.astype(F32), axis=0, keepdims=True)
    )
    moved = key_step * key_dot
    grad_log = (
        exact_left(upper[...], balance) + carry_term + exact_left(lower[...], moved) - moved
    )
    grad_step = direct + key_factor * key_dot + grad_log * rate
    lane = lax.broadcasted_iota(jnp.int32, (1, LANES), 1)
    grad_step_in = jnp.where(lane < heads, grad_step * sigmoid(step_in), 0.0)
    gstep_ref[...] = grad_step_in.astype(BF16)
    heads_ref[0:1, :] += jnp.sum(grad_log * step * rate, axis=0, keepdims=True)
    heads_ref[1:2, :] += jnp.sum(grad_step_in, axis=0, keepdims=True)
    gstate[...] = fac[3 * GROUP : 3 * GROUP + 1, :] * gstate[...] + tn(queries, entered[...])

    @pl.when(turn == pl.num_programs(0) - 1)
    def _():
        heads_ref[2:3, :] = row_collect(conv_ref[5:6, :])


def state_grad_kernel(
    rank_ref, len_ref, own_ref, other_ref, spre_ref, taps_ref, normed_t_ref, gstep_ref,
    inner_rows_ref, gain_ref, heads_ref,
    gsp_ref, rest_ref, conv_ref, ext, cext, turned, *, shard, state_shard, heads,
):
    rows, channels = own_ref.shape
    width = rest_ref.shape[0]
    half = rows - HALO
    rank = rank_ref[0, 0]
    base = pl.multiple_of(rank * (half - HALO), HALO)
    chunk = window_chunk(rows)
    ends = sequence_ends(len_ref)
    before = spre_ref[pl.ds(pl.multiple_of(jnp.maximum(base - 8, 0), 8), 8), :]
    ext[0:8, :] = jnp.where(rank > 0, before, 0.0)
    ext[8 : 8 + rows, :] = spre_ref[pl.ds(base, rows), :]
    cext[rows : rows + 8, :] = jnp.zeros((8, channels), F32)
    conv_ref[...] = jnp.zeros_like(conv_ref)
    gsp_ref[...] = jnp.zeros_like(gsp_ref)
    for at in range(0, rows, chunk):
        token = tokens_column(base + at, chunk)
        position = position_of(ends, token)
        owned = ((token >= rank * half) & (token < (rank + 1) * half)).astype(F32)
        keep = [(position >= offset).astype(F32) for offset in (1, 2, 3)]
        for part in range(channels // LANES):
            sl = slice(part * LANES, (part + 1) * LANES)
            shifted = [ext[at + 8 - offset : at + 8 - offset + chunk, sl] for offset in range(4)]
            total = taps_ref[4:5, sl] + taps_ref[3:4, sl] * shifted[0]
            for offset in (1, 2, 3):
                total = total + keep[offset - 1] * (
                    taps_ref[3 - offset : 4 - offset, sl] * shifted[offset]
                )
            logistic = sigmoid(total)
            slope = logistic * (1.0 + total * (1.0 - logistic))
            upstream = own_ref[at : at + chunk, sl].astype(F32) + other_ref[
                at : at + chunk, sl
            ].astype(F32)
            grad = upstream * slope
            cext[at : at + chunk, sl] = grad
            grad = grad * owned
            conv_ref[4:5, sl] += jnp.sum(grad, axis=0, keepdims=True)
            conv_ref[3:4, sl] += jnp.sum(grad * shifted[0], axis=0, keepdims=True)
            for offset in (1, 2, 3):
                conv_ref[3 - offset : 4 - offset, sl] += jnp.sum(
                    keep[offset - 1] * grad * shifted[offset], axis=0, keepdims=True
                )
    for at in range(0, rows, chunk):
        token = tokens_column(base + at, chunk)
        owned = ((token >= rank * half) & (token < (rank + 1) * half)).astype(F32)
        ahead = [
            (position_of(ends, token + offset) >= offset).astype(F32) for offset in (1, 2, 3)
        ]
        for part in range(channels // LANES):
            sl = slice(part * LANES, (part + 1) * LANES)
            result = taps_ref[3:4, sl] * cext[at : at + chunk, sl]
            for offset in (1, 2, 3):
                result = result + ahead[offset - 1] * (
                    taps_ref[3 - offset : 4 - offset, sl]
                    * cext[at + offset : at + offset + chunk, sl]
                )
            place = pl.ds(pl.multiple_of(base + at, HALO), chunk)
            gsp_ref[place, sl] = (result * owned).astype(BF16)
    rest_ref[:, :channels] = nn(normed_t_ref[...], gsp_ref[...]).astype(BF16)
    step_part = nn(normed_t_ref[...], gstep_ref[...])
    turned[...] = jnp.zeros_like(turned)
    turned[LANE_CONV : LANE_CONV + 5, :] = inner_rows_ref[0:5, :]
    turned[LANE_GATE : LANE_GATE + 1, :] = gain_ref[0:1, :]
    turned[LANE_STATE : LANE_STATE + 8, :] = nn(
        conv_ref[...].astype(BF16), spaced_matrix(channels, width, state_shard, shard, False)
    )
    columns = jnp.concatenate([heads_ref[...], jnp.zeros((LANES - 8, LANES), F32)], axis=0).T
    for which in range(3):
        start = LANE_HEADS + which * heads
        turned[start : start + heads, :] = jnp.broadcast_to(
            columns[0:heads, which : which + 1], (heads, width)
        )
    rest_ref[:, channels:] = (step_part + turned[...].T).astype(BF16)


def window_chunk(rows):
    return max(n for n in range(HALO, GROUP + 1, HALO) if rows % n == 0)


def finish_kernel(
    first_ref, inner_ref, rest_ref, weight_ref, state_ref, step_ref, pgi_ref, packed_ref
):
    width = first_ref.shape[1]
    states = state_ref.shape[1]
    heads = step_ref.shape[1]
    shard = step_ref.shape[0]
    gate = first_ref[...].astype(F32)
    inner = inner_ref[...]
    rest = rest_ref[...]
    pgi_ref[:, 0:1, :] = gate[:, None, :]
    pgi_ref[:, 1:2, :] = inner[:, None, :]
    weight = weight_ref[...].astype(F32)
    product = jnp.sum(gate * weight[:, :width] + inner * weight[:, width:], axis=1, keepdims=True)
    product += jnp.sum(rest[:, :states] * state_ref[...].astype(F32), axis=1, keepdims=True)
    small = rest[:, states:]
    product += jnp.sum(small[:, :heads] * step_ref[...].astype(F32), axis=1, keepdims=True)
    lane = lax.broadcasted_iota(jnp.int32, (shard, LANES), 1)
    packed_ref[:, :states] = rest[:, :states]
    packed_ref[:, states:] = jnp.where(lane == LANE_GAIN, product, small)


def unpack_kernel(
    own_ref, other_ref, norm_ref,
    state_ref, step_ref, gain_ref, conv_ref, bias_ref, taps_ref, taps_bias_ref,
    decay_ref, skip_ref, step_bias_ref, gate_ref,
):
    shard, states = state_ref.shape
    heads = step_ref.shape[1]
    state_shard = taps_ref.shape[1]
    state_ref[...] = own_ref[:, :states] + other_ref[:, :states]
    small = own_ref[:, states:]
    both = small + other_ref[:, states:]
    step_ref[...] = small[:, :heads]

    def turn(value):
        if shard < LANES:
            value = jnp.concatenate([value, jnp.zeros((LANES - shard, LANES), F32)], axis=0)
        return value.T

    small_rows, both_rows = turn(small), turn(both)
    gain_ref[...] = both_rows[LANE_GAIN : LANE_GAIN + 1, :shard] / norm_ref[...].astype(F32)
    conv_ref[...] = small_rows[LANE_CONV : LANE_CONV + 4, :shard]
    bias_ref[...] = small_rows[LANE_CONV + 4 : LANE_CONV + 5, :shard]
    gate_ref[...] = small_rows[LANE_GATE : LANE_GATE + 1, :shard]
    taps_ref[...] = both_rows[LANE_STATE : LANE_STATE + 4, :state_shard]
    taps_bias_ref[...] = both_rows[LANE_STATE + 4 : LANE_STATE + 5, :state_shard]
    first = small[0:8, :]
    for which, out_ref in enumerate((decay_ref, step_bias_ref, skip_ref)):
        start = LANE_HEADS + which * heads
        out_ref[...] = pltpu.roll(first, LANES - start, 1)[0:1, :heads]


def shape_of(dims, dtype):
    return jax.ShapeDtypeStruct(dims, dtype)


def params(**kwargs):
    return pltpu.CompilerParams(vmem_limit_bytes=VMEM_BYTES, **kwargs)


def cost(micros):
    return pl.CostEstimate(flops=int(micros * 1.1e9), bytes_accessed=0, transcendentals=0)


SMEM_SPEC = pl.BlockSpec(memory_space=pltpu.SMEM)


def whole(*dims):
    return pl.BlockSpec(dims, lambda i: (0,) * len(dims))


def bit_order(count, spread_first):
    bits = list(range(count.bit_length() - 1))
    return [0] + bits[2:] + [1] if spread_first and len(bits) > 1 else bits


def flip(value, bit, count):
    return lax.ppermute(value, "dp", [(i, i ^ (1 << bit)) for i in range(count)])


def gather_by_bits(value, rank, count, spread_first, before_second=None):
    held, begun = [], []
    rows, lanes = value.shape
    for bit in reversed(bit_order(count, spread_first)):
        if len(begun) == 1 and before_second is not None:
            value = lax.optimization_barrier((value, before_second))[0]
        begun.append(value)
        other = flip(value, bit, count)
        held = sorted(held + [bit], reverse=True)
        low = (rank >> bit) & 1 == 0
        value = jnp.stack(
            [jnp.where(low, value, other), jnp.where(low, other, value)], axis=held.index(bit)
        )
    return value.reshape(count * rows, lanes), begun


def scatter_by_bits(value, rank, count, spread_first):
    left = list(reversed(range(count.bit_length() - 1)))
    rows, lanes = value.shape[0] // count, value.shape[1]
    value = value.reshape([2] * len(left) + [rows, lanes])
    for bit in bit_order(count, spread_first):
        axis = left.index(bit)
        mine = (rank >> bit) & 1
        away = lax.dynamic_index_in_dim(value, 1 - mine, axis, keepdims=False)
        here = lax.dynamic_index_in_dim(value, mine, axis, keepdims=False)
        left.remove(bit)
        value = here.astype(F32) + flip(away, bit, count).astype(F32)
        if left:
            value = value.astype(BF16)
    return value


def on_device(
    hidden_in,
    norm_gain,
    projection_gate_inner,
    proj_state,
    proj_step,
    conv_inner,
    conv_inner_bias,
    conv_state,
    conv_state_bias,
    decay_log,
    skip_gain,
    step_bias,
    gate_gain,
    proj_out,
    lengths,
    cotangent,
):
    tensor_count = lax.axis_size("tensor")
    tensor_rank = lax.axis_index("tensor")
    shard_rank = lax.axis_index("dp")
    shard_count = lax.axis_size("dp")
    half_rows, width = hidden_in.shape
    tokens = half_rows * tensor_count
    groups = tokens // GROUP
    half_groups = groups // 2
    inner = proj_out.shape[0]
    inner_all = inner * tensor_count
    heads = decay_log.shape[0]
    head_size = inner // heads
    size = proj_state.shape[1] // 2
    taps = conv_inner.shape[0]
    shard = width // shard_count
    channels = inner + 2 * size
    swap = [(0, 1), (1, 0)]

    def exchange(value):
        return lax.ppermute(value, "tensor", swap)

    pieces = []
    for part in range(half_groups):
        piece = hidden_in[part * GROUP : (part + 1) * GROUP]
        if pieces:
            piece = lax.optimization_barrier((piece, pieces[-1]))[0]
        pieces.append(exchange(piece))
    hidden_other = jnp.concatenate(pieces, axis=0)
    cotangent_other = exchange(lax.optimization_barrier((cotangent, hidden_other))[0])

    state_shard = conv_state.shape[1]
    rest_shard = pl.pallas_call(
        pack_kernel,
        in_specs=[pl.BlockSpec(memory_space=pltpu.VMEM)] * 8,
        out_specs=pl.BlockSpec(memory_space=pltpu.VMEM),
        out_shape=shape_of((shard, 2 * size + LANES), BF16),
        scratch_shapes=[
            pltpu.VMEM((LANES, max(LANES, shard)), F32),
            pltpu.VMEM((shard, LANES), F32),
        ],
        compiler_params=params(),
        cost_estimate=cost(2),
        name="pack_small",
    )(
        proj_state, proj_step, norm_gain[None, :], conv_inner.reshape(taps, shard),
        conv_inner_bias, gate_gain, conv_state, conv_state_bias[None, :],
    )
    w_inner, begun = gather_by_bits(
        projection_gate_inner[:, 1], shard_rank, shard_count, False, pieces[0]
    )
    w_rest, _ = gather_by_bits(rest_shard, shard_rank, shard_count, True)
    second_shard = jnp.concatenate([projection_gate_inner[:, 0], proj_out.T], axis=1)
    second_shard = lax.optimization_barrier((second_shard, begun[min(2, len(begun) - 1)]))[0]
    w_second = lax.all_gather(second_shard, "dp", axis=0, tiled=True)
    w_state = w_rest[:, : 2 * size]
    w_step = w_rest[:, 2 * size :]
    w_gate = w_second[:, :inner]
    w_out = w_second[:, inner:]

    rate = -jnp.exp(decay_log.astype(F32))
    head_rows = jnp.stack([step_bias.astype(F32), rate, skip_gain.astype(F32)])
    head_rows = jnp.pad(jnp.tile(head_rows, (1, 3)), ((0, 5), (0, LANES - 3 * heads)))
    rank = tensor_rank.astype(jnp.int32).reshape(1, 1)

    def by_group(lanes):
        return pl.BlockSpec((GROUP, lanes), lambda i: (i, 0))

    half_block = pl.BlockSpec((GROUP, width), lambda i: (i % half_groups, 0))
    (
        normed, normed_t, inner_pre, state_pre, state_act, step_in, mixed, prev_states, rows,
        state_rows,
    ) = pl.pallas_call(
        functools.partial(forward_kernel, shard=shard, state_shard=state_shard),
        grid=(groups,),
        in_specs=[
            SMEM_SPEC, SMEM_SPEC, half_block, half_block,
            whole(width, inner), whole(width, 2 * size + LANES), whole(8, LANES),
        ],
        out_specs=[
            by_group(width), pl.BlockSpec((width, GROUP), lambda i: (0, i)), by_group(inner), by_group(2 * size), by_group(2 * size),
            by_group(LANES), by_group(inner), pl.BlockSpec((size, inner), lambda i: (i, 0)),
            whole(8, inner), whole(8, 2 * size),
        ],
        out_shape=[
            shape_of((tokens, width), BF16),
            shape_of((width, tokens), BF16),
            shape_of((tokens, inner), F32),
            shape_of((tokens, 2 * size), F32),
            shape_of((tokens, 2 * size), BF16),
            shape_of((tokens, LANES), F32),
            shape_of((tokens, inner), F32),
            shape_of((groups * size, inner), BF16),
            shape_of((8, inner), F32),
            shape_of((8, 2 * size), F32),
        ],
        scratch_shapes=[
            pltpu.VMEM((GROUP + 8, channels), F32),
            pltpu.VMEM((size, inner), F32),
            pltpu.VMEM((LANES, inner), BF16),
            pltpu.VMEM((GROUP, GROUP), BF16),
            pltpu.VMEM((3 * GROUP + 16, inner), F32),
            pltpu.VMEM((GROUP, inner), F32),
            pltpu.VMEM((GROUP, GROUP), F32),
            pltpu.VMEM((GROUP, GROUP), F32),
            pltpu.VMEM((GROUP, inner), BF16),
        ],
        compiler_params=params(),
        cost_estimate=cost(2),
        name="mixer_forward",
    )(rank, lengths, hidden_in, hidden_other, w_inner, w_rest, head_rows)

    gate_pre, grad_out_low, live_t, sums = pl.pallas_call(
        gate_kernel,
        grid=(groups,),
        in_specs=[
            SMEM_SPEC, SMEM_SPEC, half_block, half_block, by_group(width), by_group(inner),
            pl.BlockSpec((width, inner), lambda i: (0, 0)),
            pl.BlockSpec((width, inner), lambda i: (0, 1)),
            whole(8, inner),
        ],
        out_specs=[
            by_group(inner), by_group(inner), pl.BlockSpec((width, GROUP), lambda i: (0, i)),
            pl.BlockSpec((8, GROUP), lambda i: (0, i)),
        ],
        out_shape=[
            shape_of((tokens, inner), F32),
            shape_of((tokens, inner), F32),
            shape_of((width, tokens), BF16),
            shape_of((8, tokens), F32),
        ],
        compiler_params=params(),
        cost_estimate=cost(16),
        name="gate_forward",
    )(rank, lengths, cotangent, cotangent_other, normed, mixed, w_second, w_second, rows)

    sums_other = exchange(sums)
    sum_block = pl.BlockSpec((8, GROUP), lambda i: (0, i))
    out_low, grad_first, grad_gate_low, gain_rows = pl.pallas_call(
        functools.partial(gate_grad_kernel, inner_all=inner_all),
        grid=(groups,),
        in_specs=[
            sum_block, sum_block, by_group(inner), by_group(inner), by_group(inner),
            whole(8, inner),
        ],
        out_specs=[by_group(inner), by_group(inner), by_group(inner), whole(8, inner)],
        out_shape=[
            shape_of((tokens, inner), BF16),
            shape_of((tokens, inner), BF16),
            shape_of((tokens, inner), BF16),
            shape_of((8, inner), F32),
        ],
        compiler_params=params(),
        cost_estimate=cost(13),
        name="gate_backward",
    )(sums, sums_other, gate_pre, grad_out_low, mixed, rows)

    tiles = 2 * inner // GROUP
    half_tiles = tiles // 2
    first_grads = pl.pallas_call(
        early_grad_kernel,
        grid=(tiles,),
        in_specs=[
            whole(width, tokens),
            pl.BlockSpec((tokens, GROUP), lambda i: (0, jnp.minimum(i, half_tiles - 1))),
            whole(width, tokens),
            pl.BlockSpec((tokens, GROUP), lambda i: (0, jnp.maximum(i - half_tiles, 0))),
        ],
        out_specs=pl.BlockSpec((width, GROUP), lambda i: (0, i)),
        out_shape=shape_of((width, 2 * inner), BF16),
        compiler_params=params(),
        cost_estimate=cost(13),
        name="early_weight_grads",
    )(live_t, out_low, normed_t, grad_gate_low)

    def rows_of(value, which):
        return lax.dynamic_slice_in_dim(value, which * half_rows, half_rows)

    mix_away = nt(rows_of(out_low, 1 - tensor_rank), w_out).astype(BF16)
    grad_first, first_grads, mix_away = lax.optimization_barrier(
        (grad_first, first_grads, mix_away)
    )
    first_sum = lax.psum_scatter(first_grads, "dp", scatter_dimension=0, tiled=True)
    mix_other = exchange(mix_away)
    mix_here = nt(rows_of(out_low, tensor_rank), w_out)
    last = groups - 1
    grad_inner_low, grad_kq, grad_step_low, conv_rows, head_sums = pl.pallas_call(
        backward_kernel,
        grid=(groups,),
        in_specs=[
            SMEM_SPEC,
            pl.BlockSpec((GROUP, inner), lambda i: (last - i, 0)),
            pl.BlockSpec(
                (8, inner), lambda i: (jnp.maximum((last - i) * (GROUP // 8) - 1, 0), 0)
            ),
            pl.BlockSpec((GROUP, 2 * size), lambda i: (last - i, 0)),
            pl.BlockSpec((GROUP, LANES), lambda i: (last - i, 0)),
            pl.BlockSpec((GROUP, inner), lambda i: (last - i, 0)),
            pl.BlockSpec((GROUP, inner), lambda i: (last - i, 0)),
            pl.BlockSpec((size, inner), lambda i: (last - i, 0)),
            whole(8, inner), whole(8, LANES),
        ],
        out_specs=[
            pl.BlockSpec((GROUP, inner), lambda i: (last - i, 0)),
            pl.BlockSpec((GROUP, 2 * size), lambda i: (last - i, 0)),
            pl.BlockSpec((GROUP, LANES), lambda i: (last - i, 0)),
            whole(8, inner), whole(8, LANES),
        ],
        out_shape=[
            shape_of((tokens, inner), BF16),
            shape_of((tokens, 2 * size), BF16),
            shape_of((tokens, LANES), BF16),
            shape_of((8, inner), F32),
            shape_of((8, LANES), F32),
        ],
        scratch_shapes=[
            pltpu.VMEM((GROUP + 8, inner), F32),
            pltpu.VMEM((GROUP + 8, inner), F32),
            pltpu.VMEM((size, inner), F32),
            pltpu.VMEM((LANES, inner), BF16),
            pltpu.VMEM((inner, LANES), BF16),
            pltpu.VMEM((GROUP, GROUP), BF16),
            pltpu.VMEM((GROUP, GROUP), BF16),
            pltpu.VMEM((3 * GROUP + 16, inner), F32),
            pltpu.VMEM((GROUP, inner), F32),
            pltpu.VMEM((GROUP, GROUP), F32),
            pltpu.VMEM((GROUP, GROUP), F32),
            pltpu.VMEM((GROUP, GROUP), F32),
            pltpu.VMEM((GROUP, inner), BF16),
            pltpu.VMEM((GROUP, inner), BF16),
            pltpu.VMEM((4 * GROUP, inner), BF16),
        ],
        compiler_params=params(),
        cost_estimate=cost(2),
        name="mixer_backward",
    )(
        lengths, inner_pre, inner_pre, state_act, step_in, mixed, grad_first, prev_states,
        rows, head_rows,
    )

    window = half_rows + HALO
    kq_own = lax.dynamic_slice_in_dim(grad_kq, tensor_rank * (half_rows - HALO), window)
    kq_away = lax.dynamic_slice_in_dim(grad_kq, (1 - tensor_rank) * (half_rows - HALO), window)
    kq_other = exchange(kq_away)
    grad_inner_low, kq_other, mix_other, first_sum = lax.optimization_barrier(
        (grad_inner_low, kq_other, mix_other, first_sum)
    )
    mix = mix_here + mix_other.astype(F32)
    slot = tensor_rank * half_rows + jnp.arange(half_rows, dtype=jnp.int32)
    valid_half = slot < jnp.sum(lengths[0])
    hidden_wide = hidden_in.astype(F32)
    block_out = (hidden_wide + jnp.where(valid_half[:, None], mix, 0.0)).astype(BF16)


    def partial_normed(which):
        return (
            nt(rows_of(grad_gate_low, which), w_gate)
            + nt(rows_of(grad_inner_low, which), w_inner)
            + nt(rows_of(grad_step_low, which), w_step)
        )

    normed_away = exchange(partial_normed(1 - tensor_rank).astype(BF16))
    normed_here = partial_normed(tensor_rank)
    inner_sum = scatter_by_bits(
        nn(normed_t, grad_inner_low).astype(BF16), shard_rank, shard_count, False
    )

    vmem = pl.BlockSpec(memory_space=pltpu.VMEM)
    grad_state_low, rest_grads = pl.pallas_call(
        functools.partial(
            state_grad_kernel, shard=shard, state_shard=state_shard, heads=heads
        ),
        in_specs=[SMEM_SPEC, SMEM_SPEC] + [vmem] * 9,
        out_specs=[vmem] * 2,
        out_shape=[shape_of((tokens, 2 * size), BF16), shape_of((width, 2 * size + LANES), BF16)],
        scratch_shapes=[
            pltpu.VMEM((8, 2 * size), F32),
            pltpu.VMEM((window + 8, 2 * size), F32),
            pltpu.VMEM((window + 8, 2 * size), F32),
            pltpu.VMEM((LANES, width), F32),
        ],
        compiler_params=params(),
        cost_estimate=cost(8),
        name="state_backward",
    )(
        rank, lengths, kq_own, kq_other, state_pre, state_rows, normed_t, grad_step_low,
        conv_rows, gain_rows, head_sums,
    )
    rest_sum = scatter_by_bits(rest_grads, shard_rank, shard_count, True)

    grad_normed = normed_here + normed_away.astype(F32)
    grad_normed = grad_normed + nt(rows_of(grad_state_low, tensor_rank), w_state)
    gain = rows[ROW_NORM][None, :]
    inv_rms = lax.rsqrt(jnp.mean(hidden_wide * hidden_wide, axis=1, keepdims=True) + NORM_EPS)
    scaled_in = grad_normed * gain
    grad_hidden = (
        inv_rms * scaled_in
        - hidden_wide * inv_rms**3 * jnp.mean(scaled_in * hidden_wide, axis=1, keepdims=True)
        + cotangent.astype(F32)
    )

    grad_pgi, packed = pl.pallas_call(
        finish_kernel,
        in_specs=[vmem] * 6,
        out_specs=[vmem] * 2,
        out_shape=[shape_of((shard, 2, inner), F32), shape_of((shard, 2 * size + LANES), F32)],
        compiler_params=params(),
        cost_estimate=cost(1),
        name="finish",
    )(
        first_sum[:, inner:], inner_sum, rest_sum,
        projection_gate_inner.reshape(shard, 2 * inner), proj_state, proj_step,
    )
    (
        grad_state, grad_step, grad_gain, grad_conv, grad_bias, grad_taps, grad_taps_bias,
        grad_decay, grad_skip, grad_step_bias, grad_gate_gain,
    ) = pl.pallas_call(
        unpack_kernel,
        in_specs=[vmem] * 3,
        out_specs=[vmem] * 11,
        out_shape=[
            shape_of(dims, F32)
            for dims in (
                (shard, 2 * size), (shard, heads), (1, shard), (taps, shard), (1, shard),
                (taps, state_shard), (1, state_shard), (1, heads), (1, heads), (1, heads),
                (1, shard),
            )
        ],
        compiler_params=params(),
        cost_estimate=cost(1),
        name="unpack_small",
    )(packed, exchange(packed), norm_gain[None, :])
    return (
        block_out,
        grad_hidden,
        grad_gain[0],
        grad_pgi,
        grad_state,
        grad_step,
        grad_conv[:, None, :],
        grad_bias,
        grad_taps,
        grad_taps_bias[0],
        grad_decay[0],
        grad_skip[0],
        grad_step_bias[0],
        grad_gate_gain,
        first_sum[:, :inner].astype(F32).T,
    )


def solution(mesh):
    placed = (
        P(("dp", "tensor"), None),
        P("dp"),
        P("dp", None, "tensor"),
        P("dp", None),
        P("dp", "tensor"),
        P(None, "tensor", "dp"),
        P("tensor", "dp"),
        P(None, "dp"),
        P("dp"),
        P("tensor"),
        P("tensor"),
        P("tensor"),
        P("tensor", "dp"),
        P("tensor", "dp"),
        P("dp", None),
        P(("dp", "tensor"), None),
    )
    return jax.shard_map(
        on_device,
        mesh=mesh,
        in_specs=placed,
        out_specs=(
            P(("dp", "tensor"), None),
            P(("dp", "tensor"), None),
            P("dp"),
            P("dp", None, "tensor"),
            P("dp", None),
            P("dp", "tensor"),
            P(None, "tensor", "dp"),
            P("tensor", "dp"),
            P(None, "dp"),
            P("dp"),
            P("tensor"),
            P("tensor"),
            P("tensor"),
            P("tensor", "dp"),
            P("tensor", "dp"),
        ),
        check_vma=False,
    )
```

```python
import functools

import jax
import jax.numpy as jnp
from jax import lax
from jax.experimental import pallas as pl
from jax.experimental.pallas import tpu as pltpu
from jax.sharding import PartitionSpec as P

GROUP = 256
HALF = GROUP // 2
LANES = 128
PAIR_HEADS = 2
NORM_EPS = 1e-05
LOG2E = 1.4426950408889634
MASKED = -1e30
VMEM_BYTES = 56 * 1024 * 1024

LANE_CONV, LANE_GATE, LANE_STATE, LANE_HEADS, LANE_GAIN = 16, 21, 24, 32, 127
HALO = 16

F32 = jnp.float32
BF16 = jnp.bfloat16

ROW_NORM, ROW_TAP, ROW_BIAS, ROW_GATE, ROW_SKIP = 0, 1, 5, 6, 7


def nn(left, right):
    return lax.dot_general(left, right, (((1,), (0,)), ((), ())), preferred_element_type=F32)


def nt(left, right):
    return lax.dot_general(left, right, (((1,), (1,)), ((), ())), preferred_element_type=F32)


def tn(left, right):
    return lax.dot_general(left, right, (((0,), (0,)), ((), ())), preferred_element_type=F32)


def split3(value):
    high = value.astype(BF16)
    rest = value - high.astype(F32)
    mid = rest.astype(BF16)
    low = (rest - mid.astype(F32)).astype(BF16)
    return high, mid, low


def exact_left(ones, value):
    lanes = value.shape[1]
    found = nn(ones, jnp.concatenate(split3(value), axis=1))
    return found[:, :lanes] + found[:, lanes : 2 * lanes] + found[:, 2 * lanes :]


def three_in_lanes(value, heads):
    high, mid, low = split3(value)
    lane = lax.broadcasted_iota(jnp.int32, value.shape, 1)
    parts = jnp.where(
        lane < heads,
        high.astype(F32),
        jnp.where(lane < 2 * heads, mid.astype(F32), low.astype(F32)),
    )
    return parts.astype(BF16)


def spread_matrix(heads, head_size):
    shape = (LANES, heads * head_size)
    lane = lax.broadcasted_iota(jnp.int32, shape, 0)
    channel = lax.broadcasted_iota(jnp.int32, shape, 1)
    owner = channel // head_size
    hit = (lane == owner) | (lane == owner + heads) | (lane == owner + 2 * heads)
    return hit.astype(F32).astype(BF16)


def collect_matrix(heads, head_size):
    shape = (heads * head_size, LANES)
    lane = lax.broadcasted_iota(jnp.int32, shape, 1)
    owner = lax.broadcasted_iota(jnp.int32, shape, 0) // head_size
    hit = (lane == owner) | (lane == owner + heads) | (lane == owner + 2 * heads)
    return hit.astype(F32).astype(BF16)


def spaced_matrix(narrow, wide, narrow_shard, wide_shard, compress):
    shape = (wide, narrow) if compress else (narrow, wide)
    at_wide = lax.broadcasted_iota(jnp.int32, shape, 0 if compress else 1)
    at_narrow = lax.broadcasted_iota(jnp.int32, shape, 1 if compress else 0)
    owner, place = at_wide // wide_shard, at_wide % wide_shard
    hit = (place < narrow_shard) & (at_narrow == owner * narrow_shard + place)
    return hit.astype(F32).astype(BF16)


def pack_kernel(
    inner_ref, state_ref, step_ref, norm_ref, conv_ref, bias_ref, gate_ref, taps_ref,
    taps_bias_ref, out_ref, turned, lanes,
):
    shard, heads = step_ref.shape
    inner, states = inner_ref.shape[1], state_ref.shape[1]
    state_shard = taps_ref.shape[1]
    base = 3 * heads
    turned[...] = jnp.zeros_like(turned)
    turned[base : base + 1, 0:shard] = norm_ref[...].astype(F32)
    turned[base + 1 : base + 5, 0:shard] = conv_ref[...].astype(F32)
    turned[base + 5 : base + 6, 0:shard] = bias_ref[...].astype(F32)
    turned[base + 6 : base + 7, 0:shard] = gate_ref[...].astype(F32)
    turned[base + 8 : base + 12, 0:state_shard] = taps_ref[...].astype(F32)
    turned[base + 12 : base + 13, 0:state_shard] = taps_bias_ref[...].astype(F32)
    lanes[...] = jnp.zeros_like(lanes)
    step = step_ref[...].astype(F32)
    for copy in range(3):
        lanes[:, copy * heads : (copy + 1) * heads] = step
    out_ref[:, :inner] = inner_ref[...]
    out_ref[:, inner : inner + states] = state_ref[...]
    out_ref[:, inner + states :] = (turned[...].T[0:shard, :] + lanes[...]).astype(BF16)


def lower_matrix(upper=False):
    row = lax.broadcasted_iota(jnp.int32, (GROUP, GROUP), 0)
    col = lax.broadcasted_iota(jnp.int32, (GROUP, GROUP), 1)
    hit = (col >= row) if upper else (col <= row)
    return hit.astype(F32).astype(BF16)


def sequence_ends(len_ref):
    ends, total = [], jnp.int32(0)
    for slot in range(len_ref.shape[1]):
        total = total + len_ref[0, slot]
        ends.append(total)
    return ends


def sequence_of(ends, token):
    found = (token >= ends[0]).astype(jnp.int32)
    for end in ends[1:]:
        found = found + (token >= end).astype(jnp.int32)
    return found


def scalar_sequence_of(ends, token):
    found = jnp.where(token >= ends[0], 1, 0)
    for end in ends[1:]:
        found = found + jnp.where(token >= end, 1, 0)
    return found


def position_of(ends, token):
    start = jnp.zeros_like(token)
    for end in ends:
        start = jnp.where(token >= end, end, start)
    return token - start


def tokens_column(first, rows=GROUP):
    return first + lax.broadcasted_iota(jnp.int32, (rows, 1), 0)


def additive_mask(ends, first, transposed):
    rows = first + lax.broadcasted_iota(jnp.int32, (GROUP, GROUP), 0)
    cols = first + lax.broadcasted_iota(jnp.int32, (GROUP, GROUP), 1)
    ordered = (cols >= rows) if transposed else (rows >= cols)
    kept = (sequence_of(ends, rows) == sequence_of(ends, cols)) & ordered
    return jnp.where(kept, 0.0, MASKED)


def softplus(value):
    return jnp.maximum(value, 0.0) + jnp.log1p(jnp.exp(-jnp.abs(value)))


def sigmoid(value):
    return 0.5 * jnp.tanh(0.5 * value) + 0.5


def decay_terms(ends, first, step_in, rate, lower):
    group = first // GROUP
    step = softplus(step_in)
    cum = exact_left(lower, step * (rate * LOG2E))
    last = cum[GROUP - 1 : GROUP, :]
    sequence = sequence_of(ends, tokens_column(first))
    tail = scalar_sequence_of(ends, first + GROUP - 1)
    before = jnp.where(group > 0, scalar_sequence_of(ends, first - 1), -1)
    in_tail = (sequence == tail).astype(F32)
    entered = (sequence == before).astype(F32)
    carried = jnp.where(tail == before, 1.0, 0.0)
    key_factor = jnp.exp2(last - cum) * in_tail
    entry = jnp.exp2(cum) * entered
    decay = jnp.exp2(last) * carried
    return step, cum, key_factor, entry, decay


def head_masks():
    lane = lax.broadcasted_iota(jnp.int32, (1, LANES), 1)
    first = (lane < LANES // 2).astype(F32)
    return first, 1.0 - first


def forward_kernel(
    rank_ref, len_ref, own_ref, other_ref, w_ref, head_ref,
    normed_ref, normed_t_ref, ipre_ref, spre_ref, sact_ref, stepin_ref, mixed_ref, sprev_ref,
    rows_ref, taps_ref,
    ext, state, spread, lower, fac, read, mask, scores, weighted, factors, *, shard, state_shard,
):
    inner = rows_ref.shape[1]
    channels = ext.shape[1]
    heads = inner // (LANES // PAIR_HEADS)
    size = sprev_ref.shape[0]
    group = pl.program_id(0)
    first = group * GROUP
    ends = sequence_ends(len_ref)

    @pl.when(group == 0)
    def _():
        ext[0:8, :] = jnp.zeros((8, channels), F32)
        state[...] = jnp.zeros_like(state)
        spread[...] = spread_matrix(heads, LANES // PAIR_HEADS)
        lower[...] = lower_matrix()
        factors[...] = jnp.zeros_like(factors)
        packed = w_ref[:, channels:].astype(F32).T
        base = 3 * heads
        rows_ref[0:7, :] = packed[base : base + 7, :]
        once = lax.broadcasted_iota(jnp.int32, (16, LANES), 1) < heads
        skip_row = jnp.where(once, head_ref[2:3, :], 0.0).astype(BF16)
        rows_ref[7:8, :] = nn(skip_row, spread[...])[0:1, :]
        taps_ref[...] = nn(
            packed[base + 8 : base + 16, :].astype(BF16),
            spaced_matrix(2 * size, w_ref.shape[0], state_shard, shard, True),
        )

    mine = rank_ref[0, 0] == group // (pl.num_programs(0) // 2)
    gain = rows_ref[ROW_NORM : ROW_NORM + 1, :]
    for part in range(4):
        sl = slice(part * 64, part * 64 + 64)
        hidden = jnp.where(mine, own_ref[sl, :].astype(F32), other_ref[sl, :].astype(F32))
        inv = lax.rsqrt(jnp.mean(hidden * hidden, axis=1, keepdims=True) + NORM_EPS)
        normed_ref[sl, :] = (hidden * inv * gain).astype(BF16)

    normed_t_ref[...] = normed_ref[...].T
    pre = nn(normed_ref[...], w_ref[:, :inner])
    ext[8 : 8 + GROUP, 0:inner] = pre
    ipre_ref[...] = pre
    rest = nn(normed_ref[...], w_ref[:, inner:])
    ext[8 : 8 + GROUP, inner:channels] = rest[:, : 2 * size]
    spre_ref[...] = rest[:, : 2 * size]
    lane = lax.broadcasted_iota(jnp.int32, (1, LANES), 1)
    step_in = jnp.where(lane < 3 * heads, rest[:, 2 * size :], 0.0) + head_ref[0:1, :]
    stepin_ref[...] = step_in

    token = tokens_column(first)
    position = position_of(ends, token)
    keep = [(position >= offset).astype(F32) for offset in (1, 2, 3)]

    def conv(sl, taps, bias):
        total = bias + taps[3:4, :] * ext[8 : 8 + GROUP, sl]
        for offset in (1, 2, 3):
            total = total + keep[offset - 1] * (
                taps[3 - offset : 4 - offset, :] * ext[8 - offset : 8 - offset + GROUP, sl]
            )
        return total

    for part in range(2):
        sl = slice(inner + part * size, inner + (part + 1) * size)
        own = slice(part * size, (part + 1) * size)
        total = conv(sl, taps_ref[0:4, own], taps_ref[4:5, own])
        sact_ref[:, own] = (total * sigmoid(total)).astype(BF16)
    keys = sact_ref[:, :size]
    queries = sact_ref[:, size:]
    scores[...] = nt(queries, keys)
    mask[...] = additive_mask(ends, first, False)

    step, cum, key_factor, entry, decay = decay_terms(
        ends, first, step_in, head_ref[1:2, :], lower[...]
    )
    cum_rows = cum.T
    stacked = jnp.concatenate(
        [step, key_factor * step, entry, jnp.broadcast_to(decay, (16, LANES))], axis=0
    )
    fac[...] = nn(three_in_lanes(stacked, heads), spread[...])
    held = state[...].astype(BF16)
    sprev_ref[...] = held
    read[...] = nn(queries, held)

    first_head = lax.broadcasted_iota(jnp.int32, (1, LANES), 1) < LANES // PAIR_HEADS
    lo, hi = slice(0, HALF), slice(HALF, GROUP)
    for pair in range(inner // LANES):
        sl = slice(pair * LANES, (pair + 1) * LANES)
        total = conv(sl, rows_ref[ROW_TAP : ROW_TAP + 4, sl], rows_ref[ROW_BIAS : ROW_BIAS + 1, sl])
        values = (total * sigmoid(total)).astype(BF16).astype(F32)
        stepped = (values * fac[0:GROUP, sl]).astype(BF16)
        weighted[:, sl] = (values * fac[GROUP : 2 * GROUP, sl]).astype(BF16)
        slot = pair % 2
        for which in range(PAIR_HEADS):
            head = pair * PAIR_HEADS + which
            column = cum[:, head : head + 1]
            row = cum_rows[head : head + 1, :]
            for rs, cs in ((lo, lo), (hi, lo), (hi, hi)):
                gap = column[rs] - row[:, cs] + mask[rs, cs]
                place = slice(which * GROUP + rs.start, which * GROUP + rs.stop)
                factors[slot, place, cs] = (jnp.exp2(gap) * scores[rs, cs]).astype(BF16)
        both = nn(factors[slot], stepped)
        within = jnp.where(first_head, both[:GROUP], both[GROUP:])
        mixed_ref[:, sl] = (
            within
            + fac[2 * GROUP : 3 * GROUP, sl] * read[:, sl]
            + rows_ref[ROW_SKIP : ROW_SKIP + 1, sl] * values
        )

    state[...] = fac[3 * GROUP : 3 * GROUP + 1, :] * state[...] + tn(keys, weighted[...])
    ext[0:8, :] = ext[GROUP : GROUP + 8, :]


def gate_kernel(
    rank_ref, len_ref, own_ref, other_ref, normed_ref, mixed_ref, w_ref, proj_ref, rows_ref,
    gate_ref, gol_ref, live_t_ref, sums_ref,
):
    group = pl.program_id(0)
    first = group * GROUP
    ends = sequence_ends(len_ref)
    mine = rank_ref[0, 0] == group // (pl.num_programs(0) // 2)
    valid = tokens_column(first) < ends[-1]
    cotangent = jnp.where(mine, own_ref[...].astype(F32), other_ref[...].astype(F32))
    live = jnp.where(valid, cotangent, 0.0).astype(BF16)
    live_t_ref[...] = live.T
    square = jnp.zeros((GROUP, LANES), F32)
    inner = jnp.zeros((GROUP, LANES), F32)
    for part in range(gate_ref.shape[1] // GROUP):
        sl = slice(part * GROUP, (part + 1) * GROUP)
        gate = nn(normed_ref[...], w_ref[:, sl])
        gol = nn(live, proj_ref[:, sl])
        gate_ref[:, sl] = gate
        gol_ref[:, sl] = gol
        gated = mixed_ref[:, sl] * (gate * sigmoid(gate))
        squares = gated * gated
        inners = gol * rows_ref[ROW_GATE : ROW_GATE + 1, sl] * gated
        square = square + squares[:, :LANES] + squares[:, LANES:]
        inner = inner + inners[:, :LANES] + inners[:, LANES:]
    lane = lax.broadcasted_iota(jnp.int32, (GROUP, LANES), 1)
    columns = jnp.where(
        lane < 4,
        jnp.sum(square, axis=1, keepdims=True),
        jnp.sum(inner, axis=1, keepdims=True),
    )
    sums_ref[...] = columns.T[0:8, :]


def gate_grad_kernel(
    own_sums_ref, other_sums_ref, gate_ref, gol_ref, mixed_ref, rows_ref,
    low_ref, first_ref, ggp_ref, gain_ref, *, inner_all,
):
    @pl.when(pl.program_id(0) == 0)
    def _():
        gain_ref[...] = jnp.zeros_like(gain_ref)

    totals = own_sums_ref[...] + other_sums_ref[...]
    columns = jnp.concatenate([totals, jnp.zeros((LANES - 8, GROUP), F32)], axis=0).T
    inv_all = lax.rsqrt(columns[:, 0:1] / inner_all + NORM_EPS)
    slope_all = inv_all * inv_all * inv_all * columns[:, 4:5] / inner_all
    gain = rows_ref[ROW_GATE : ROW_GATE + 1, :]
    total = jnp.zeros((1, gate_ref.shape[1]), F32)
    for part in range(8):
        sl = slice(part * 32, part * 32 + 32)
        inv, slope = inv_all[sl], slope_all[sl]
        gate, gol, mixed = gate_ref[sl, :], gol_ref[sl, :], mixed_ref[sl, :]
        logistic = sigmoid(gate)
        silu = gate * logistic
        gated = mixed * silu
        scaled = gated * inv
        low_ref[sl, :] = (scaled * gain).astype(BF16)
        total = total + jnp.sum(gol * scaled, axis=0, keepdims=True)
        grad = inv * (gol * gain) - gated * slope
        first_ref[sl, :] = (grad * silu).astype(BF16)
        ggp_ref[sl, :] = (grad * mixed * (logistic * (1.0 + gate * (1.0 - logistic)))).astype(BF16)
    gain_ref[0:1, :] += total


def product_kernel(left_ref, right_ref, out_ref):
    out_ref[...] = nn(left_ref[...], right_ref[...]).astype(out_ref.dtype)


def normed_grad_kernel(
    begin_ref, gate_ref, inner_ref, step_ref, w_gate_ref, w_inner_ref, w_step_ref, out_ref
):
    total = nt(gate_ref[...], w_gate_ref[...]) + nt(inner_ref[...], w_inner_ref[...])
    out_ref[...] = (total + nt(step_ref[...], w_step_ref[...])).astype(out_ref.dtype)


def backward_kernel(
    len_ref, ipre_ref, halo_ref, sact_ref, stepin_ref, mixed_ref, first_ref, sprev_ref,
    rows_ref, head_ref,
    gip_ref, gkq_ref, gstep_ref, conv_ref, heads_ref,
    ext, cext, gstate, spread, collect, lower, upper, fac, reads, mask, scores, gscores,
    weighted, entered, sums, factors,
):
    inner = rows_ref.shape[1]
    heads = inner // (LANES // PAIR_HEADS)
    size = sprev_ref.shape[0]
    turn = pl.program_id(0)
    group = pl.num_programs(0) - 1 - turn
    first = group * GROUP
    ends = sequence_ends(len_ref)

    @pl.when(turn == 0)
    def _():
        cext[GROUP : GROUP + 8, :] = jnp.zeros((8, inner), F32)
        gstate[...] = jnp.zeros_like(gstate)
        spread[...] = spread_matrix(heads, LANES // PAIR_HEADS)
        collect[...] = collect_matrix(heads, LANES // PAIR_HEADS)
        lower[...] = lower_matrix()
        upper[...] = lower_matrix(upper=True)
        factors[...] = jnp.zeros_like(factors)
        conv_ref[...] = jnp.zeros_like(conv_ref)
        heads_ref[...] = jnp.zeros_like(heads_ref)

    ext[0:8, :] = jnp.where(group > 0, halo_ref[...], 0.0)
    ext[8 : 8 + GROUP, :] = ipre_ref[...]
    token = tokens_column(first)
    position = position_of(ends, token)
    keep = [(position >= offset).astype(F32) for offset in (1, 2, 3)]
    ahead = [(position_of(ends, token + offset) >= offset).astype(F32) for offset in (1, 2, 3)]

    step_in = stepin_ref[...]
    rate = head_ref[1:2, :]
    step, cum, key_factor, entry, decay = decay_terms(ends, first, step_in, rate, lower[...])
    cum_rows = cum.T
    key_step = key_factor * step
    stacked = jnp.concatenate(
        [step, key_step, entry, jnp.broadcast_to(decay, (16, LANES))], axis=0
    )
    fac[...] = nn(three_in_lanes(stacked, heads), spread[...])

    keys = sact_ref[:, :size]
    queries = sact_ref[:, size:]
    scores[...] = nt(keys, queries)
    mask[...] = additive_mask(ends, first, True)
    gscores[...] = jnp.zeros_like(gscores)
    held = gstate[...].astype(BF16)
    reads[...] = nn(keys, held)

    masks = head_masks()
    first_head = lax.broadcasted_iota(jnp.int32, (1, LANES), 1) < LANES // PAIR_HEADS
    lo, hi = slice(0, HALF), slice(HALF, GROUP)
    for pair in range(inner // LANES):
        sl = slice(pair * LANES, (pair + 1) * LANES)
        taps = rows_ref[ROW_TAP : ROW_TAP + 4, sl]
        shifted = [ext[8 - offset : 8 - offset + GROUP, sl] for offset in range(4)]
        total = rows_ref[ROW_BIAS : ROW_BIAS + 1, sl] + taps[3:4, :] * shifted[0]
        for offset in (1, 2, 3):
            total = total + keep[offset - 1] * (taps[3 - offset : 4 - offset, :] * shifted[offset])
        logistic = sigmoid(total)
        values = (total * logistic).astype(BF16).astype(F32)
        slope = logistic * (1.0 + total * (1.0 - logistic))
        step_wide = fac[0:GROUP, sl]
        key_wide = fac[GROUP : 2 * GROUP, sl]
        stepped = (values * step_wide).astype(BF16)
        stepped_wide = stepped.astype(F32)
        weighted[:, sl] = (values * key_wide).astype(BF16)
        upstream = first_ref[:, sl]
        upstream_wide = upstream.astype(F32)
        entered[:, sl] = (upstream_wide * fac[2 * GROUP : 3 * GROUP, sl]).astype(BF16)

        slot = pair % 2
        split = [(values * step_wide * one).astype(BF16) for one in masks]
        grads = nn(jnp.concatenate(split, axis=0), upstream.T)
        blocks = [None, None, None]
        for which in range(PAIR_HEADS):
            head = pair * PAIR_HEADS + which
            column = cum[:, head : head + 1]
            row = cum_rows[head : head + 1, :]
            for index, (rs, cs) in enumerate(((lo, lo), (lo, hi), (hi, hi))):
                factor = jnp.exp2(row[:, cs] - column[rs] + mask[rs, cs])
                place = slice(which * GROUP + rs.start, which * GROUP + rs.stop)
                factors[slot, place, cs] = (factor * scores[rs, cs]).astype(BF16)
                part = factor * grads[place, cs]
                blocks[index] = part if blocks[index] is None else blocks[index] + part
        gscores[lo, lo] += blocks[0]
        gscores[lo, hi] += blocks[1]
        gscores[hi, hi] += blocks[2]
        both = nn(factors[slot], upstream)
        raw = jnp.where(first_head, both[:GROUP], both[GROUP:])
        skip = rows_ref[ROW_SKIP : ROW_SKIP + 1, sl]
        across = reads[:, sl]

        balance = upstream_wide * (mixed_ref[:, sl] - skip * values) - stepped_wide * raw
        high = balance.astype(BF16)
        sums[0:GROUP, sl] = high
        sums[GROUP : 2 * GROUP, sl] = (balance - high.astype(F32)).astype(BF16)
        sums[2 * GROUP : 3 * GROUP, sl] = (values * raw).astype(BF16)
        sums[3 * GROUP : 4 * GROUP, sl] = (values * across).astype(BF16)
        conv_ref[5:6, sl] += jnp.sum(upstream_wide * values, axis=0, keepdims=True)
        inner_grad = step_wide * raw + key_wide * across + skip * upstream_wide
        grad = inner_grad * slope
        cext[0:GROUP, sl] = grad
        conv_ref[3:4, sl] += jnp.sum(grad * shifted[0], axis=0, keepdims=True)
        conv_ref[4:5, sl] += jnp.sum(grad, axis=0, keepdims=True)
        result = taps[3:4, :] * grad
        for offset in (1, 2, 3):
            conv_ref[3 - offset : 4 - offset, sl] += jnp.sum(
                keep[offset - 1] * grad * shifted[offset], axis=0, keepdims=True
            )
            result = result + ahead[offset - 1] * (
                taps[3 - offset : 4 - offset, :] * cext[offset : offset + GROUP, sl]
            )
        gip_ref[:, sl] = result.astype(BF16)

    cext[GROUP : GROUP + 8, :] = cext[0:8, :]
    state = sprev_ref[...]
    grad_scores = gscores[...].astype(BF16)
    gkq_ref[:, :size] = (nn(grad_scores, queries) + nt(weighted[...], held)).astype(BF16)
    gkq_ref[:, size:] = (tn(grad_scores, keys) + nt(entered[...], state)).astype(BF16)

    collected = nn(sums[...], collect[...])
    balance = collected[:GROUP] + collected[GROUP : 2 * GROUP]
    direct = collected[2 * GROUP : 3 * GROUP]
    key_dot = collected[3 * GROUP :]

    def row_collect(value):
        high = value.astype(BF16)
        low = (value - high.astype(F32)).astype(BF16)
        rows16 = jnp.concatenate(
            [jnp.broadcast_to(high, (8, inner)), jnp.broadcast_to(low, (8, inner))], axis=0
        )
        found = nn(rows16, collect[...])
        return found[0:1, :] + found[8:9, :]

    carry_term = decay * row_collect(
        jnp.sum(gstate[...] * state.astype(F32), axis=0, keepdims=True)
    )
    moved = key_step * key_dot
    grad_log = (
        exact_left(upper[...], balance) + carry_term + exact_left(lower[...], moved) - moved
    )
    grad_step = direct + key_factor * key_dot + grad_log * rate
    lane = lax.broadcasted_iota(jnp.int32, (1, LANES), 1)
    grad_step_in = jnp.where(lane < heads, grad_step * sigmoid(step_in), 0.0)
    gstep_ref[...] = grad_step_in.astype(BF16)
    heads_ref[0:1, :] += jnp.sum(grad_log * step * rate, axis=0, keepdims=True)
    heads_ref[1:2, :] += jnp.sum(grad_step_in, axis=0, keepdims=True)
    gstate[...] = fac[3 * GROUP : 3 * GROUP + 1, :] * gstate[...] + tn(queries, entered[...])

    @pl.when(turn == pl.num_programs(0) - 1)
    def _():
        heads_ref[2:3, :] = row_collect(conv_ref[5:6, :])


def state_grad_kernel(
    rank_ref, len_ref, own_ref, other_ref, spre_ref, taps_ref, normed_t_ref, gstep_ref,
    inner_rows_ref, gain_ref, heads_ref,
    gsp_ref, rest_ref, conv_ref, ext, cext, turned, *, shard, state_shard, heads,
):
    rows, channels = own_ref.shape
    width = rest_ref.shape[0]
    half = rows - HALO
    rank = rank_ref[0, 0]
    base = pl.multiple_of(rank * (half - HALO), HALO)
    chunk = window_chunk(rows)
    ends = sequence_ends(len_ref)
    before = spre_ref[pl.ds(pl.multiple_of(jnp.maximum(base - 8, 0), 8), 8), :]
    ext[0:8, :] = jnp.where(rank > 0, before, 0.0)
    ext[8 : 8 + rows, :] = spre_ref[pl.ds(base, rows), :]
    cext[rows : rows + 8, :] = jnp.zeros((8, channels), F32)
    conv_ref[...] = jnp.zeros_like(conv_ref)
    gsp_ref[...] = jnp.zeros_like(gsp_ref)
    for at in range(0, rows, chunk):
        token = tokens_column(base + at, chunk)
        position = position_of(ends, token)
        owned = ((token >= rank * half) & (token < (rank + 1) * half)).astype(F32)
        keep = [(position >= offset).astype(F32) for offset in (1, 2, 3)]
        for part in range(channels // LANES):
            sl = slice(part * LANES, (part + 1) * LANES)
            shifted = [ext[at + 8 - offset : at + 8 - offset + chunk, sl] for offset in range(4)]
            total = taps_ref[4:5, sl] + taps_ref[3:4, sl] * shifted[0]
            for offset in (1, 2, 3):
                total = total + keep[offset - 1] * (
                    taps_ref[3 - offset : 4 - offset, sl] * shifted[offset]
                )
            logistic = sigmoid(total)
            slope = logistic * (1.0 + total * (1.0 - logistic))
            upstream = own_ref[at : at + chunk, sl].astype(F32) + other_ref[
                at : at + chunk, sl
            ].astype(F32)
            grad = upstream * slope
            cext[at : at + chunk, sl] = grad
            grad = grad * owned
            conv_ref[4:5, sl] += jnp.sum(grad, axis=0, keepdims=True)
            conv_ref[3:4, sl] += jnp.sum(grad * shifted[0], axis=0, keepdims=True)
            for offset in (1, 2, 3):
                conv_ref[3 - offset : 4 - offset, sl] += jnp.sum(
                    keep[offset - 1] * grad * shifted[offset], axis=0, keepdims=True
                )
    for at in range(0, rows, chunk):
        token = tokens_column(base + at, chunk)
        owned = ((token >= rank * half) & (token < (rank + 1) * half)).astype(F32)
        ahead = [
            (position_of(ends, token + offset) >= offset).astype(F32) for offset in (1, 2, 3)
        ]
        for part in range(channels // LANES):
            sl = slice(part * LANES, (part + 1) * LANES)
            result = taps_ref[3:4, sl] * cext[at : at + chunk, sl]
            for offset in (1, 2, 3):
                result = result + ahead[offset - 1] * (
                    taps_ref[3 - offset : 4 - offset, sl]
                    * cext[at + offset : at + offset + chunk, sl]
                )
            place = pl.ds(pl.multiple_of(base + at, HALO), chunk)
            gsp_ref[place, sl] = (result * owned).astype(BF16)
    rest_ref[:, :channels] = nn(normed_t_ref[...], gsp_ref[...]).astype(BF16)
    step_part = nn(normed_t_ref[...], gstep_ref[...])
    turned[...] = jnp.zeros_like(turned)
    turned[LANE_CONV : LANE_CONV + 5, :] = inner_rows_ref[0:5, :]
    turned[LANE_GATE : LANE_GATE + 1, :] = gain_ref[0:1, :]
    turned[LANE_STATE : LANE_STATE + 8, :] = nn(
        conv_ref[...].astype(BF16), spaced_matrix(channels, width, state_shard, shard, False)
    )
    columns = jnp.concatenate([heads_ref[...], jnp.zeros((LANES - 8, LANES), F32)], axis=0).T
    for which in range(3):
        start = LANE_HEADS + which * heads
        turned[start : start + heads, :] = jnp.broadcast_to(
            columns[0:heads, which : which + 1], (heads, width)
        )
    rest_ref[:, channels:] = (step_part + turned[...].T).astype(BF16)


def window_chunk(rows):
    return max(n for n in range(HALO, GROUP + 1, HALO) if rows % n == 0)


def finish_kernel(
    first_ref, inner_ref, rest_ref, weight_ref, state_ref, step_ref, pgi_ref, packed_ref
):
    width = first_ref.shape[1]
    states = state_ref.shape[1]
    heads = step_ref.shape[1]
    shard = step_ref.shape[0]
    gate = first_ref[...].astype(F32)
    inner = inner_ref[...]
    rest = rest_ref[...]
    pgi_ref[:, 0:1, :] = gate[:, None, :]
    pgi_ref[:, 1:2, :] = inner[:, None, :]
    weight = weight_ref[...].astype(F32)
    product = jnp.sum(gate * weight[:, :width] + inner * weight[:, width:], axis=1, keepdims=True)
    product += jnp.sum(rest[:, :states] * state_ref[...].astype(F32), axis=1, keepdims=True)
    small = rest[:, states:]
    product += jnp.sum(small[:, :heads] * step_ref[...].astype(F32), axis=1, keepdims=True)
    lane = lax.broadcasted_iota(jnp.int32, (shard, LANES), 1)
    packed_ref[:, :states] = rest[:, :states]
    packed_ref[:, states:] = jnp.where(lane == LANE_GAIN, product, small)


def unpack_kernel(
    own_ref, other_ref, norm_ref,
    state_ref, step_ref, gain_ref, conv_ref, bias_ref, taps_ref, taps_bias_ref,
    decay_ref, skip_ref, step_bias_ref, gate_ref,
):
    shard, states = state_ref.shape
    heads = step_ref.shape[1]
    state_shard = taps_ref.shape[1]
    state_ref[...] = own_ref[:, :states] + other_ref[:, :states]
    small = own_ref[:, states:]
    both = small + other_ref[:, states:]
    step_ref[...] = small[:, :heads]

    def turn(value):
        if shard < LANES:
            value = jnp.concatenate([value, jnp.zeros((LANES - shard, LANES), F32)], axis=0)
        return value.T

    small_rows, both_rows = turn(small), turn(both)
    gain_ref[...] = both_rows[LANE_GAIN : LANE_GAIN + 1, :shard] / norm_ref[...].astype(F32)
    conv_ref[...] = small_rows[LANE_CONV : LANE_CONV + 4, :shard]
    bias_ref[...] = small_rows[LANE_CONV + 4 : LANE_CONV + 5, :shard]
    gate_ref[...] = small_rows[LANE_GATE : LANE_GATE + 1, :shard]
    taps_ref[...] = both_rows[LANE_STATE : LANE_STATE + 4, :state_shard]
    taps_bias_ref[...] = both_rows[LANE_STATE + 4 : LANE_STATE + 5, :state_shard]
    first = small[0:8, :]
    for which, out_ref in enumerate((decay_ref, step_bias_ref, skip_ref)):
        start = LANE_HEADS + which * heads
        out_ref[...] = pltpu.roll(first, LANES - start, 1)[0:1, :heads]


def shape_of(dims, dtype):
    return jax.ShapeDtypeStruct(dims, dtype)


def params(**kwargs):
    return pltpu.CompilerParams(vmem_limit_bytes=VMEM_BYTES, **kwargs)


def cost(micros):
    return pl.CostEstimate(flops=int(micros * 1.1e9), bytes_accessed=0, transcendentals=0)


SMEM_SPEC = pl.BlockSpec(memory_space=pltpu.SMEM)


def whole(*dims):
    return pl.BlockSpec(dims, lambda i: (0,) * len(dims))


def bit_order(count, spread_first):
    bits = list(range(count.bit_length() - 1))
    return [0] + bits[2:] + [1] if spread_first and len(bits) > 1 else bits


def flip(value, bit, count):
    return lax.ppermute(value, "dp", [(i, i ^ (1 << bit)) for i in range(count)])


def after(value, *others):
    return lax.optimization_barrier((value, *others))[0]


def gather_by_bits(value, rank, count, spread_first, waits):
    held, begun = [], []
    rows, lanes = value.shape
    for bit in reversed(bit_order(count, spread_first)):
        if 0 < len(begun) <= len(waits):
            value = after(value, waits[len(begun) - 1])
        begun.append(value)
        other = flip(value, bit, count)
        held = sorted(held + [bit], reverse=True)
        low = (rank >> bit) & 1 == 0
        value = jnp.stack(
            [jnp.where(low, value, other), jnp.where(low, other, value)], axis=held.index(bit)
        )
    return value.reshape(count * rows, lanes), begun


class HalvingSum:
    def __init__(self, value, rank, count, spread_first):
        self.rank, self.count = rank, count
        self.left = list(reversed(range(count.bit_length() - 1)))
        self.order = bit_order(count, spread_first)
        rows = value.shape[0] // count
        self.value = value.reshape([2] * len(self.left) + [rows, value.shape[1]])

    def start(self):
        bit = self.order.pop(0)
        axis = self.left.index(bit)
        mine = (self.rank >> bit) & 1
        self.away = lax.dynamic_index_in_dim(self.value, 1 - mine, axis, keepdims=False)
        self.here = lax.dynamic_index_in_dim(self.value, mine, axis, keepdims=False)
        self.came = flip(self.away, bit, self.count)
        self.bit = bit

    def step(self, *others):
        came = after(self.came, *others) if others else self.came
        self.left.remove(self.bit)
        self.value = self.here.astype(F32) + came.astype(F32)
        if self.left:
            self.value = self.value.astype(BF16)
            self.start()


def on_device(
    hidden_in,
    norm_gain,
    projection_gate_inner,
    proj_state,
    proj_step,
    conv_inner,
    conv_inner_bias,
    conv_state,
    conv_state_bias,
    decay_log,
    skip_gain,
    step_bias,
    gate_gain,
    proj_out,
    lengths,
    cotangent,
):
    tensor_count = lax.axis_size("tensor")
    tensor_rank = lax.axis_index("tensor")
    shard_rank = lax.axis_index("dp")
    shard_count = lax.axis_size("dp")
    half_rows, width = hidden_in.shape
    tokens = half_rows * tensor_count
    groups = tokens // GROUP
    half_groups = groups // 2
    inner = proj_out.shape[0]
    inner_all = inner * tensor_count
    heads = decay_log.shape[0]
    head_size = inner // heads
    size = proj_state.shape[1] // 2
    taps = conv_inner.shape[0]
    shard = width // shard_count
    channels = inner + 2 * size
    swap = [(0, 1), (1, 0)]

    def exchange(value):
        return lax.ppermute(value, "tensor", swap)

    pieces = []
    cuts = [0, GROUP // 4] + [GROUP * count for count in range(1, half_groups + 1)]
    for begin, end in zip(cuts, cuts[1:]):
        piece = hidden_in[begin:end]
        pieces.append(exchange(after(piece, pieces[-1]) if pieces else piece))
    hidden_other = jnp.concatenate(pieces, axis=0)
    cotangent_other = exchange(after(cotangent, pieces[-1]))

    state_shard = conv_state.shape[1]
    first_shard = pl.pallas_call(
        pack_kernel,
        in_specs=[pl.BlockSpec(memory_space=pltpu.VMEM)] * 9,
        out_specs=pl.BlockSpec(memory_space=pltpu.VMEM),
        out_shape=shape_of((shard, channels + LANES), BF16),
        scratch_shapes=[
            pltpu.VMEM((LANES, max(LANES, shard)), F32),
            pltpu.VMEM((shard, LANES), F32),
        ],
        compiler_params=params(),
        cost_estimate=cost(0),
        name="pack_small",
    )(
        projection_gate_inner[:, 1], proj_state, proj_step, norm_gain[None, :], conv_inner.reshape(taps, shard),
        conv_inner_bias, gate_gain, conv_state, conv_state_bias[None, :],
    )
    w_first, begun = gather_by_bits(first_shard, shard_rank, shard_count, False, pieces)
    second_shard = jnp.concatenate([projection_gate_inner[:, 0], proj_out.T], axis=1)
    second_shard = after(second_shard, begun[min(2, len(begun) - 1)])
    w_second = lax.all_gather(second_shard, "dp", axis=0, tiled=True)
    w_out = w_second[:, inner:]

    rate = -jnp.exp(decay_log.astype(F32))
    head_rows = jnp.stack([step_bias.astype(F32), rate, skip_gain.astype(F32)])
    head_rows = jnp.pad(jnp.tile(head_rows, (1, 3)), ((0, 5), (0, LANES - 3 * heads)))
    rank = tensor_rank.astype(jnp.int32).reshape(1, 1)

    def by_group(lanes):
        return pl.BlockSpec((GROUP, lanes), lambda i: (i, 0))

    half_block = pl.BlockSpec((GROUP, width), lambda i: (i % half_groups, 0))
    (
        normed, normed_t, inner_pre, state_pre, state_act, step_in, mixed, prev_states, rows,
        state_rows,
    ) = pl.pallas_call(
        functools.partial(forward_kernel, shard=shard, state_shard=state_shard),
        grid=(groups,),
        in_specs=[
            SMEM_SPEC, SMEM_SPEC, half_block, half_block,
            whole(width, channels + LANES), whole(8, LANES),
        ],
        out_specs=[
            by_group(width), pl.BlockSpec((width, GROUP), lambda i: (0, i)), by_group(inner), by_group(2 * size), by_group(2 * size),
            by_group(LANES), by_group(inner), pl.BlockSpec((size, inner), lambda i: (i, 0)),
            whole(8, inner), whole(8, 2 * size),
        ],
        out_shape=[
            shape_of((tokens, width), BF16),
            shape_of((width, tokens), BF16),
            shape_of((tokens, inner), F32),
            shape_of((tokens, 2 * size), F32),
            shape_of((tokens, 2 * size), BF16),
            shape_of((tokens, LANES), F32),
            shape_of((tokens, inner), F32),
            shape_of((groups * size, inner), BF16),
            shape_of((8, inner), F32),
            shape_of((8, 2 * size), F32),
        ],
        scratch_shapes=[
            pltpu.VMEM((GROUP + 8, channels), F32),
            pltpu.VMEM((size, inner), F32),
            pltpu.VMEM((LANES, inner), BF16),
            pltpu.VMEM((GROUP, GROUP), BF16),
            pltpu.VMEM((3 * GROUP + 16, inner), F32),
            pltpu.VMEM((GROUP, inner), F32),
            pltpu.VMEM((GROUP, GROUP), F32),
            pltpu.VMEM((GROUP, GROUP), F32),
            pltpu.VMEM((GROUP, inner), BF16),
            pltpu.VMEM((2, PAIR_HEADS * GROUP, GROUP), BF16),
        ],
        compiler_params=params(),
        cost_estimate=cost(2),
        name="mixer_forward",
    )(rank, lengths, hidden_in, hidden_other, w_first, head_rows)

    gate_pre, grad_out_low, live_t, sums = pl.pallas_call(
        gate_kernel,
        grid=(groups,),
        in_specs=[
            SMEM_SPEC, SMEM_SPEC, half_block, half_block, by_group(width), by_group(inner),
            pl.BlockSpec((width, inner), lambda i: (0, 0)),
            pl.BlockSpec((width, inner), lambda i: (0, 1)),
            whole(8, inner),
        ],
        out_specs=[
            by_group(inner), by_group(inner), pl.BlockSpec((width, GROUP), lambda i: (0, i)),
            pl.BlockSpec((8, GROUP), lambda i: (0, i)),
        ],
        out_shape=[
            shape_of((tokens, inner), F32),
            shape_of((tokens, inner), F32),
            shape_of((width, tokens), BF16),
            shape_of((8, tokens), F32),
        ],
        compiler_params=params(),
        cost_estimate=cost(16),
        name="gate_forward",
    )(rank, lengths, cotangent, cotangent_other, normed, mixed, w_second, w_second, rows)

    sums_other = exchange(sums)
    sum_block = pl.BlockSpec((8, GROUP), lambda i: (0, i))
    out_low, grad_first, grad_gate_low, gain_rows = pl.pallas_call(
        functools.partial(gate_grad_kernel, inner_all=inner_all),
        grid=(groups,),
        in_specs=[
            sum_block, sum_block, by_group(inner), by_group(inner), by_group(inner),
            whole(8, inner),
        ],
        out_specs=[by_group(inner), by_group(inner), by_group(inner), whole(8, inner)],
        out_shape=[
            shape_of((tokens, inner), BF16),
            shape_of((tokens, inner), BF16),
            shape_of((tokens, inner), BF16),
            shape_of((8, inner), F32),
        ],
        compiler_params=params(),
        cost_estimate=cost(13),
        name="gate_backward",
    )(sums, sums_other, gate_pre, grad_out_low, mixed, rows)

    first_grads = jnp.concatenate(
        [nn(live_t, out_low).astype(BF16), nn(normed_t, grad_gate_low).astype(BF16)], axis=1
    )
    def rows_of(value, which):
        return lax.dynamic_slice_in_dim(value, which * half_rows, half_rows)

    first_sum = lax.psum_scatter(first_grads, "dp", scatter_dimension=0, tiled=True)
    out_low = after(out_low, first_grads)
    mix_away = nt(rows_of(out_low, 1 - tensor_rank), w_out).astype(BF16)
    grad_first = after(grad_first, mix_away)
    mix_other = exchange(mix_away)
    mix_here = nt(rows_of(out_low, tensor_rank), w_out)
    last = groups - 1
    grad_inner_low, grad_kq, grad_step_low, conv_rows, head_sums = pl.pallas_call(
        backward_kernel,
        grid=(groups,),
        in_specs=[
            SMEM_SPEC,
            pl.BlockSpec((GROUP, inner), lambda i: (last - i, 0)),
            pl.BlockSpec(
                (8, inner), lambda i: (jnp.maximum((last - i) * (GROUP // 8) - 1, 0), 0)
            ),
            pl.BlockSpec((GROUP, 2 * size), lambda i: (last - i, 0)),
            pl.BlockSpec((GROUP, LANES), lambda i: (last - i, 0)),
            pl.BlockSpec((GROUP, inner), lambda i: (last - i, 0)),
            pl.BlockSpec((GROUP, inner), lambda i: (last - i, 0)),
            pl.BlockSpec((size, inner), lambda i: (last - i, 0)),
            whole(8, inner), whole(8, LANES),
        ],
        out_specs=[
            pl.BlockSpec((GROUP, inner), lambda i: (last - i, 0)),
            pl.BlockSpec((GROUP, 2 * size), lambda i: (last - i, 0)),
            pl.BlockSpec((GROUP, LANES), lambda i: (last - i, 0)),
            whole(8, inner), whole(8, LANES),
        ],
        out_shape=[
            shape_of((tokens, inner), BF16),
            shape_of((tokens, 2 * size), BF16),
            shape_of((tokens, LANES), BF16),
            shape_of((8, inner), F32),
            shape_of((8, LANES), F32),
        ],
        scratch_shapes=[
            pltpu.VMEM((GROUP + 8, inner), F32),
            pltpu.VMEM((GROUP + 8, inner), F32),
            pltpu.VMEM((size, inner), F32),
            pltpu.VMEM((LANES, inner), BF16),
            pltpu.VMEM((inner, LANES), BF16),
            pltpu.VMEM((GROUP, GROUP), BF16),
            pltpu.VMEM((GROUP, GROUP), BF16),
            pltpu.VMEM((3 * GROUP + 16, inner), F32),
            pltpu.VMEM((GROUP, inner), F32),
            pltpu.VMEM((GROUP, GROUP), F32),
            pltpu.VMEM((GROUP, GROUP), F32),
            pltpu.VMEM((GROUP, GROUP), F32),
            pltpu.VMEM((GROUP, inner), BF16),
            pltpu.VMEM((GROUP, inner), BF16),
            pltpu.VMEM((4 * GROUP, inner), BF16),
            pltpu.VMEM((2, PAIR_HEADS * GROUP, GROUP), BF16),
        ],
        compiler_params=params(),
        cost_estimate=cost(2),
        name="mixer_backward",
    )(
        lengths, inner_pre, inner_pre, state_act, step_in, mixed, grad_first, prev_states,
        rows, head_rows,
    )

    window = half_rows + HALO
    kq_own = lax.dynamic_slice_in_dim(grad_kq, tensor_rank * (half_rows - HALO), window)
    kq_away = lax.dynamic_slice_in_dim(grad_kq, (1 - tensor_rank) * (half_rows - HALO), window)
    kq_other = exchange(kq_away)

    grad_inner_low = after(grad_inner_low, mix_other)
    inner_grads = pl.pallas_call(
        product_kernel,
        grid=(inner // GROUP,),
        in_specs=[whole(width, tokens), pl.BlockSpec((tokens, GROUP), lambda i: (0, i))],
        out_specs=pl.BlockSpec((width, GROUP), lambda i: (0, i)),
        out_shape=shape_of((width, inner), BF16),
        compiler_params=params(),
        cost_estimate=cost(0),
        name="inner_weight_grads",
    )(normed_t, grad_inner_low)
    inner_sum = HalvingSum(inner_grads, shard_rank, shard_count, False)
    inner_sum.start()

    def normed_part(which, gip, dtype):
        def block(i, begin):
            return (begin[0] + i, 0)

        return pl.pallas_call(
            normed_grad_kernel,
            grid_spec=pltpu.PrefetchScalarGridSpec(
                num_scalar_prefetch=1,
                grid=(half_groups,),
                in_specs=[
                    pl.BlockSpec((GROUP, inner), block),
                    pl.BlockSpec((GROUP, inner), block),
                    pl.BlockSpec((GROUP, LANES), block),
                    pl.BlockSpec((width, inner), lambda i, begin: (0, 0)),
                    pl.BlockSpec((width, inner), lambda i, begin: (0, 0)),
                    pl.BlockSpec((width, LANES), lambda i, begin: (0, channels // LANES)),
                ],
                out_specs=pl.BlockSpec((GROUP, width), lambda i, begin: (i, 0)),
            ),
            out_shape=shape_of((half_rows, width), dtype),
            compiler_params=params(),
            cost_estimate=cost(0),
            name="normed_grads",
        )(
            (which * half_groups).astype(jnp.int32).reshape(1),
            grad_gate_low, gip, grad_step_low, w_second, w_first, w_first,
        )

    grad_inner_low, first_sum, _ = lax.optimization_barrier(
        (grad_inner_low, first_sum, inner_sum.away)
    )
    normed_away = normed_part(1 - tensor_rank, grad_inner_low, BF16)
    normed_other = exchange(normed_away)
    mix = mix_here + mix_other.astype(F32)
    slot = tensor_rank * half_rows + jnp.arange(half_rows, dtype=jnp.int32)
    valid_half = slot < jnp.sum(lengths[0])
    hidden_wide = hidden_in.astype(F32)
    block_out = (hidden_wide + jnp.where(valid_half[:, None], mix, 0.0)).astype(BF16)

    vmem = pl.BlockSpec(memory_space=pltpu.VMEM)
    kq_other = after(kq_other, normed_away)
    grad_state_low, rest_grads = pl.pallas_call(
        functools.partial(
            state_grad_kernel, shard=shard, state_shard=state_shard, heads=heads
        ),
        in_specs=[SMEM_SPEC, SMEM_SPEC] + [vmem] * 9,
        out_specs=[vmem] * 2,
        out_shape=[shape_of((tokens, 2 * size), BF16), shape_of((width, 2 * size + LANES), BF16)],
        scratch_shapes=[
            pltpu.VMEM((8, 2 * size), F32),
            pltpu.VMEM((window + 8, 2 * size), F32),
            pltpu.VMEM((window + 8, 2 * size), F32),
            pltpu.VMEM((LANES, width), F32),
        ],
        compiler_params=params(),
        cost_estimate=cost(0),
        name="state_backward",
    )(
        rank, lengths, kq_own, kq_other, state_pre, state_rows, normed_t, grad_step_low,
        conv_rows, gain_rows, head_sums,
    )
    rest_sum = HalvingSum(rest_grads, shard_rank, shard_count, True)
    rest_sum.start()
    inner_sum.step()
    normed_here = normed_part(
        tensor_rank, after(grad_inner_low, rest_sum.away, inner_sum.away), F32
    )
    rest_sum.step(inner_sum.away, normed_here)
    while inner_sum.left or rest_sum.left:
        if inner_sum.left:
            inner_sum.step()
        if rest_sum.left:
            rest_sum.step(inner_sum.away, normed_other)
    inner_sum, rest_sum = inner_sum.value, rest_sum.value

    grad_normed = normed_here + normed_other.astype(F32)
    grad_normed = grad_normed + nt(
        rows_of(grad_state_low, tensor_rank), w_first[:, inner:channels]
    )
    gain = rows[ROW_NORM][None, :]
    inv_rms = lax.rsqrt(jnp.mean(hidden_wide * hidden_wide, axis=1, keepdims=True) + NORM_EPS)
    scaled_in = grad_normed * gain
    grad_hidden = (
        inv_rms * scaled_in
        - hidden_wide * inv_rms**3 * jnp.mean(scaled_in * hidden_wide, axis=1, keepdims=True)
        + cotangent.astype(F32)
    )

    grad_pgi, packed = pl.pallas_call(
        finish_kernel,
        in_specs=[vmem] * 6,
        out_specs=[vmem] * 2,
        out_shape=[shape_of((shard, 2, inner), F32), shape_of((shard, 2 * size + LANES), F32)],
        compiler_params=params(),
        cost_estimate=cost(1),
        name="finish",
    )(
        first_sum[:, inner:], inner_sum, rest_sum,
        projection_gate_inner.reshape(shard, 2 * inner), proj_state, proj_step,
    )
    (
        grad_state, grad_step, grad_gain, grad_conv, grad_bias, grad_taps, grad_taps_bias,
        grad_decay, grad_skip, grad_step_bias, grad_gate_gain,
    ) = pl.pallas_call(
        unpack_kernel,
        in_specs=[vmem] * 3,
        out_specs=[vmem] * 11,
        out_shape=[
            shape_of(dims, F32)
            for dims in (
                (shard, 2 * size), (shard, heads), (1, shard), (taps, shard), (1, shard),
                (taps, state_shard), (1, state_shard), (1, heads), (1, heads), (1, heads),
                (1, shard),
            )
        ],
        compiler_params=params(),
        cost_estimate=cost(1),
        name="unpack_small",
    )(packed, exchange(packed), norm_gain[None, :])
    return (
        block_out,
        grad_hidden,
        grad_gain[0],
        grad_pgi,
        grad_state,
        grad_step,
        grad_conv[:, None, :],
        grad_bias,
        grad_taps,
        grad_taps_bias[0],
        grad_decay[0],
        grad_skip[0],
        grad_step_bias[0],
        grad_gate_gain,
        first_sum[:, :inner].astype(F32).T,
    )


def solution(mesh):
    placed = (
        P(("dp", "tensor"), None),
        P("dp"),
        P("dp", None, "tensor"),
        P("dp", None),
        P("dp", "tensor"),
        P(None, "tensor", "dp"),
        P("tensor", "dp"),
        P(None, "dp"),
        P("dp"),
        P("tensor"),
        P("tensor"),
        P("tensor"),
        P("tensor", "dp"),
        P("tensor", "dp"),
        P("dp", None),
        P(("dp", "tensor"), None),
    )
    return jax.shard_map(
        on_device,
        mesh=mesh,
        in_specs=placed,
        out_specs=(
            P(("dp", "tensor"), None),
            P(("dp", "tensor"), None),
            P("dp"),
            P("dp", None, "tensor"),
            P("dp", None),
            P("dp", "tensor"),
            P(None, "tensor", "dp"),
            P("tensor", "dp"),
            P(None, "dp"),
            P("dp"),
            P("tensor"),
            P("tensor"),
            P("tensor"),
            P("tensor", "dp"),
            P("tensor", "dp"),
        ),
        check_vma=False,
    )
```

```python
import functools

import jax
import jax.numpy as jnp
from jax import lax
from jax.experimental import pallas as pl
from jax.experimental.pallas import tpu as pltpu
from jax.sharding import PartitionSpec as P

GROUP = 256
HALF = GROUP // 2
LANES = 128
PAIR_HEADS = 2
NORM_EPS = 1e-05
LOG2E = 1.4426950408889634
MASKED = -1e30
VMEM_BYTES = 56 * 1024 * 1024

LANE_CONV, LANE_GATE, LANE_STATE, LANE_HEADS, LANE_GAIN = 16, 21, 24, 32, 127
HALO = 16

STRIP = 32
STRIPS = [slice(at, at + STRIP) for at in range(0, GROUP, STRIP)]

F32 = jnp.float32
BF16 = jnp.bfloat16

ROW_NORM, ROW_TAP, ROW_BIAS, ROW_GATE, ROW_SKIP = 0, 1, 5, 6, 7


def nn(left, right):
    return lax.dot_general(left, right, (((1,), (0,)), ((), ())), preferred_element_type=F32)


def nt(left, right):
    return lax.dot_general(left, right, (((1,), (1,)), ((), ())), preferred_element_type=F32)


def tn(left, right):
    return lax.dot_general(left, right, (((0,), (0,)), ((), ())), preferred_element_type=F32)


def split3(value):
    high = value.astype(BF16)
    rest = value - high.astype(F32)
    mid = rest.astype(BF16)
    low = (rest - mid.astype(F32)).astype(BF16)
    return high, mid, low


def exact_left(ones, value):
    lanes = value.shape[1]
    found = nn(ones, jnp.concatenate(split3(value), axis=1))
    return found[:, :lanes] + found[:, lanes : 2 * lanes] + found[:, 2 * lanes :]


def three_in_lanes(value, heads):
    high, mid, low = split3(value)
    lane = lax.broadcasted_iota(jnp.int32, value.shape, 1)
    parts = jnp.where(
        lane < heads,
        high.astype(F32),
        jnp.where(lane < 2 * heads, mid.astype(F32), low.astype(F32)),
    )
    return parts.astype(BF16)


def spread_matrix(heads, head_size):
    shape = (LANES, heads * head_size)
    lane = lax.broadcasted_iota(jnp.int32, shape, 0)
    channel = lax.broadcasted_iota(jnp.int32, shape, 1)
    owner = channel // head_size
    hit = (lane == owner) | (lane == owner + heads) | (lane == owner + 2 * heads)
    return hit.astype(F32).astype(BF16)


def collect_matrix(heads, head_size):
    shape = (heads * head_size, LANES)
    lane = lax.broadcasted_iota(jnp.int32, shape, 1)
    owner = lax.broadcasted_iota(jnp.int32, shape, 0) // head_size
    hit = (lane == owner) | (lane == owner + heads) | (lane == owner + 2 * heads)
    return hit.astype(F32).astype(BF16)


def spaced_matrix(narrow, wide, narrow_shard, wide_shard, compress):
    shape = (wide, narrow) if compress else (narrow, wide)
    at_wide = lax.broadcasted_iota(jnp.int32, shape, 0 if compress else 1)
    at_narrow = lax.broadcasted_iota(jnp.int32, shape, 1 if compress else 0)
    owner, place = at_wide // wide_shard, at_wide % wide_shard
    hit = (place < narrow_shard) & (at_narrow == owner * narrow_shard + place)
    return hit.astype(F32).astype(BF16)


def pack_kernel(
    inner_ref, state_ref, step_ref, norm_ref, conv_ref, bias_ref, gate_ref, taps_ref,
    taps_bias_ref, out_ref, turned, lanes,
):
    shard, heads = step_ref.shape
    inner, states = inner_ref.shape[1], state_ref.shape[1]
    state_shard = taps_ref.shape[1]
    base = 3 * heads
    turned[...] = jnp.zeros_like(turned)
    turned[base : base + 1, 0:shard] = norm_ref[...].astype(F32)
    turned[base + 1 : base + 5, 0:shard] = conv_ref[...].astype(F32)
    turned[base + 5 : base + 6, 0:shard] = bias_ref[...].astype(F32)
    turned[base + 6 : base + 7, 0:shard] = gate_ref[...].astype(F32)
    turned[base + 8 : base + 12, 0:state_shard] = taps_ref[...].astype(F32)
    turned[base + 12 : base + 13, 0:state_shard] = taps_bias_ref[...].astype(F32)
    lanes[...] = jnp.zeros_like(lanes)
    step = step_ref[...].astype(F32)
    for copy in range(3):
        lanes[:, copy * heads : (copy + 1) * heads] = step
    out_ref[:, :inner] = inner_ref[...]
    out_ref[:, inner : inner + states] = state_ref[...]
    out_ref[:, inner + states :] = (turned[...].T[0:shard, :] + lanes[...]).astype(BF16)


def lower_matrix(upper=False):
    row = lax.broadcasted_iota(jnp.int32, (GROUP, GROUP), 0)
    col = lax.broadcasted_iota(jnp.int32, (GROUP, GROUP), 1)
    hit = (col >= row) if upper else (col <= row)
    return hit.astype(F32).astype(BF16)


def sequence_ends(len_ref):
    ends, total = [], jnp.int32(0)
    for slot in range(len_ref.shape[1]):
        total = total + len_ref[0, slot]
        ends.append(total)
    return ends


def sequence_of(ends, token):
    found = (token >= ends[0]).astype(jnp.int32)
    for end in ends[1:]:
        found = found + (token >= end).astype(jnp.int32)
    return found


def scalar_sequence_of(ends, token):
    found = jnp.where(token >= ends[0], 1, 0)
    for end in ends[1:]:
        found = found + jnp.where(token >= end, 1, 0)
    return found


def position_of(ends, token):
    start = jnp.zeros_like(token)
    for end in ends:
        start = jnp.where(token >= end, end, start)
    return token - start


def tokens_column(first, rows=GROUP):
    return first + lax.broadcasted_iota(jnp.int32, (rows, 1), 0)


def additive_mask(ends, first, transposed):
    rows = first + lax.broadcasted_iota(jnp.int32, (GROUP, GROUP), 0)
    cols = first + lax.broadcasted_iota(jnp.int32, (GROUP, GROUP), 1)
    ordered = (cols >= rows) if transposed else (rows >= cols)
    kept = (sequence_of(ends, rows) == sequence_of(ends, cols)) & ordered
    return jnp.where(kept, 0.0, MASKED)


def softplus(value):
    return jnp.maximum(value, 0.0) + jnp.log1p(jnp.exp(-jnp.abs(value)))


def sigmoid(value):
    return 0.5 * jnp.tanh(0.5 * value) + 0.5


def decay_terms(ends, first, step_in, rate, lower):
    group = first // GROUP
    step = softplus(step_in)
    cum = exact_left(lower, step * (rate * LOG2E))
    last = cum[GROUP - 1 : GROUP, :]
    sequence = sequence_of(ends, tokens_column(first))
    tail = scalar_sequence_of(ends, first + GROUP - 1)
    before = jnp.where(group > 0, scalar_sequence_of(ends, first - 1), -1)
    in_tail = (sequence == tail).astype(F32)
    entered = (sequence == before).astype(F32)
    carried = jnp.where(tail == before, 1.0, 0.0)
    key_factor = jnp.exp2(last - cum) * in_tail
    entry = jnp.exp2(cum) * entered
    decay = jnp.exp2(last) * carried
    return step, cum, key_factor, entry, decay


def strip_at(strip, base):
    return slice(base + strip.start, base + strip.stop)


def fold_rows(value):
    total = value[0:8]
    for at in range(8, STRIP, 8):
        total = total + value[at : at + 8]
    return total


def head_masks():
    lane = lax.broadcasted_iota(jnp.int32, (1, LANES), 1)
    first = (lane < LANES // 2).astype(F32)
    return first, 1.0 - first


def forward_kernel(
    rank_ref, len_ref, own_ref, other_ref, w_ref, head_ref,
    normed_ref, normed_t_ref, ipre_ref, spre_ref, sact_ref, stepin_ref, mixed_ref, sprev_ref,
    rows_ref, taps_ref,
    ext, state, spread, lower, fac, read, mask, scores, weighted, factors,
    values, stepped, both, *, shard, state_shard,
):
    inner = rows_ref.shape[1]
    channels = ext.shape[1]
    heads = inner // (LANES // PAIR_HEADS)
    size = sprev_ref.shape[0]
    group = pl.program_id(0)
    first = group * GROUP
    ends = sequence_ends(len_ref)

    @pl.when(group == 0)
    def _():
        ext[0:8, :] = jnp.zeros((8, channels), F32)
        state[...] = jnp.zeros_like(state)
        spread[...] = spread_matrix(heads, LANES // PAIR_HEADS)
        lower[...] = lower_matrix()
        factors[...] = jnp.zeros_like(factors)
        packed = w_ref[:, channels:].astype(F32).T
        base = 3 * heads
        rows_ref[0:7, :] = packed[base : base + 7, :]
        once = lax.broadcasted_iota(jnp.int32, (16, LANES), 1) < heads
        skip_row = jnp.where(once, head_ref[2:3, :], 0.0).astype(BF16)
        rows_ref[7:8, :] = nn(skip_row, spread[...])[0:1, :]
        taps_ref[...] = nn(
            packed[base + 8 : base + 16, :].astype(BF16),
            spaced_matrix(2 * size, w_ref.shape[0], state_shard, shard, True),
        )

    mine = rank_ref[0, 0] == group // (pl.num_programs(0) // 2)
    gain = rows_ref[ROW_NORM : ROW_NORM + 1, :]
    for part in range(4):
        sl = slice(part * 64, part * 64 + 64)
        hidden = jnp.where(mine, own_ref[sl, :].astype(F32), other_ref[sl, :].astype(F32))
        inv = lax.rsqrt(jnp.mean(hidden * hidden, axis=1, keepdims=True) + NORM_EPS)
        normed_ref[sl, :] = (hidden * inv * gain).astype(BF16)

    normed_t_ref[...] = normed_ref[...].T
    pre = nn(normed_ref[...], w_ref[:, :inner])
    ext[8 : 8 + GROUP, 0:inner] = pre
    ipre_ref[...] = pre
    rest = nn(normed_ref[...], w_ref[:, inner:])
    ext[8 : 8 + GROUP, inner:channels] = rest[:, : 2 * size]
    spre_ref[...] = rest[:, : 2 * size]
    lane = lax.broadcasted_iota(jnp.int32, (1, LANES), 1)
    step_in = jnp.where(lane < 3 * heads, rest[:, 2 * size :], 0.0) + head_ref[0:1, :]
    stepin_ref[...] = step_in

    token = tokens_column(first)
    position = position_of(ends, token)
    keep = [(position >= offset).astype(F32) for offset in (1, 2, 3)]

    def conv(strip, sl, taps, bias):
        at = strip.start
        total = bias + taps[3:4, :] * ext[8 + at : 8 + at + STRIP, sl]
        for offset in (1, 2, 3):
            total = total + keep[offset - 1][strip] * (
                taps[3 - offset : 4 - offset, :]
                * ext[8 - offset + at : 8 - offset + at + STRIP, sl]
            )
        return total

    for part in range(2):
        sl = slice(inner + part * size, inner + (part + 1) * size)
        own = slice(part * size, (part + 1) * size)
        for strip in STRIPS:
            total = conv(strip, sl, taps_ref[0:4, own], taps_ref[4:5, own])
            sact_ref[strip, own] = (total * sigmoid(total)).astype(BF16)
    keys = sact_ref[:, :size]
    queries = sact_ref[:, size:]
    scores[...] = nt(queries, keys)
    mask[...] = additive_mask(ends, first, False)

    step, cum, key_factor, entry, decay = decay_terms(
        ends, first, step_in, head_ref[1:2, :], lower[...]
    )
    cum_rows = cum.T
    stacked = jnp.concatenate(
        [step, key_factor * step, entry, jnp.broadcast_to(decay, (16, LANES))], axis=0
    )
    fac[...] = nn(three_in_lanes(stacked, heads), spread[...])
    held = state[...].astype(BF16)
    sprev_ref[...] = held
    read[...] = nn(queries, held)

    first_head = lax.broadcasted_iota(jnp.int32, (1, LANES), 1) < LANES // PAIR_HEADS
    lo, hi = slice(0, HALF), slice(HALF, GROUP)
    for pair in range(inner // LANES):
        sl = slice(pair * LANES, (pair + 1) * LANES)
        slot = pair % 2
        taps, bias = rows_ref[ROW_TAP : ROW_TAP + 4, sl], rows_ref[ROW_BIAS : ROW_BIAS + 1, sl]
        for strip in STRIPS:
            total = conv(strip, sl, taps, bias)
            value = (total * sigmoid(total)).astype(BF16).astype(F32)
            values[slot, strip] = value
            stepped[slot, strip] = (value * fac[strip, sl]).astype(BF16)
            weighted[strip, sl] = (value * fac[strip_at(strip, GROUP), sl]).astype(BF16)
        for which in range(PAIR_HEADS):
            head = pair * PAIR_HEADS + which
            for strip in STRIPS:
                column = jnp.broadcast_to(cum[strip, head : head + 1], (STRIP, LANES))
                place = strip_at(strip, which * GROUP)
                for cs in (lo, hi) if strip.start >= HALF else (lo,):
                    gap = column - cum_rows[head : head + 1, cs] + mask[strip, cs]
                    factors[slot, place, cs] = (jnp.exp2(gap) * scores[strip, cs]).astype(BF16)
        both[slot] = nn(factors[slot], stepped[slot])
        skip = rows_ref[ROW_SKIP : ROW_SKIP + 1, sl]
        for strip in STRIPS:
            within = jnp.where(
                first_head, both[slot, strip], both[slot, strip_at(strip, GROUP)]
            )
            mixed_ref[strip, sl] = (
                within
                + fac[strip_at(strip, 2 * GROUP), sl] * read[strip, sl]
                + skip * values[slot, strip]
            )

    state[...] = fac[3 * GROUP : 3 * GROUP + 1, :] * state[...] + tn(keys, weighted[...])
    ext[0:8, :] = ext[GROUP : GROUP + 8, :]


def gate_kernel(
    rank_ref, len_ref, own_ref, other_ref, normed_ref, mixed_ref, w_ref, proj_ref, rows_ref,
    gate_ref, gol_ref, live_t_ref, sums_ref,
):
    group = pl.program_id(0)
    first = group * GROUP
    ends = sequence_ends(len_ref)
    mine = rank_ref[0, 0] == group // (pl.num_programs(0) // 2)
    valid = tokens_column(first) < ends[-1]
    cotangent = jnp.where(mine, own_ref[...].astype(F32), other_ref[...].astype(F32))
    live = jnp.where(valid, cotangent, 0.0).astype(BF16)
    live_t_ref[...] = live.T
    square = jnp.zeros((GROUP, LANES), F32)
    inner = jnp.zeros((GROUP, LANES), F32)
    for part in range(gate_ref.shape[1] // GROUP):
        sl = slice(part * GROUP, (part + 1) * GROUP)
        gate = nn(normed_ref[...], w_ref[:, sl])
        gol = nn(live, proj_ref[:, sl])
        gate_ref[:, sl] = gate
        gol_ref[:, sl] = gol
        gated = mixed_ref[:, sl] * (gate * sigmoid(gate))
        squares = gated * gated
        inners = gol * rows_ref[ROW_GATE : ROW_GATE + 1, sl] * gated
        square = square + squares[:, :LANES] + squares[:, LANES:]
        inner = inner + inners[:, :LANES] + inners[:, LANES:]
    lane = lax.broadcasted_iota(jnp.int32, (GROUP, LANES), 1)
    columns = jnp.where(
        lane < 4,
        jnp.sum(square, axis=1, keepdims=True),
        jnp.sum(inner, axis=1, keepdims=True),
    )
    sums_ref[...] = columns.T[0:8, :]


def gate_grad_kernel(
    own_sums_ref, other_sums_ref, gate_ref, gol_ref, mixed_ref, rows_ref,
    low_ref, first_ref, ggp_ref, gain_ref, *, inner_all,
):
    @pl.when(pl.program_id(0) == 0)
    def _():
        gain_ref[...] = jnp.zeros_like(gain_ref)

    totals = own_sums_ref[...] + other_sums_ref[...]
    columns = jnp.concatenate([totals, jnp.zeros((LANES - 8, GROUP), F32)], axis=0).T
    inv_all = lax.rsqrt(columns[:, 0:1] / inner_all + NORM_EPS)
    slope_all = inv_all * inv_all * inv_all * columns[:, 4:5] / inner_all
    gain = rows_ref[ROW_GATE : ROW_GATE + 1, :]
    for part in range(gate_ref.shape[1] // GROUP):
        sl = slice(part * GROUP, (part + 1) * GROUP)
        gain_row = gain[:, sl]
        total = jnp.zeros((8, GROUP), F32)
        for at in range(0, GROUP, 16):
            strip = slice(at, at + 16)
            inv, slope = inv_all[strip], slope_all[strip]
            gate, gol, mixed = gate_ref[strip, sl], gol_ref[strip, sl], mixed_ref[strip, sl]
            logistic = sigmoid(gate)
            silu = gate * logistic
            gated = mixed * silu
            scaled = gated * inv
            low_ref[strip, sl] = (scaled * gain_row).astype(BF16)
            product = gol * scaled
            total = total + product[0:8] + product[8:16]
            grad = inv * (gol * gain_row) - gated * slope
            first_ref[strip, sl] = (grad * silu).astype(BF16)
            ggp_ref[strip, sl] = (
                grad * mixed * (logistic * (1.0 + gate * (1.0 - logistic)))
            ).astype(BF16)
        gain_ref[0:1, sl] += jnp.sum(total, axis=0, keepdims=True)


def product_kernel(left_ref, right_ref, out_ref):
    out_ref[...] = nn(left_ref[...], right_ref[...]).astype(out_ref.dtype)


def normed_grad_kernel(
    begin_ref, gate_ref, inner_ref, step_ref, w_gate_ref, w_inner_ref, w_step_ref, out_ref
):
    total = nt(gate_ref[...], w_gate_ref[...]) + nt(inner_ref[...], w_inner_ref[...])
    out_ref[...] = (total + nt(step_ref[...], w_step_ref[...])).astype(out_ref.dtype)


def backward_kernel(
    len_ref, ipre_ref, halo_ref, sact_ref, stepin_ref, mixed_ref, first_ref, sprev_ref,
    rows_ref, head_ref,
    gip_ref, gkq_ref, gstep_ref, conv_ref, heads_ref,
    ext, cext, gstate, spread, collect, lower, upper, fac, reads, mask, scores, gscores,
    weighted, entered, sums, factors, values, slopes, split, grads, both,
):
    inner = rows_ref.shape[1]
    heads = inner // (LANES // PAIR_HEADS)
    size = sprev_ref.shape[0]
    turn = pl.program_id(0)
    group = pl.num_programs(0) - 1 - turn
    first = group * GROUP
    ends = sequence_ends(len_ref)

    @pl.when(turn == 0)
    def _():
        cext[GROUP : GROUP + 8, :] = jnp.zeros((8, inner), F32)
        gstate[...] = jnp.zeros_like(gstate)
        spread[...] = spread_matrix(heads, LANES // PAIR_HEADS)
        collect[...] = collect_matrix(heads, LANES // PAIR_HEADS)
        lower[...] = lower_matrix()
        upper[...] = lower_matrix(upper=True)
        factors[...] = jnp.zeros_like(factors)
        conv_ref[...] = jnp.zeros_like(conv_ref)
        heads_ref[...] = jnp.zeros_like(heads_ref)

    ext[0:8, :] = jnp.where(group > 0, halo_ref[...], 0.0)
    ext[8 : 8 + GROUP, :] = ipre_ref[...]
    token = tokens_column(first)
    position = position_of(ends, token)
    keep = [(position >= offset).astype(F32) for offset in (1, 2, 3)]
    ahead = [(position_of(ends, token + offset) >= offset).astype(F32) for offset in (1, 2, 3)]

    step_in = stepin_ref[...]
    rate = head_ref[1:2, :]
    step, cum, key_factor, entry, decay = decay_terms(ends, first, step_in, rate, lower[...])
    cum_rows = cum.T
    key_step = key_factor * step
    stacked = jnp.concatenate(
        [step, key_step, entry, jnp.broadcast_to(decay, (16, LANES))], axis=0
    )
    fac[...] = nn(three_in_lanes(stacked, heads), spread[...])

    keys = sact_ref[:, :size]
    queries = sact_ref[:, size:]
    scores[...] = nt(keys, queries)
    mask[...] = additive_mask(ends, first, True)
    gscores[...] = jnp.zeros_like(gscores)
    held = gstate[...].astype(BF16)
    reads[...] = nn(keys, held)

    masks = head_masks()
    first_head = lax.broadcasted_iota(jnp.int32, (1, LANES), 1) < LANES // PAIR_HEADS
    lo, hi = slice(0, HALF), slice(HALF, GROUP)
    for pair in range(inner // LANES):
        sl = slice(pair * LANES, (pair + 1) * LANES)
        taps = rows_ref[ROW_TAP : ROW_TAP + 4, sl]
        bias = rows_ref[ROW_BIAS : ROW_BIAS + 1, sl]
        skip = rows_ref[ROW_SKIP : ROW_SKIP + 1, sl]
        slot = pair % 2

        def shifted(strip, offset):
            return ext[8 - offset + strip.start : 8 - offset + strip.stop, sl]

        for strip in STRIPS:
            total = bias + taps[3:4, :] * shifted(strip, 0)
            for offset in (1, 2, 3):
                total = total + keep[offset - 1][strip] * (
                    taps[3 - offset : 4 - offset, :] * shifted(strip, offset)
                )
            logistic = sigmoid(total)
            value = (total * logistic).astype(BF16).astype(F32)
            values[slot, strip] = value
            slopes[slot, strip] = logistic * (1.0 + total * (1.0 - logistic))
            step_value = value * fac[strip, sl]
            for which in range(PAIR_HEADS):
                split[slot, strip_at(strip, which * GROUP)] = (step_value * masks[which]).astype(
                    BF16
                )
            weighted[strip, sl] = (value * fac[strip_at(strip, GROUP), sl]).astype(BF16)
            entered[strip, sl] = (
                first_ref[strip, sl].astype(F32) * fac[strip_at(strip, 2 * GROUP), sl]
            ).astype(BF16)

        grads[slot] = nn(split[slot], first_ref[:, sl].T)
        for strip in STRIPS:
            columns = [
                jnp.broadcast_to(cum[strip, head : head + 1], (STRIP, LANES))
                for head in range(pair * PAIR_HEADS, (pair + 1) * PAIR_HEADS)
            ]
            for cs in (lo, hi) if strip.start < HALF else (hi,):
                total = gscores[strip, cs]
                for which in range(PAIR_HEADS):
                    head = pair * PAIR_HEADS + which
                    place = strip_at(strip, which * GROUP)
                    gap = cum_rows[head : head + 1, cs] - columns[which] + mask[strip, cs]
                    factor = jnp.exp2(gap)
                    factors[slot, place, cs] = (factor * scores[strip, cs]).astype(BF16)
                    total = total + factor * grads[slot, place, cs]
                gscores[strip, cs] = total

        both[slot] = nn(factors[slot], first_ref[:, sl])
        folds = [jnp.zeros((8, LANES), F32) for _ in range(6)]
        for strip in STRIPS:
            raw = jnp.where(first_head, both[slot, strip], both[slot, strip_at(strip, GROUP)])
            value = values[slot, strip]
            upstream = first_ref[strip, sl].astype(F32)
            across = reads[strip, sl]
            stepped = (value * fac[strip, sl]).astype(BF16).astype(F32)
            balance = upstream * (mixed_ref[strip, sl] - skip * value) - stepped * raw
            high = balance.astype(BF16)
            sums[strip, sl] = high
            sums[strip_at(strip, GROUP), sl] = (balance - high.astype(F32)).astype(BF16)
            sums[strip_at(strip, 2 * GROUP), sl] = (value * raw).astype(BF16)
            sums[strip_at(strip, 3 * GROUP), sl] = (value * across).astype(BF16)
            grad = (
                fac[strip, sl] * raw + fac[strip_at(strip, GROUP), sl] * across + skip * upstream
            ) * slopes[slot, strip]
            cext[strip, sl] = grad
            folds[5] = folds[5] + fold_rows(upstream * value)
            folds[4] = folds[4] + fold_rows(grad)
            folds[3] = folds[3] + fold_rows(grad * shifted(strip, 0))
            for offset in (1, 2, 3):
                folds[3 - offset] = folds[3 - offset] + fold_rows(
                    keep[offset - 1][strip] * grad * shifted(strip, offset)
                )
        for row in range(6):
            conv_ref[row : row + 1, sl] += jnp.sum(folds[row], axis=0, keepdims=True)
        for strip in STRIPS:
            result = taps[3:4, :] * cext[strip, sl]
            for offset in (1, 2, 3):
                result = result + ahead[offset - 1][strip] * (
                    taps[3 - offset : 4 - offset, :] * cext[strip_at(strip, offset), sl]
                )
            gip_ref[strip, sl] = result.astype(BF16)

    cext[GROUP : GROUP + 8, :] = cext[0:8, :]
    state = sprev_ref[...]
    grad_scores = gscores[...].astype(BF16)
    gkq_ref[:, :size] = (nn(grad_scores, queries) + nt(weighted[...], held)).astype(BF16)
    gkq_ref[:, size:] = (tn(grad_scores, keys) + nt(entered[...], state)).astype(BF16)

    collected = nn(sums[...], collect[...])
    balance = collected[:GROUP] + collected[GROUP : 2 * GROUP]
    direct = collected[2 * GROUP : 3 * GROUP]
    key_dot = collected[3 * GROUP :]

    def row_collect(value):
        high = value.astype(BF16)
        low = (value - high.astype(F32)).astype(BF16)
        rows16 = jnp.concatenate(
            [jnp.broadcast_to(high, (8, inner)), jnp.broadcast_to(low, (8, inner))], axis=0
        )
        found = nn(rows16, collect[...])
        return found[0:1, :] + found[8:9, :]

    carry_term = decay * row_collect(
        jnp.sum(gstate[...] * state.astype(F32), axis=0, keepdims=True)
    )
    moved = key_step * key_dot
    grad_log = (
        exact_left(upper[...], balance) + carry_term + exact_left(lower[...], moved) - moved
    )
    grad_step = direct + key_factor * key_dot + grad_log * rate
    lane = lax.broadcasted_iota(jnp.int32, (1, LANES), 1)
    grad_step_in = jnp.where(lane < heads, grad_step * sigmoid(step_in), 0.0)
    gstep_ref[...] = grad_step_in.astype(BF16)
    heads_ref[0:1, :] += jnp.sum(grad_log * step * rate, axis=0, keepdims=True)
    heads_ref[1:2, :] += jnp.sum(grad_step_in, axis=0, keepdims=True)
    gstate[...] = fac[3 * GROUP : 3 * GROUP + 1, :] * gstate[...] + tn(queries, entered[...])

    @pl.when(turn == pl.num_programs(0) - 1)
    def _():
        heads_ref[2:3, :] = row_collect(conv_ref[5:6, :])


def state_grad_kernel(
    rank_ref, len_ref, own_ref, other_ref, spre_ref, taps_ref, normed_t_ref, gstep_ref,
    inner_rows_ref, gain_ref, heads_ref,
    gsp_ref, rest_ref, conv_ref, ext, cext, turned, *, shard, state_shard, heads,
):
    rows, channels = own_ref.shape
    width = rest_ref.shape[0]
    half = rows - HALO
    rank = rank_ref[0, 0]
    base = pl.multiple_of(rank * (half - HALO), HALO)
    chunk = window_chunk(rows)
    ends = sequence_ends(len_ref)
    before = spre_ref[pl.ds(pl.multiple_of(jnp.maximum(base - 8, 0), 8), 8), :]
    ext[0:8, :] = jnp.where(rank > 0, before, 0.0)
    ext[8 : 8 + rows, :] = spre_ref[pl.ds(base, rows), :]
    cext[rows : rows + 8, :] = jnp.zeros((8, channels), F32)
    conv_ref[...] = jnp.zeros_like(conv_ref)
    gsp_ref[...] = jnp.zeros_like(gsp_ref)
    for at in range(0, rows, chunk):
        token = tokens_column(base + at, chunk)
        position = position_of(ends, token)
        owned = ((token >= rank * half) & (token < (rank + 1) * half)).astype(F32)
        keep = [(position >= offset).astype(F32) for offset in (1, 2, 3)]
        for part in range(channels // LANES):
            sl = slice(part * LANES, (part + 1) * LANES)
            shifted = [ext[at + 8 - offset : at + 8 - offset + chunk, sl] for offset in range(4)]
            total = taps_ref[4:5, sl] + taps_ref[3:4, sl] * shifted[0]
            for offset in (1, 2, 3):
                total = total + keep[offset - 1] * (
                    taps_ref[3 - offset : 4 - offset, sl] * shifted[offset]
                )
            logistic = sigmoid(total)
            slope = logistic * (1.0 + total * (1.0 - logistic))
            upstream = own_ref[at : at + chunk, sl].astype(F32) + other_ref[
                at : at + chunk, sl
            ].astype(F32)
            grad = upstream * slope
            cext[at : at + chunk, sl] = grad
            grad = grad * owned
            conv_ref[4:5, sl] += jnp.sum(grad, axis=0, keepdims=True)
            conv_ref[3:4, sl] += jnp.sum(grad * shifted[0], axis=0, keepdims=True)
            for offset in (1, 2, 3):
                conv_ref[3 - offset : 4 - offset, sl] += jnp.sum(
                    keep[offset - 1] * grad * shifted[offset], axis=0, keepdims=True
                )
    for at in range(0, rows, chunk):
        token = tokens_column(base + at, chunk)
        owned = ((token >= rank * half) & (token < (rank + 1) * half)).astype(F32)
        ahead = [
            (position_of(ends, token + offset) >= offset).astype(F32) for offset in (1, 2, 3)
        ]
        for part in range(channels // LANES):
            sl = slice(part * LANES, (part + 1) * LANES)
            result = taps_ref[3:4, sl] * cext[at : at + chunk, sl]
            for offset in (1, 2, 3):
                result = result + ahead[offset - 1] * (
                    taps_ref[3 - offset : 4 - offset, sl]
                    * cext[at + offset : at + offset + chunk, sl]
                )
            place = pl.ds(pl.multiple_of(base + at, HALO), chunk)
            gsp_ref[place, sl] = (result * owned).astype(BF16)
    rest_ref[:, :channels] = nn(normed_t_ref[...], gsp_ref[...]).astype(BF16)
    step_part = nn(normed_t_ref[...], gstep_ref[...])
    turned[...] = jnp.zeros_like(turned)
    turned[LANE_CONV : LANE_CONV + 5, :] = inner_rows_ref[0:5, :]
    turned[LANE_GATE : LANE_GATE + 1, :] = gain_ref[0:1, :]
    turned[LANE_STATE : LANE_STATE + 8, :] = nn(
        conv_ref[...].astype(BF16), spaced_matrix(channels, width, state_shard, shard, False)
    )
    columns = jnp.concatenate([heads_ref[...], jnp.zeros((LANES - 8, LANES), F32)], axis=0).T
    for which in range(3):
        start = LANE_HEADS + which * heads
        turned[start : start + heads, :] = jnp.broadcast_to(
            columns[0:heads, which : which + 1], (heads, width)
        )
    rest_ref[:, channels:] = (step_part + turned[...].T).astype(BF16)


def window_chunk(rows):
    return max(n for n in range(HALO, GROUP + 1, HALO) if rows % n == 0)


def finish_kernel(
    first_ref, inner_ref, rest_ref, weight_ref, state_ref, step_ref, pgi_ref, packed_ref
):
    width = first_ref.shape[1]
    states = state_ref.shape[1]
    heads = step_ref.shape[1]
    shard = step_ref.shape[0]
    gate = first_ref[...].astype(F32)
    inner = inner_ref[...]
    rest = rest_ref[...]
    pgi_ref[:, 0:1, :] = gate[:, None, :]
    pgi_ref[:, 1:2, :] = inner[:, None, :]
    weight = weight_ref[...].astype(F32)
    product = jnp.sum(gate * weight[:, :width] + inner * weight[:, width:], axis=1, keepdims=True)
    product += jnp.sum(rest[:, :states] * state_ref[...].astype(F32), axis=1, keepdims=True)
    small = rest[:, states:]
    product += jnp.sum(small[:, :heads] * step_ref[...].astype(F32), axis=1, keepdims=True)
    lane = lax.broadcasted_iota(jnp.int32, (shard, LANES), 1)
    packed_ref[:, :states] = rest[:, :states]
    packed_ref[:, states:] = jnp.where(lane == LANE_GAIN, product, small)


def unpack_kernel(
    own_ref, other_ref, norm_ref,
    state_ref, step_ref, gain_ref, conv_ref, bias_ref, taps_ref, taps_bias_ref,
    decay_ref, skip_ref, step_bias_ref, gate_ref,
):
    shard, states = state_ref.shape
    heads = step_ref.shape[1]
    state_shard = taps_ref.shape[1]
    state_ref[...] = own_ref[:, :states] + other_ref[:, :states]
    small = own_ref[:, states:]
    both = small + other_ref[:, states:]
    step_ref[...] = small[:, :heads]

    def turn(value):
        if shard < LANES:
            value = jnp.concatenate([value, jnp.zeros((LANES - shard, LANES), F32)], axis=0)
        return value.T

    small_rows, both_rows = turn(small), turn(both)
    gain_ref[...] = both_rows[LANE_GAIN : LANE_GAIN + 1, :shard] / norm_ref[...].astype(F32)
    conv_ref[...] = small_rows[LANE_CONV : LANE_CONV + 4, :shard]
    bias_ref[...] = small_rows[LANE_CONV + 4 : LANE_CONV + 5, :shard]
    gate_ref[...] = small_rows[LANE_GATE : LANE_GATE + 1, :shard]
    taps_ref[...] = both_rows[LANE_STATE : LANE_STATE + 4, :state_shard]
    taps_bias_ref[...] = both_rows[LANE_STATE + 4 : LANE_STATE + 5, :state_shard]
    first = small[0:8, :]
    for which, out_ref in enumerate((decay_ref, step_bias_ref, skip_ref)):
        start = LANE_HEADS + which * heads
        out_ref[...] = pltpu.roll(first, LANES - start, 1)[0:1, :heads]


def shape_of(dims, dtype):
    return jax.ShapeDtypeStruct(dims, dtype)


def params(**kwargs):
    return pltpu.CompilerParams(vmem_limit_bytes=VMEM_BYTES, **kwargs)


def cost(micros):
    return pl.CostEstimate(flops=int(micros * 1.1e9), bytes_accessed=0, transcendentals=0)


SMEM_SPEC = pl.BlockSpec(memory_space=pltpu.SMEM)


def whole(*dims):
    return pl.BlockSpec(dims, lambda i: (0,) * len(dims))


def bit_order(count, spread_first):
    bits = list(range(count.bit_length() - 1))
    return [0] + bits[2:] + [1] if spread_first and len(bits) > 1 else bits


def flip(value, bit, count):
    return lax.ppermute(value, "dp", [(i, i ^ (1 << bit)) for i in range(count)])


def after(value, *others):
    return lax.optimization_barrier((value, *others))[0]


def gather_by_bits(value, rank, count, spread_first, waits):
    held, begun = [], []
    rows, lanes = value.shape
    for bit in reversed(bit_order(count, spread_first)):
        if 0 < len(begun) <= len(waits):
            value = after(value, waits[len(begun) - 1])
        begun.append(value)
        other = flip(value, bit, count)
        held = sorted(held + [bit], reverse=True)
        low = (rank >> bit) & 1 == 0
        value = jnp.stack(
            [jnp.where(low, value, other), jnp.where(low, other, value)], axis=held.index(bit)
        )
    return value.reshape(count * rows, lanes), begun


class HalvingSum:
    def __init__(self, value, rank, count, spread_first):
        self.rank, self.count = rank, count
        self.left = list(reversed(range(count.bit_length() - 1)))
        self.order = bit_order(count, spread_first)
        rows = value.shape[0] // count
        self.value = value.reshape([2] * len(self.left) + [rows, value.shape[1]])

    def start(self):
        bit = self.order.pop(0)
        axis = self.left.index(bit)
        mine = (self.rank >> bit) & 1
        self.away = lax.dynamic_index_in_dim(self.value, 1 - mine, axis, keepdims=False)
        self.here = lax.dynamic_index_in_dim(self.value, mine, axis, keepdims=False)
        self.came = flip(self.away, bit, self.count)
        self.bit = bit

    def step(self, *others):
        if not self.left:
            return
        came = after(self.came, *others) if others else self.came
        self.left.remove(self.bit)
        self.value = self.here.astype(F32) + came.astype(F32)
        if self.left:
            self.value = self.value.astype(BF16)
            self.start()


def on_device(
    hidden_in,
    norm_gain,
    projection_gate_inner,
    proj_state,
    proj_step,
    conv_inner,
    conv_inner_bias,
    conv_state,
    conv_state_bias,
    decay_log,
    skip_gain,
    step_bias,
    gate_gain,
    proj_out,
    lengths,
    cotangent,
):
    tensor_count = lax.axis_size("tensor")
    tensor_rank = lax.axis_index("tensor")
    shard_rank = lax.axis_index("dp")
    shard_count = lax.axis_size("dp")
    half_rows, width = hidden_in.shape
    tokens = half_rows * tensor_count
    groups = tokens // GROUP
    half_groups = groups // 2
    inner = proj_out.shape[0]
    inner_all = inner * tensor_count
    heads = decay_log.shape[0]
    head_size = inner // heads
    size = proj_state.shape[1] // 2
    taps = conv_inner.shape[0]
    shard = width // shard_count
    channels = inner + 2 * size
    swap = [(0, 1), (1, 0)]

    def exchange(value):
        return lax.ppermute(value, "tensor", swap)

    pieces = []
    cuts = [0, half_rows // 6, half_rows * 7 // 12, half_rows]
    for begin, end in zip(cuts, cuts[1:]):
        piece = hidden_in[begin:end]
        pieces.append(exchange(after(piece, pieces[-1]) if pieces else piece))
    hidden_other = jnp.concatenate(pieces, axis=0)
    cotangent_other = exchange(after(cotangent, pieces[-1]))

    state_shard = conv_state.shape[1]
    first_shard = pl.pallas_call(
        pack_kernel,
        in_specs=[pl.BlockSpec(memory_space=pltpu.VMEM)] * 9,
        out_specs=pl.BlockSpec(memory_space=pltpu.VMEM),
        out_shape=shape_of((shard, channels + LANES), BF16),
        scratch_shapes=[
            pltpu.VMEM((LANES, max(LANES, shard)), F32),
            pltpu.VMEM((shard, LANES), F32),
        ],
        compiler_params=params(),
        cost_estimate=cost(0),
        name="pack_small",
    )(
        projection_gate_inner[:, 1], proj_state, proj_step, norm_gain[None, :], conv_inner.reshape(taps, shard),
        conv_inner_bias, gate_gain, conv_state, conv_state_bias[None, :],
    )
    w_first, begun = gather_by_bits(first_shard, shard_rank, shard_count, False, pieces)
    second_shard = jnp.concatenate([projection_gate_inner[:, 0], proj_out.T], axis=1)
    second_shard = after(second_shard, begun[min(2, len(begun) - 1)])
    w_second = lax.all_gather(second_shard, "dp", axis=0, tiled=True)
    w_out = w_second[:, inner:]

    rate = -jnp.exp(decay_log.astype(F32))
    head_rows = jnp.stack([step_bias.astype(F32), rate, skip_gain.astype(F32)])
    head_rows = jnp.pad(jnp.tile(head_rows, (1, 3)), ((0, 5), (0, LANES - 3 * heads)))
    rank = tensor_rank.astype(jnp.int32).reshape(1, 1)

    def by_group(lanes):
        return pl.BlockSpec((GROUP, lanes), lambda i: (i, 0))

    half_block = pl.BlockSpec((GROUP, width), lambda i: (i % half_groups, 0))
    (
        normed, normed_t, inner_pre, state_pre, state_act, step_in, mixed, prev_states, rows,
        state_rows,
    ) = pl.pallas_call(
        functools.partial(forward_kernel, shard=shard, state_shard=state_shard),
        grid=(groups,),
        in_specs=[
            SMEM_SPEC, SMEM_SPEC, half_block, half_block,
            whole(width, channels + LANES), whole(8, LANES),
        ],
        out_specs=[
            by_group(width), pl.BlockSpec((width, GROUP), lambda i: (0, i)), by_group(inner), by_group(2 * size), by_group(2 * size),
            by_group(LANES), by_group(inner), pl.BlockSpec((size, inner), lambda i: (i, 0)),
            whole(8, inner), whole(8, 2 * size),
        ],
        out_shape=[
            shape_of((tokens, width), BF16),
            shape_of((width, tokens), BF16),
            shape_of((tokens, inner), F32),
            shape_of((tokens, 2 * size), F32),
            shape_of((tokens, 2 * size), BF16),
            shape_of((tokens, LANES), F32),
            shape_of((tokens, inner), F32),
            shape_of((groups * size, inner), BF16),
            shape_of((8, inner), F32),
            shape_of((8, 2 * size), F32),
        ],
        scratch_shapes=[
            pltpu.VMEM((GROUP + 8, channels), F32),
            pltpu.VMEM((size, inner), F32),
            pltpu.VMEM((LANES, inner), BF16),
            pltpu.VMEM((GROUP, GROUP), BF16),
            pltpu.VMEM((3 * GROUP + 16, inner), F32),
            pltpu.VMEM((GROUP, inner), F32),
            pltpu.VMEM((GROUP, GROUP), F32),
            pltpu.VMEM((GROUP, GROUP), F32),
            pltpu.VMEM((GROUP, inner), BF16),
            pltpu.VMEM((2, PAIR_HEADS * GROUP, GROUP), BF16),
            pltpu.VMEM((2, GROUP, LANES), F32),
            pltpu.VMEM((2, GROUP, LANES), BF16),
            pltpu.VMEM((2, PAIR_HEADS * GROUP, LANES), F32),
        ],
        compiler_params=params(),
        cost_estimate=cost(2),
        name="mixer_forward",
    )(rank, lengths, hidden_in, hidden_other, w_first, head_rows)

    gate_pre, grad_out_low, live_t, sums = pl.pallas_call(
        gate_kernel,
        grid=(groups,),
        in_specs=[
            SMEM_SPEC, SMEM_SPEC, half_block, half_block, by_group(width), by_group(inner),
            pl.BlockSpec((width, inner), lambda i: (0, 0)),
            pl.BlockSpec((width, inner), lambda i: (0, 1)),
            whole(8, inner),
        ],
        out_specs=[
            by_group(inner), by_group(inner), pl.BlockSpec((width, GROUP), lambda i: (0, i)),
            pl.BlockSpec((8, GROUP), lambda i: (0, i)),
        ],
        out_shape=[
            shape_of((tokens, inner), F32),
            shape_of((tokens, inner), F32),
            shape_of((width, tokens), BF16),
            shape_of((8, tokens), F32),
        ],
        compiler_params=params(),
        cost_estimate=cost(16),
        name="gate_forward",
    )(rank, lengths, cotangent, cotangent_other, normed, mixed, w_second, w_second, rows)

    sums_other = exchange(sums)
    sum_block = pl.BlockSpec((8, GROUP), lambda i: (0, i))
    out_low, grad_first, grad_gate_low, gain_rows = pl.pallas_call(
        functools.partial(gate_grad_kernel, inner_all=inner_all),
        grid=(groups,),
        in_specs=[
            sum_block, sum_block, by_group(inner), by_group(inner), by_group(inner),
            whole(8, inner),
        ],
        out_specs=[by_group(inner), by_group(inner), by_group(inner), whole(8, inner)],
        out_shape=[
            shape_of((tokens, inner), BF16),
            shape_of((tokens, inner), BF16),
            shape_of((tokens, inner), BF16),
            shape_of((8, inner), F32),
        ],
        compiler_params=params(),
        cost_estimate=cost(13),
        name="gate_backward",
    )(sums, sums_other, gate_pre, grad_out_low, mixed, rows)

    first_grads = jnp.concatenate(
        [nn(live_t, out_low).astype(BF16), nn(normed_t, grad_gate_low).astype(BF16)], axis=1
    )
    def rows_of(value, which):
        return lax.dynamic_slice_in_dim(value, which * half_rows, half_rows)

    first_sum = lax.psum_scatter(first_grads, "dp", scatter_dimension=0, tiled=True)
    out_low = after(out_low, first_grads)
    mix_away = nt(rows_of(out_low, 1 - tensor_rank), w_out).astype(BF16)
    grad_first = after(grad_first, mix_away)
    mix_other = exchange(mix_away)
    mix_here = nt(rows_of(out_low, tensor_rank), w_out)
    last = groups - 1
    grad_inner_low, grad_kq, grad_step_low, conv_rows, head_sums = pl.pallas_call(
        backward_kernel,
        grid=(groups,),
        in_specs=[
            SMEM_SPEC,
            pl.BlockSpec((GROUP, inner), lambda i: (last - i, 0)),
            pl.BlockSpec(
                (8, inner), lambda i: (jnp.maximum((last - i) * (GROUP // 8) - 1, 0), 0)
            ),
            pl.BlockSpec((GROUP, 2 * size), lambda i: (last - i, 0)),
            pl.BlockSpec((GROUP, LANES), lambda i: (last - i, 0)),
            pl.BlockSpec((GROUP, inner), lambda i: (last - i, 0)),
            pl.BlockSpec((GROUP, inner), lambda i: (last - i, 0)),
            pl.BlockSpec((size, inner), lambda i: (last - i, 0)),
            whole(8, inner), whole(8, LANES),
        ],
        out_specs=[
            pl.BlockSpec((GROUP, inner), lambda i: (last - i, 0)),
            pl.BlockSpec((GROUP, 2 * size), lambda i: (last - i, 0)),
            pl.BlockSpec((GROUP, LANES), lambda i: (last - i, 0)),
            whole(8, inner), whole(8, LANES),
        ],
        out_shape=[
            shape_of((tokens, inner), BF16),
            shape_of((tokens, 2 * size), BF16),
            shape_of((tokens, LANES), BF16),
            shape_of((8, inner), F32),
            shape_of((8, LANES), F32),
        ],
        scratch_shapes=[
            pltpu.VMEM((GROUP + 8, inner), F32),
            pltpu.VMEM((GROUP + 8, inner), F32),
            pltpu.VMEM((size, inner), F32),
            pltpu.VMEM((LANES, inner), BF16),
            pltpu.VMEM((inner, LANES), BF16),
            pltpu.VMEM((GROUP, GROUP), BF16),
            pltpu.VMEM((GROUP, GROUP), BF16),
            pltpu.VMEM((3 * GROUP + 16, inner), F32),
            pltpu.VMEM((GROUP, inner), F32),
            pltpu.VMEM((GROUP, GROUP), F32),
            pltpu.VMEM((GROUP, GROUP), F32),
            pltpu.VMEM((GROUP, GROUP), F32),
            pltpu.VMEM((GROUP, inner), BF16),
            pltpu.VMEM((GROUP, inner), BF16),
            pltpu.VMEM((4 * GROUP, inner), BF16),
            pltpu.VMEM((2, PAIR_HEADS * GROUP, GROUP), BF16),
            pltpu.VMEM((2, GROUP, LANES), F32),
            pltpu.VMEM((2, GROUP, LANES), F32),
            pltpu.VMEM((2, PAIR_HEADS * GROUP, LANES), BF16),
            pltpu.VMEM((2, PAIR_HEADS * GROUP, GROUP), F32),
            pltpu.VMEM((2, PAIR_HEADS * GROUP, LANES), F32),
        ],
        compiler_params=params(),
        cost_estimate=cost(2),
        name="mixer_backward",
    )(
        lengths, inner_pre, inner_pre, state_act, step_in, mixed, grad_first, prev_states,
        rows, head_rows,
    )

    window = half_rows + HALO
    kq_own = lax.dynamic_slice_in_dim(grad_kq, tensor_rank * (half_rows - HALO), window)
    kq_away = lax.dynamic_slice_in_dim(grad_kq, (1 - tensor_rank) * (half_rows - HALO), window)
    kq_other = exchange(kq_away)

    grad_inner_low = after(grad_inner_low, mix_other)
    inner_grads = pl.pallas_call(
        product_kernel,
        grid=(inner // GROUP,),
        in_specs=[whole(width, tokens), pl.BlockSpec((tokens, GROUP), lambda i: (0, i))],
        out_specs=pl.BlockSpec((width, GROUP), lambda i: (0, i)),
        out_shape=shape_of((width, inner), BF16),
        compiler_params=params(),
        cost_estimate=cost(0),
        name="inner_weight_grads",
    )(normed_t, grad_inner_low)
    inner_sum = HalvingSum(inner_grads, shard_rank, shard_count, False)
    inner_sum.start()

    def normed_part(which, gip, dtype):
        def block(i, begin):
            return (begin[0] + i, 0)

        return pl.pallas_call(
            normed_grad_kernel,
            grid_spec=pltpu.PrefetchScalarGridSpec(
                num_scalar_prefetch=1,
                grid=(half_groups,),
                in_specs=[
                    pl.BlockSpec((GROUP, inner), block),
                    pl.BlockSpec((GROUP, inner), block),
                    pl.BlockSpec((GROUP, LANES), block),
                    pl.BlockSpec((width, inner), lambda i, begin: (0, 0)),
                    pl.BlockSpec((width, inner), lambda i, begin: (0, 0)),
                    pl.BlockSpec((width, LANES), lambda i, begin: (0, channels // LANES)),
                ],
                out_specs=pl.BlockSpec((GROUP, width), lambda i, begin: (i, 0)),
            ),
            out_shape=shape_of((half_rows, width), dtype),
            compiler_params=params(),
            cost_estimate=cost(0),
            name="normed_grads",
        )(
            (which * half_groups).astype(jnp.int32).reshape(1),
            grad_gate_low, gip, grad_step_low, w_second, w_first, w_first,
        )

    grad_inner_low, first_sum, _ = lax.optimization_barrier(
        (grad_inner_low, first_sum, inner_sum.away)
    )
    normed_away = normed_part(1 - tensor_rank, grad_inner_low, BF16)
    normed_other = exchange(normed_away)
    inner_sum.step()
    vmem = pl.BlockSpec(memory_space=pltpu.VMEM)
    kq_other = after(kq_other, normed_away, inner_sum.away)
    grad_state_low, rest_grads = pl.pallas_call(
        functools.partial(
            state_grad_kernel, shard=shard, state_shard=state_shard, heads=heads
        ),
        in_specs=[SMEM_SPEC, SMEM_SPEC] + [vmem] * 9,
        out_specs=[vmem] * 2,
        out_shape=[shape_of((tokens, 2 * size), BF16), shape_of((width, 2 * size + LANES), BF16)],
        scratch_shapes=[
            pltpu.VMEM((8, 2 * size), F32),
            pltpu.VMEM((window + 8, 2 * size), F32),
            pltpu.VMEM((window + 8, 2 * size), F32),
            pltpu.VMEM((LANES, width), F32),
        ],
        compiler_params=params(),
        cost_estimate=cost(0),
        name="state_backward",
    )(
        rank, lengths, kq_own, kq_other, state_pre, state_rows, normed_t, grad_step_low,
        conv_rows, gain_rows, head_sums,
    )
    rest_sum = HalvingSum(rest_grads, shard_rank, shard_count, True)
    rest_sum.start()
    inner_sum.step(rest_sum.away)
    normed_here = normed_part(
        tensor_rank, after(grad_inner_low, rest_sum.away, inner_sum.away), F32
    )
    rest_sum.step(inner_sum.away, normed_here)
    while inner_sum.left or rest_sum.left:
        if inner_sum.left:
            inner_sum.step()
        if rest_sum.left:
            rest_sum.step(inner_sum.away, normed_other)
    inner_sum, rest_sum = inner_sum.value, rest_sum.value

    mix = mix_here + after(mix_other, normed_here).astype(F32)
    slot = tensor_rank * half_rows + jnp.arange(half_rows, dtype=jnp.int32)
    valid_half = slot < jnp.sum(lengths[0])
    hidden_wide = hidden_in.astype(F32)
    block_out = (hidden_wide + jnp.where(valid_half[:, None], mix, 0.0)).astype(BF16)


    grad_normed = normed_here + normed_other.astype(F32)
    grad_normed = grad_normed + nt(
        rows_of(grad_state_low, tensor_rank), w_first[:, inner:channels]
    )
    gain = rows[ROW_NORM][None, :]
    inv_rms = lax.rsqrt(jnp.mean(hidden_wide * hidden_wide, axis=1, keepdims=True) + NORM_EPS)
    scaled_in = grad_normed * gain
    grad_hidden = (
        inv_rms * scaled_in
        - hidden_wide * inv_rms**3 * jnp.mean(scaled_in * hidden_wide, axis=1, keepdims=True)
        + cotangent.astype(F32)
    )

    grad_pgi, packed = pl.pallas_call(
        finish_kernel,
        in_specs=[vmem] * 6,
        out_specs=[vmem] * 2,
        out_shape=[shape_of((shard, 2, inner), F32), shape_of((shard, 2 * size + LANES), F32)],
        compiler_params=params(),
        cost_estimate=cost(1),
        name="finish",
    )(
        first_sum[:, inner:], inner_sum, rest_sum,
        projection_gate_inner.reshape(shard, 2 * inner), proj_state, proj_step,
    )
    (
        grad_state, grad_step, grad_gain, grad_conv, grad_bias, grad_taps, grad_taps_bias,
        grad_decay, grad_skip, grad_step_bias, grad_gate_gain,
    ) = pl.pallas_call(
        unpack_kernel,
        in_specs=[vmem] * 3,
        out_specs=[vmem] * 11,
        out_shape=[
            shape_of(dims, F32)
            for dims in (
                (shard, 2 * size), (shard, heads), (1, shard), (taps, shard), (1, shard),
                (taps, state_shard), (1, state_shard), (1, heads), (1, heads), (1, heads),
                (1, shard),
            )
        ],
        compiler_params=params(),
        cost_estimate=cost(1),
        name="unpack_small",
    )(packed, exchange(packed), norm_gain[None, :])
    return (
        block_out,
        grad_hidden,
        grad_gain[0],
        grad_pgi,
        grad_state,
        grad_step,
        grad_conv[:, None, :],
        grad_bias,
        grad_taps,
        grad_taps_bias[0],
        grad_decay[0],
        grad_skip[0],
        grad_step_bias[0],
        grad_gate_gain,
        first_sum[:, :inner].astype(F32).T,
    )


def solution(mesh):
    placed = (
        P(("dp", "tensor"), None),
        P("dp"),
        P("dp", None, "tensor"),
        P("dp", None),
        P("dp", "tensor"),
        P(None, "tensor", "dp"),
        P("tensor", "dp"),
        P(None, "dp"),
        P("dp"),
        P("tensor"),
        P("tensor"),
        P("tensor"),
        P("tensor", "dp"),
        P("tensor", "dp"),
        P("dp", None),
        P(("dp", "tensor"), None),
    )
    return jax.shard_map(
        on_device,
        mesh=mesh,
        in_specs=placed,
        out_specs=(
            P(("dp", "tensor"), None),
            P(("dp", "tensor"), None),
            P("dp"),
            P("dp", None, "tensor"),
            P("dp", None),
            P("dp", "tensor"),
            P(None, "tensor", "dp"),
            P("tensor", "dp"),
            P(None, "dp"),
            P("dp"),
            P("tensor"),
            P("tensor"),
            P("tensor"),
            P("tensor", "dp"),
            P("tensor", "dp"),
        ),
        check_vma=False,
    )
```

```python
import functools

import jax
import jax.numpy as jnp
from jax import lax
from jax.experimental import pallas as pl
from jax.experimental.pallas import tpu as pltpu
from jax.sharding import PartitionSpec as P

GROUP = 256
HALF = GROUP // 2
LANES = 128
PAIR_HEADS = 2
NORM_EPS = 1e-05
LOG2E = 1.4426950408889634
MASKED = -1e30
VMEM_BYTES = 56 * 1024 * 1024

LANE_CONV, LANE_GATE, LANE_STATE, LANE_HEADS, LANE_GAIN = 16, 21, 24, 32, 127
HALO = 16

F32 = jnp.float32
BF16 = jnp.bfloat16

ROW_NORM, ROW_TAP, ROW_BIAS, ROW_GATE, ROW_SKIP = 0, 1, 5, 6, 7


def nn(left, right):
    return lax.dot_general(left, right, (((1,), (0,)), ((), ())), preferred_element_type=F32)


def nt(left, right):
    return lax.dot_general(left, right, (((1,), (1,)), ((), ())), preferred_element_type=F32)


def tn(left, right):
    return lax.dot_general(left, right, (((0,), (0,)), ((), ())), preferred_element_type=F32)


def split3(value):
    high = value.astype(BF16)
    rest = value - high.astype(F32)
    mid = rest.astype(BF16)
    low = (rest - mid.astype(F32)).astype(BF16)
    return high, mid, low


def exact_left(ones, value):
    lanes = value.shape[1]
    found = nn(ones, jnp.concatenate(split3(value), axis=1))
    return found[:, :lanes] + found[:, lanes : 2 * lanes] + found[:, 2 * lanes :]


def three_in_lanes(value, heads):
    high, mid, low = split3(value)
    lane = lax.broadcasted_iota(jnp.int32, value.shape, 1)
    parts = jnp.where(
        lane < heads,
        high.astype(F32),
        jnp.where(lane < 2 * heads, mid.astype(F32), low.astype(F32)),
    )
    return parts.astype(BF16)


def spread_matrix(heads, head_size):
    shape = (LANES, heads * head_size)
    lane = lax.broadcasted_iota(jnp.int32, shape, 0)
    channel = lax.broadcasted_iota(jnp.int32, shape, 1)
    owner = channel // head_size
    hit = (lane == owner) | (lane == owner + heads) | (lane == owner + 2 * heads)
    return hit.astype(F32).astype(BF16)


def collect_matrix(heads, head_size):
    shape = (heads * head_size, LANES)
    lane = lax.broadcasted_iota(jnp.int32, shape, 1)
    owner = lax.broadcasted_iota(jnp.int32, shape, 0) // head_size
    hit = (lane == owner) | (lane == owner + heads) | (lane == owner + 2 * heads)
    return hit.astype(F32).astype(BF16)


def spaced_matrix(narrow, wide, narrow_shard, wide_shard, compress):
    shape = (wide, narrow) if compress else (narrow, wide)
    at_wide = lax.broadcasted_iota(jnp.int32, shape, 0 if compress else 1)
    at_narrow = lax.broadcasted_iota(jnp.int32, shape, 1 if compress else 0)
    owner, place = at_wide // wide_shard, at_wide % wide_shard
    hit = (place < narrow_shard) & (at_narrow == owner * narrow_shard + place)
    return hit.astype(F32).astype(BF16)


def pack_kernel(
    inner_ref, state_ref, step_ref, norm_ref, conv_ref, bias_ref, gate_ref, taps_ref,
    taps_bias_ref, out_ref, turned, lanes,
):
    shard, heads = step_ref.shape
    inner, states = inner_ref.shape[1], state_ref.shape[1]
    state_shard = taps_ref.shape[1]
    base = 3 * heads
    turned[...] = jnp.zeros_like(turned)
    turned[base : base + 1, 0:shard] = norm_ref[...].astype(F32)
    turned[base + 1 : base + 5, 0:shard] = conv_ref[...].astype(F32)
    turned[base + 5 : base + 6, 0:shard] = bias_ref[...].astype(F32)
    turned[base + 6 : base + 7, 0:shard] = gate_ref[...].astype(F32)
    turned[base + 8 : base + 12, 0:state_shard] = taps_ref[...].astype(F32)
    turned[base + 12 : base + 13, 0:state_shard] = taps_bias_ref[...].astype(F32)
    lanes[...] = jnp.zeros_like(lanes)
    step = step_ref[...].astype(F32)
    for copy in range(3):
        lanes[:, copy * heads : (copy + 1) * heads] = step
    out_ref[:, :inner] = inner_ref[...]
    out_ref[:, inner : inner + states] = state_ref[...]
    out_ref[:, inner + states :] = (turned[...].T[0:shard, :] + lanes[...]).astype(BF16)


def lower_matrix(upper=False):
    row = lax.broadcasted_iota(jnp.int32, (GROUP, GROUP), 0)
    col = lax.broadcasted_iota(jnp.int32, (GROUP, GROUP), 1)
    hit = (col >= row) if upper else (col <= row)
    return hit.astype(F32).astype(BF16)


def sequence_ends(len_ref):
    ends, total = [], jnp.int32(0)
    for slot in range(len_ref.shape[1]):
        total = total + len_ref[0, slot]
        ends.append(total)
    return ends


def sequence_of(ends, token):
    found = (token >= ends[0]).astype(jnp.int32)
    for end in ends[1:]:
        found = found + (token >= end).astype(jnp.int32)
    return found


def scalar_sequence_of(ends, token):
    found = jnp.where(token >= ends[0], 1, 0)
    for end in ends[1:]:
        found = found + jnp.where(token >= end, 1, 0)
    return found


def position_of(ends, token):
    start = jnp.zeros_like(token)
    for end in ends:
        start = jnp.where(token >= end, end, start)
    return token - start


def tokens_column(first, rows=GROUP):
    return first + lax.broadcasted_iota(jnp.int32, (rows, 1), 0)


def additive_mask(ends, first, transposed):
    rows = first + lax.broadcasted_iota(jnp.int32, (GROUP, GROUP), 0)
    cols = first + lax.broadcasted_iota(jnp.int32, (GROUP, GROUP), 1)
    ordered = (cols >= rows) if transposed else (rows >= cols)
    kept = (sequence_of(ends, rows) == sequence_of(ends, cols)) & ordered
    return jnp.where(kept, 0.0, MASKED)


def softplus(value):
    return jnp.maximum(value, 0.0) + jnp.log1p(jnp.exp(-jnp.abs(value)))


def sigmoid(value):
    return 0.5 * jnp.tanh(0.5 * value) + 0.5


def decay_terms(ends, first, step_in, rate, lower):
    group = first // GROUP
    step = softplus(step_in)
    cum = exact_left(lower, step * (rate * LOG2E))
    last = cum[GROUP - 1 : GROUP, :]
    sequence = sequence_of(ends, tokens_column(first))
    tail = scalar_sequence_of(ends, first + GROUP - 1)
    before = jnp.where(group > 0, scalar_sequence_of(ends, first - 1), -1)
    in_tail = (sequence == tail).astype(F32)
    entered = (sequence == before).astype(F32)
    carried = jnp.where(tail == before, 1.0, 0.0)
    key_factor = jnp.exp2(last - cum) * in_tail
    entry = jnp.exp2(cum) * entered
    decay = jnp.exp2(last) * carried
    return step, cum, key_factor, entry, decay


def head_masks():
    lane = lax.broadcasted_iota(jnp.int32, (1, LANES), 1)
    first = (lane < LANES // 2).astype(F32)
    return first, 1.0 - first


def forward_kernel(
    rank_ref, len_ref, own_ref, other_ref, w_ref, head_ref,
    normed_ref, normed_t_ref, ipre_ref, spre_ref, sact_ref, stepin_ref, mixed_ref, sprev_ref,
    rows_ref, taps_ref,
    ext, state, spread, lower, fac, read, mask, scores, weighted, *, shard, state_shard,
):
    inner = rows_ref.shape[1]
    channels = ext.shape[1]
    heads = inner // (LANES // PAIR_HEADS)
    size = sprev_ref.shape[0]
    group = pl.program_id(0)
    first = group * GROUP
    ends = sequence_ends(len_ref)

    @pl.when(group == 0)
    def _():
        ext[0:8, :] = jnp.zeros((8, channels), F32)
        state[...] = jnp.zeros_like(state)
        spread[...] = spread_matrix(heads, LANES // PAIR_HEADS)
        lower[...] = lower_matrix()
        packed = w_ref[:, channels:].astype(F32).T
        base = 3 * heads
        rows_ref[0:7, :] = packed[base : base + 7, :]
        once = lax.broadcasted_iota(jnp.int32, (16, LANES), 1) < heads
        skip_row = jnp.where(once, head_ref[2:3, :], 0.0).astype(BF16)
        rows_ref[7:8, :] = nn(skip_row, spread[...])[0:1, :]
        taps_ref[...] = nn(
            packed[base + 8 : base + 16, :].astype(BF16),
            spaced_matrix(2 * size, w_ref.shape[0], state_shard, shard, True),
        )

    mine = rank_ref[0, 0] == group // (pl.num_programs(0) // 2)
    gain = rows_ref[ROW_NORM : ROW_NORM + 1, :]
    for part in range(4):
        sl = slice(part * 64, part * 64 + 64)
        hidden = jnp.where(mine, own_ref[sl, :].astype(F32), other_ref[sl, :].astype(F32))
        inv = lax.rsqrt(jnp.mean(hidden * hidden, axis=1, keepdims=True) + NORM_EPS)
        normed_ref[sl, :] = (hidden * inv * gain).astype(BF16)

    normed_t_ref[...] = normed_ref[...].T
    pre = nn(normed_ref[...], w_ref[:, :inner])
    ext[8 : 8 + GROUP, 0:inner] = pre
    ipre_ref[...] = pre
    rest = nn(normed_ref[...], w_ref[:, inner:])
    ext[8 : 8 + GROUP, inner:channels] = rest[:, : 2 * size]
    spre_ref[...] = rest[:, : 2 * size]
    lane = lax.broadcasted_iota(jnp.int32, (1, LANES), 1)
    step_in = jnp.where(lane < 3 * heads, rest[:, 2 * size :], 0.0) + head_ref[0:1, :]
    stepin_ref[...] = step_in

    token = tokens_column(first)
    position = position_of(ends, token)
    keep = [(position >= offset).astype(F32) for offset in (1, 2, 3)]

    def conv(sl, taps, bias):
        total = bias + taps[3:4, :] * ext[8 : 8 + GROUP, sl]
        for offset in (1, 2, 3):
            total = total + keep[offset - 1] * (
                taps[3 - offset : 4 - offset, :] * ext[8 - offset : 8 - offset + GROUP, sl]
            )
        return total

    for part in range(2):
        sl = slice(inner + part * size, inner + (part + 1) * size)
        own = slice(part * size, (part + 1) * size)
        total = conv(sl, taps_ref[0:4, own], taps_ref[4:5, own])
        sact_ref[:, own] = (total * sigmoid(total)).astype(BF16)
    keys = sact_ref[:, :size]
    queries = sact_ref[:, size:]
    scores[...] = nt(queries, keys)
    mask[...] = additive_mask(ends, first, False)

    step, cum, key_factor, entry, decay = decay_terms(
        ends, first, step_in, head_ref[1:2, :], lower[...]
    )
    cum_rows = cum.T
    stacked = jnp.concatenate(
        [step, key_factor * step, entry, jnp.broadcast_to(decay, (16, LANES))], axis=0
    )
    fac[...] = nn(three_in_lanes(stacked, heads), spread[...])
    held = state[...].astype(BF16)
    sprev_ref[...] = held
    read[...] = nn(queries, held)

    masks = head_masks()
    for pair in range(inner // LANES):
        sl = slice(pair * LANES, (pair + 1) * LANES)
        total = conv(sl, rows_ref[ROW_TAP : ROW_TAP + 4, sl], rows_ref[ROW_BIAS : ROW_BIAS + 1, sl])
        values = (total * sigmoid(total)).astype(BF16).astype(F32)
        stepped = values * fac[0:GROUP, sl]
        weighted[:, sl] = (values * fac[GROUP : 2 * GROUP, sl]).astype(BF16)
        top, bottom, low_values, high_values = [], [], [], []
        for which in range(PAIR_HEADS):
            head = pair * PAIR_HEADS + which
            column = cum[:, head : head + 1]
            row = cum_rows[head : head + 1, :]

            def factor(rs, cs):
                gap = column[rs] - row[:, cs] + mask[rs, cs]
                return (jnp.exp2(gap) * scores[rs, cs]).astype(BF16)

            lo, hi = slice(0, HALF), slice(HALF, GROUP)
            top.append(factor(lo, lo))
            bottom.append(factor(hi, lo))
            bottom.append(factor(hi, hi))
            masked = (stepped * masks[which]).astype(BF16)
            low_values.append(masked[:HALF])
            high_values.append(masked)
        upper_part = nn(jnp.concatenate(top, axis=1), jnp.concatenate(low_values, axis=0))
        lower_part = nn(jnp.concatenate(bottom, axis=1), jnp.concatenate(high_values, axis=0))
        rest = fac[2 * GROUP : 3 * GROUP, sl] * read[:, sl] + (
            rows_ref[ROW_SKIP : ROW_SKIP + 1, sl] * values
        )
        mixed_ref[0:HALF, sl] = upper_part + rest[:HALF]
        mixed_ref[HALF:GROUP, sl] = lower_part + rest[HALF:]

    state[...] = fac[3 * GROUP : 3 * GROUP + 1, :] * state[...] + tn(keys, weighted[...])
    ext[0:8, :] = ext[GROUP : GROUP + 8, :]


def gate_kernel(
    rank_ref, len_ref, own_ref, other_ref, normed_ref, mixed_ref, w_ref, proj_ref, rows_ref,
    gate_ref, gol_ref, live_t_ref, sums_ref,
):
    group = pl.program_id(0)
    first = group * GROUP
    ends = sequence_ends(len_ref)
    mine = rank_ref[0, 0] == group // (pl.num_programs(0) // 2)
    valid = tokens_column(first) < ends[-1]
    cotangent = jnp.where(mine, own_ref[...].astype(F32), other_ref[...].astype(F32))
    live = jnp.where(valid, cotangent, 0.0).astype(BF16)
    live_t_ref[...] = live.T
    square = jnp.zeros((GROUP, LANES), F32)
    inner = jnp.zeros((GROUP, LANES), F32)
    for part in range(gate_ref.shape[1] // GROUP):
        sl = slice(part * GROUP, (part + 1) * GROUP)
        gate = nn(normed_ref[...], w_ref[:, sl])
        gol = nn(live, proj_ref[:, sl])
        gate_ref[:, sl] = gate
        gol_ref[:, sl] = gol
        gated = mixed_ref[:, sl] * (gate * sigmoid(gate))
        squares = gated * gated
        inners = gol * rows_ref[ROW_GATE : ROW_GATE + 1, sl] * gated
        square = square + squares[:, :LANES] + squares[:, LANES:]
        inner = inner + inners[:, :LANES] + inners[:, LANES:]
    lane = lax.broadcasted_iota(jnp.int32, (GROUP, LANES), 1)
    columns = jnp.where(
        lane < 4,
        jnp.sum(square, axis=1, keepdims=True),
        jnp.sum(inner, axis=1, keepdims=True),
    )
    sums_ref[...] = columns.T[0:8, :]


def gate_grad_kernel(
    own_sums_ref, other_sums_ref, gate_ref, gol_ref, mixed_ref, rows_ref,
    low_ref, first_ref, ggp_ref, gain_ref, *, inner_all,
):
    @pl.when(pl.program_id(0) == 0)
    def _():
        gain_ref[...] = jnp.zeros_like(gain_ref)

    totals = own_sums_ref[...] + other_sums_ref[...]
    columns = jnp.concatenate([totals, jnp.zeros((LANES - 8, GROUP), F32)], axis=0).T
    inv_all = lax.rsqrt(columns[:, 0:1] / inner_all + NORM_EPS)
    slope_all = inv_all * inv_all * inv_all * columns[:, 4:5] / inner_all
    gain = rows_ref[ROW_GATE : ROW_GATE + 1, :]
    for part in range(gate_ref.shape[1] // GROUP):
        sl = slice(part * GROUP, (part + 1) * GROUP)
        gain_row = gain[:, sl]
        total = jnp.zeros((8, GROUP), F32)
        for at in range(0, GROUP, 16):
            strip = slice(at, at + 16)
            inv, slope = inv_all[strip], slope_all[strip]
            gate, gol, mixed = gate_ref[strip, sl], gol_ref[strip, sl], mixed_ref[strip, sl]
            logistic = sigmoid(gate)
            silu = gate * logistic
            gated = mixed * silu
            scaled = gated * inv
            low_ref[strip, sl] = (scaled * gain_row).astype(BF16)
            product = gol * scaled
            total = total + product[0:8] + product[8:16]
            grad = inv * (gol * gain_row) - gated * slope
            first_ref[strip, sl] = (grad * silu).astype(BF16)
            ggp_ref[strip, sl] = (
                grad * mixed * (logistic * (1.0 + gate * (1.0 - logistic)))
            ).astype(BF16)
        gain_ref[0:1, sl] += jnp.sum(total, axis=0, keepdims=True)


def product_kernel(left_ref, right_ref, out_ref):
    out_ref[...] = nn(left_ref[...], right_ref[...]).astype(out_ref.dtype)


def normed_grad_kernel(
    begin_ref, gate_ref, inner_ref, step_ref, w_gate_ref, w_inner_ref, w_step_ref, out_ref
):
    total = nt(gate_ref[...], w_gate_ref[...]) + nt(inner_ref[...], w_inner_ref[...])
    out_ref[...] = (total + nt(step_ref[...], w_step_ref[...])).astype(out_ref.dtype)


def backward_kernel(
    len_ref, ipre_ref, halo_ref, sact_ref, stepin_ref, mixed_ref, first_ref, sprev_ref,
    rows_ref, head_ref,
    gip_ref, gkq_ref, gstep_ref, conv_ref, heads_ref,
    ext, cext, gstate, spread, collect, lower, upper, fac, reads, mask, scores, gscores,
    weighted, entered, sums,
):
    inner = rows_ref.shape[1]
    heads = inner // (LANES // PAIR_HEADS)
    size = sprev_ref.shape[0]
    turn = pl.program_id(0)
    group = pl.num_programs(0) - 1 - turn
    first = group * GROUP
    ends = sequence_ends(len_ref)

    @pl.when(turn == 0)
    def _():
        cext[GROUP : GROUP + 8, :] = jnp.zeros((8, inner), F32)
        gstate[...] = jnp.zeros_like(gstate)
        spread[...] = spread_matrix(heads, LANES // PAIR_HEADS)
        collect[...] = collect_matrix(heads, LANES // PAIR_HEADS)
        lower[...] = lower_matrix()
        upper[...] = lower_matrix(upper=True)
        conv_ref[...] = jnp.zeros_like(conv_ref)
        heads_ref[...] = jnp.zeros_like(heads_ref)

    ext[0:8, :] = jnp.where(group > 0, halo_ref[...], 0.0)
    ext[8 : 8 + GROUP, :] = ipre_ref[...]
    token = tokens_column(first)
    position = position_of(ends, token)
    keep = [(position >= offset).astype(F32) for offset in (1, 2, 3)]
    ahead = [(position_of(ends, token + offset) >= offset).astype(F32) for offset in (1, 2, 3)]

    step_in = stepin_ref[...]
    rate = head_ref[1:2, :]
    step, cum, key_factor, entry, decay = decay_terms(ends, first, step_in, rate, lower[...])
    cum_rows = cum.T
    key_step = key_factor * step
    stacked = jnp.concatenate(
        [step, key_step, entry, jnp.broadcast_to(decay, (16, LANES))], axis=0
    )
    fac[...] = nn(three_in_lanes(stacked, heads), spread[...])

    keys = sact_ref[:, :size]
    queries = sact_ref[:, size:]
    scores[...] = nt(keys, queries)
    mask[...] = additive_mask(ends, first, True)
    gscores[...] = jnp.zeros_like(gscores)
    held = gstate[...].astype(BF16)
    reads[...] = nn(keys, held)

    masks = head_masks()
    lo, hi = slice(0, HALF), slice(HALF, GROUP)
    for pair in range(inner // LANES):
        sl = slice(pair * LANES, (pair + 1) * LANES)
        taps = rows_ref[ROW_TAP : ROW_TAP + 4, sl]
        shifted = [ext[8 - offset : 8 - offset + GROUP, sl] for offset in range(4)]
        total = rows_ref[ROW_BIAS : ROW_BIAS + 1, sl] + taps[3:4, :] * shifted[0]
        for offset in (1, 2, 3):
            total = total + keep[offset - 1] * (taps[3 - offset : 4 - offset, :] * shifted[offset])
        logistic = sigmoid(total)
        values = (total * logistic).astype(BF16).astype(F32)
        slope = logistic * (1.0 + total * (1.0 - logistic))
        step_wide = fac[0:GROUP, sl]
        key_wide = fac[GROUP : 2 * GROUP, sl]
        stepped = (values * step_wide).astype(BF16)
        stepped_wide = stepped.astype(F32)
        weighted[:, sl] = (values * key_wide).astype(BF16)
        upstream = first_ref[:, sl]
        upstream_wide = upstream.astype(F32)
        entered[:, sl] = (upstream_wide * fac[2 * GROUP : 3 * GROUP, sl]).astype(BF16)

        top, bottom, top_grads, low_grads = [], [], [], []
        g00 = g01 = g11 = None
        split_up = [(upstream_wide * one).astype(BF16) for one in masks]
        grads_low = nt(stepped[HALF:], jnp.concatenate([one[HALF:] for one in split_up], axis=0))
        for which in range(PAIR_HEADS):
            head = pair * PAIR_HEADS + which
            column = cum[:, head : head + 1]
            row = cum_rows[head : head + 1, :]
            masked = split_up[which]
            grads_top = nt(stepped[:HALF], masked)

            def factors(rs, cs, grads):
                gap = row[:, cs] - column[rs] + mask[rs, cs]
                factor = jnp.exp2(gap)
                return (factor * scores[rs, cs]).astype(BF16), factor * grads

            a00, d00 = factors(lo, lo, grads_top[:, lo])
            a01, d01 = factors(lo, hi, grads_top[:, hi])
            a11, d11 = factors(hi, hi, grads_low[:, which * HALF : (which + 1) * HALF])
            g00 = d00 if g00 is None else g00 + d00
            g01 = d01 if g01 is None else g01 + d01
            g11 = d11 if g11 is None else g11 + d11
            top.extend([a00, a01])
            bottom.append(a11)
            top_grads.append(masked)
            low_grads.append(masked[HALF:])
        gscores[lo, lo] += g00
        gscores[lo, hi] += g01
        gscores[hi, hi] += g11
        raw = jnp.concatenate(
            [
                nn(jnp.concatenate(top, axis=1), jnp.concatenate(top_grads, axis=0)),
                nn(jnp.concatenate(bottom, axis=1), jnp.concatenate(low_grads, axis=0)),
            ],
            axis=0,
        )
        skip = rows_ref[ROW_SKIP : ROW_SKIP + 1, sl]
        across = reads[:, sl]

        balance = upstream_wide * (mixed_ref[:, sl] - skip * values) - stepped_wide * raw
        high = balance.astype(BF16)
        sums[0:GROUP, sl] = high
        sums[GROUP : 2 * GROUP, sl] = (balance - high.astype(F32)).astype(BF16)
        sums[2 * GROUP : 3 * GROUP, sl] = (values * raw).astype(BF16)
        sums[3 * GROUP : 4 * GROUP, sl] = (values * across).astype(BF16)
        conv_ref[5:6, sl] += jnp.sum(upstream_wide * values, axis=0, keepdims=True)
        inner_grad = step_wide * raw + key_wide * across + skip * upstream_wide
        grad = inner_grad * slope
        cext[0:GROUP, sl] = grad
        conv_ref[3:4, sl] += jnp.sum(grad * shifted[0], axis=0, keepdims=True)
        conv_ref[4:5, sl] += jnp.sum(grad, axis=0, keepdims=True)
        result = taps[3:4, :] * grad
        for offset in (1, 2, 3):
            conv_ref[3 - offset : 4 - offset, sl] += jnp.sum(
                keep[offset - 1] * grad * shifted[offset], axis=0, keepdims=True
            )
            result = result + ahead[offset - 1] * (
                taps[3 - offset : 4 - offset, :] * cext[offset : offset + GROUP, sl]
            )
        gip_ref[:, sl] = result.astype(BF16)

    cext[GROUP : GROUP + 8, :] = cext[0:8, :]
    state = sprev_ref[...]
    grad_scores = gscores[...].astype(BF16)
    gkq_ref[:, :size] = (nn(grad_scores, queries) + nt(weighted[...], held)).astype(BF16)
    gkq_ref[:, size:] = (tn(grad_scores, keys) + nt(entered[...], state)).astype(BF16)

    collected = nn(sums[...], collect[...])
    balance = collected[:GROUP] + collected[GROUP : 2 * GROUP]
    direct = collected[2 * GROUP : 3 * GROUP]
    key_dot = collected[3 * GROUP :]

    def row_collect(value):
        high = value.astype(BF16)
        low = (value - high.astype(F32)).astype(BF16)
        rows16 = jnp.concatenate(
            [jnp.broadcast_to(high, (8, inner)), jnp.broadcast_to(low, (8, inner))], axis=0
        )
        found = nn(rows16, collect[...])
        return found[0:1, :] + found[8:9, :]

    carry_term = decay * row_collect(
        jnp.sum(gstate[...] * state.astype(F32), axis=0, keepdims=True)
    )
    moved = key_step * key_dot
    grad_log = (
        exact_left(upper[...], balance) + carry_term + exact_left(lower[...], moved) - moved
    )
    grad_step = direct + key_factor * key_dot + grad_log * rate
    lane = lax.broadcasted_iota(jnp.int32, (1, LANES), 1)
    grad_step_in = jnp.where(lane < heads, grad_step * sigmoid(step_in), 0.0)
    gstep_ref[...] = grad_step_in.astype(BF16)
    heads_ref[0:1, :] += jnp.sum(grad_log * step * rate, axis=0, keepdims=True)
    heads_ref[1:2, :] += jnp.sum(grad_step_in, axis=0, keepdims=True)
    gstate[...] = fac[3 * GROUP : 3 * GROUP + 1, :] * gstate[...] + tn(queries, entered[...])

    @pl.when(turn == pl.num_programs(0) - 1)
    def _():
        heads_ref[2:3, :] = row_collect(conv_ref[5:6, :])


def state_grad_kernel(
    rank_ref, len_ref, own_ref, other_ref, spre_ref, taps_ref, normed_t_ref, gstep_ref,
    inner_rows_ref, gain_ref, heads_ref,
    gsp_ref, rest_ref, conv_ref, ext, cext, turned, *, shard, state_shard, heads,
):
    rows, channels = own_ref.shape
    width = rest_ref.shape[0]
    half = rows - HALO
    rank = rank_ref[0, 0]
    base = pl.multiple_of(rank * (half - HALO), HALO)
    chunk = window_chunk(rows)
    ends = sequence_ends(len_ref)
    before = spre_ref[pl.ds(pl.multiple_of(jnp.maximum(base - 8, 0), 8), 8), :]
    ext[0:8, :] = jnp.where(rank > 0, before, 0.0)
    ext[8 : 8 + rows, :] = spre_ref[pl.ds(base, rows), :]
    cext[rows : rows + 8, :] = jnp.zeros((8, channels), F32)
    conv_ref[...] = jnp.zeros_like(conv_ref)
    gsp_ref[...] = jnp.zeros_like(gsp_ref)
    for at in range(0, rows, chunk):
        token = tokens_column(base + at, chunk)
        position = position_of(ends, token)
        owned = ((token >= rank * half) & (token < (rank + 1) * half)).astype(F32)
        keep = [(position >= offset).astype(F32) for offset in (1, 2, 3)]
        for part in range(channels // LANES):
            sl = slice(part * LANES, (part + 1) * LANES)
            shifted = [ext[at + 8 - offset : at + 8 - offset + chunk, sl] for offset in range(4)]
            total = taps_ref[4:5, sl] + taps_ref[3:4, sl] * shifted[0]
            for offset in (1, 2, 3):
                total = total + keep[offset - 1] * (
                    taps_ref[3 - offset : 4 - offset, sl] * shifted[offset]
                )
            logistic = sigmoid(total)
            slope = logistic * (1.0 + total * (1.0 - logistic))
            upstream = own_ref[at : at + chunk, sl].astype(F32) + other_ref[
                at : at + chunk, sl
            ].astype(F32)
            grad = upstream * slope
            cext[at : at + chunk, sl] = grad
            grad = grad * owned
            conv_ref[4:5, sl] += jnp.sum(grad, axis=0, keepdims=True)
            conv_ref[3:4, sl] += jnp.sum(grad * shifted[0], axis=0, keepdims=True)
            for offset in (1, 2, 3):
                conv_ref[3 - offset : 4 - offset, sl] += jnp.sum(
                    keep[offset - 1] * grad * shifted[offset], axis=0, keepdims=True
                )
    for at in range(0, rows, chunk):
        token = tokens_column(base + at, chunk)
        owned = ((token >= rank * half) & (token < (rank + 1) * half)).astype(F32)
        ahead = [
            (position_of(ends, token + offset) >= offset).astype(F32) for offset in (1, 2, 3)
        ]
        for part in range(channels // LANES):
            sl = slice(part * LANES, (part + 1) * LANES)
            result = taps_ref[3:4, sl] * cext[at : at + chunk, sl]
            for offset in (1, 2, 3):
                result = result + ahead[offset - 1] * (
                    taps_ref[3 - offset : 4 - offset, sl]
                    * cext[at + offset : at + offset + chunk, sl]
                )
            place = pl.ds(pl.multiple_of(base + at, HALO), chunk)
            gsp_ref[place, sl] = (result * owned).astype(BF16)
    rest_ref[:, :channels] = nn(normed_t_ref[...], gsp_ref[...]).astype(BF16)
    step_part = nn(normed_t_ref[...], gstep_ref[...])
    turned[...] = jnp.zeros_like(turned)
    turned[LANE_CONV : LANE_CONV + 5, :] = inner_rows_ref[0:5, :]
    turned[LANE_GATE : LANE_GATE + 1, :] = gain_ref[0:1, :]
    turned[LANE_STATE : LANE_STATE + 8, :] = nn(
        conv_ref[...].astype(BF16), spaced_matrix(channels, width, state_shard, shard, False)
    )
    columns = jnp.concatenate([heads_ref[...], jnp.zeros((LANES - 8, LANES), F32)], axis=0).T
    for which in range(3):
        start = LANE_HEADS + which * heads
        turned[start : start + heads, :] = jnp.broadcast_to(
            columns[0:heads, which : which + 1], (heads, width)
        )
    rest_ref[:, channels:] = (step_part + turned[...].T).astype(BF16)


def window_chunk(rows):
    return max(n for n in range(HALO, GROUP + 1, HALO) if rows % n == 0)


def finish_kernel(
    first_ref, inner_ref, rest_ref, weight_ref, state_ref, step_ref, pgi_ref, packed_ref
):
    width = first_ref.shape[1]
    states = state_ref.shape[1]
    heads = step_ref.shape[1]
    shard = step_ref.shape[0]
    gate = first_ref[...].astype(F32)
    inner = inner_ref[...]
    rest = rest_ref[...]
    pgi_ref[:, 0:1, :] = gate[:, None, :]
    pgi_ref[:, 1:2, :] = inner[:, None, :]
    weight = weight_ref[...].astype(F32)
    product = jnp.sum(gate * weight[:, :width] + inner * weight[:, width:], axis=1, keepdims=True)
    product += jnp.sum(rest[:, :states] * state_ref[...].astype(F32), axis=1, keepdims=True)
    small = rest[:, states:]
    product += jnp.sum(small[:, :heads] * step_ref[...].astype(F32), axis=1, keepdims=True)
    lane = lax.broadcasted_iota(jnp.int32, (shard, LANES), 1)
    packed_ref[:, :states] = rest[:, :states]
    packed_ref[:, states:] = jnp.where(lane == LANE_GAIN, product, small)


def unpack_kernel(
    own_ref, other_ref, norm_ref,
    state_ref, step_ref, gain_ref, conv_ref, bias_ref, taps_ref, taps_bias_ref,
    decay_ref, skip_ref, step_bias_ref, gate_ref,
):
    shard, states = state_ref.shape
    heads = step_ref.shape[1]
    state_shard = taps_ref.shape[1]
    state_ref[...] = own_ref[:, :states] + other_ref[:, :states]
    small = own_ref[:, states:]
    both = small + other_ref[:, states:]
    step_ref[...] = small[:, :heads]

    def turn(value):
        if shard < LANES:
            value = jnp.concatenate([value, jnp.zeros((LANES - shard, LANES), F32)], axis=0)
        return value.T

    small_rows, both_rows = turn(small), turn(both)
    gain_ref[...] = both_rows[LANE_GAIN : LANE_GAIN + 1, :shard] / norm_ref[...].astype(F32)
    conv_ref[...] = small_rows[LANE_CONV : LANE_CONV + 4, :shard]
    bias_ref[...] = small_rows[LANE_CONV + 4 : LANE_CONV + 5, :shard]
    gate_ref[...] = small_rows[LANE_GATE : LANE_GATE + 1, :shard]
    taps_ref[...] = both_rows[LANE_STATE : LANE_STATE + 4, :state_shard]
    taps_bias_ref[...] = both_rows[LANE_STATE + 4 : LANE_STATE + 5, :state_shard]
    first = small[0:8, :]
    for which, out_ref in enumerate((decay_ref, step_bias_ref, skip_ref)):
        start = LANE_HEADS + which * heads
        out_ref[...] = pltpu.roll(first, LANES - start, 1)[0:1, :heads]


def shape_of(dims, dtype):
    return jax.ShapeDtypeStruct(dims, dtype)


def params(**kwargs):
    return pltpu.CompilerParams(vmem_limit_bytes=VMEM_BYTES, **kwargs)


def cost(micros):
    return pl.CostEstimate(flops=int(micros * 1.1e9), bytes_accessed=0, transcendentals=0)


SMEM_SPEC = pl.BlockSpec(memory_space=pltpu.SMEM)


def whole(*dims):
    return pl.BlockSpec(dims, lambda i: (0,) * len(dims))


def bit_order(count, spread_first):
    bits = list(range(count.bit_length() - 1))
    return [0] + bits[2:] + [1] if spread_first and len(bits) > 1 else bits


def flip(value, bit, count):
    return lax.ppermute(value, "dp", [(i, i ^ (1 << bit)) for i in range(count)])


def after(value, *others):
    return lax.optimization_barrier((value, *others))[0]


def gather_by_bits(value, rank, count, spread_first, waits):
    held, begun = [], []
    rows, lanes = value.shape
    for bit in reversed(bit_order(count, spread_first)):
        if 0 < len(begun) <= len(waits):
            value = after(value, waits[len(begun) - 1])
        begun.append(value)
        other = flip(value, bit, count)
        held = sorted(held + [bit], reverse=True)
        low = (rank >> bit) & 1 == 0
        value = jnp.stack(
            [jnp.where(low, value, other), jnp.where(low, other, value)], axis=held.index(bit)
        )
    return value.reshape(count * rows, lanes), begun


class HalvingSum:
    def __init__(self, value, rank, count, spread_first):
        self.rank, self.count = rank, count
        self.left = list(reversed(range(count.bit_length() - 1)))
        self.order = bit_order(count, spread_first)
        rows = value.shape[0] // count
        self.value = value.reshape([2] * len(self.left) + [rows, value.shape[1]])

    def start(self):
        bit = self.order.pop(0)
        axis = self.left.index(bit)
        mine = (self.rank >> bit) & 1
        self.away = lax.dynamic_index_in_dim(self.value, 1 - mine, axis, keepdims=False)
        self.here = lax.dynamic_index_in_dim(self.value, mine, axis, keepdims=False)
        self.came = flip(self.away, bit, self.count)
        self.bit = bit

    def step(self, *others):
        if not self.left:
            return
        came = after(self.came, *others) if others else self.came
        self.left.remove(self.bit)
        self.value = self.here.astype(F32) + came.astype(F32)
        if self.left:
            self.value = self.value.astype(BF16)
            self.start()


def on_device(
    hidden_in,
    norm_gain,
    projection_gate_inner,
    proj_state,
    proj_step,
    conv_inner,
    conv_inner_bias,
    conv_state,
    conv_state_bias,
    decay_log,
    skip_gain,
    step_bias,
    gate_gain,
    proj_out,
    lengths,
    cotangent,
):
    tensor_count = lax.axis_size("tensor")
    tensor_rank = lax.axis_index("tensor")
    shard_rank = lax.axis_index("dp")
    shard_count = lax.axis_size("dp")
    half_rows, width = hidden_in.shape
    tokens = half_rows * tensor_count
    groups = tokens // GROUP
    half_groups = groups // 2
    inner = proj_out.shape[0]
    inner_all = inner * tensor_count
    heads = decay_log.shape[0]
    head_size = inner // heads
    size = proj_state.shape[1] // 2
    taps = conv_inner.shape[0]
    shard = width // shard_count
    channels = inner + 2 * size
    swap = [(0, 1), (1, 0)]

    def exchange(value):
        return lax.ppermute(value, "tensor", swap)

    pieces = []
    cuts = [0, half_rows // 6, half_rows * 5 // 12, half_rows]
    for begin, end in zip(cuts, cuts[1:]):
        piece = hidden_in[begin:end]
        pieces.append(exchange(after(piece, pieces[-1]) if pieces else piece))
    hidden_other = jnp.concatenate(pieces, axis=0)
    cotangent_other = exchange(after(cotangent, pieces[-1]))

    state_shard = conv_state.shape[1]
    first_shard = pl.pallas_call(
        pack_kernel,
        in_specs=[pl.BlockSpec(memory_space=pltpu.VMEM)] * 9,
        out_specs=pl.BlockSpec(memory_space=pltpu.VMEM),
        out_shape=shape_of((shard, channels + LANES), BF16),
        scratch_shapes=[
            pltpu.VMEM((LANES, max(LANES, shard)), F32),
            pltpu.VMEM((shard, LANES), F32),
        ],
        compiler_params=params(),
        cost_estimate=cost(0),
        name="pack_small",
    )(
        projection_gate_inner[:, 1], proj_state, proj_step, norm_gain[None, :], conv_inner.reshape(taps, shard),
        conv_inner_bias, gate_gain, conv_state, conv_state_bias[None, :],
    )
    w_first, begun = gather_by_bits(first_shard, shard_rank, shard_count, False, pieces)
    second_shard = jnp.concatenate([projection_gate_inner[:, 0], proj_out.T], axis=1)
    second_shard = after(second_shard, begun[min(2, len(begun) - 1)])
    w_second = lax.all_gather(second_shard, "dp", axis=0, tiled=True)
    w_out = w_second[:, inner:]

    rate = -jnp.exp(decay_log.astype(F32))
    head_rows = jnp.stack([step_bias.astype(F32), rate, skip_gain.astype(F32)])
    head_rows = jnp.pad(jnp.tile(head_rows, (1, 3)), ((0, 5), (0, LANES - 3 * heads)))
    rank = tensor_rank.astype(jnp.int32).reshape(1, 1)

    def by_group(lanes):
        return pl.BlockSpec((GROUP, lanes), lambda i: (i, 0))

    half_block = pl.BlockSpec((GROUP, width), lambda i: (i % half_groups, 0))
    (
        normed, normed_t, inner_pre, state_pre, state_act, step_in, mixed, prev_states, rows,
        state_rows,
    ) = pl.pallas_call(
        functools.partial(forward_kernel, shard=shard, state_shard=state_shard),
        grid=(groups,),
        in_specs=[
            SMEM_SPEC, SMEM_SPEC, half_block, half_block,
            whole(width, channels + LANES), whole(8, LANES),
        ],
        out_specs=[
            by_group(width), pl.BlockSpec((width, GROUP), lambda i: (0, i)), by_group(inner), by_group(2 * size), by_group(2 * size),
            by_group(LANES), by_group(inner), pl.BlockSpec((size, inner), lambda i: (i, 0)),
            whole(8, inner), whole(8, 2 * size),
        ],
        out_shape=[
            shape_of((tokens, width), BF16),
            shape_of((width, tokens), BF16),
            shape_of((tokens, inner), F32),
            shape_of((tokens, 2 * size), F32),
            shape_of((tokens, 2 * size), BF16),
            shape_of((tokens, LANES), F32),
            shape_of((tokens, inner), F32),
            shape_of((groups * size, inner), BF16),
            shape_of((8, inner), F32),
            shape_of((8, 2 * size), F32),
        ],
        scratch_shapes=[
            pltpu.VMEM((GROUP + 8, channels), F32),
            pltpu.VMEM((size, inner), F32),
            pltpu.VMEM((LANES, inner), BF16),
            pltpu.VMEM((GROUP, GROUP), BF16),
            pltpu.VMEM((3 * GROUP + 16, inner), F32),
            pltpu.VMEM((GROUP, inner), F32),
            pltpu.VMEM((GROUP, GROUP), F32),
            pltpu.VMEM((GROUP, GROUP), F32),
            pltpu.VMEM((GROUP, inner), BF16),
        ],
        compiler_params=params(),
        cost_estimate=cost(2),
        name="mixer_forward",
    )(rank, lengths, hidden_in, hidden_other, w_first, head_rows)

    gate_pre, grad_out_low, live_t, sums = pl.pallas_call(
        gate_kernel,
        grid=(groups,),
        in_specs=[
            SMEM_SPEC, SMEM_SPEC, half_block, half_block, by_group(width), by_group(inner),
            pl.BlockSpec((width, inner), lambda i: (0, 0)),
            pl.BlockSpec((width, inner), lambda i: (0, 1)),
            whole(8, inner),
        ],
        out_specs=[
            by_group(inner), by_group(inner), pl.BlockSpec((width, GROUP), lambda i: (0, i)),
            pl.BlockSpec((8, GROUP), lambda i: (0, i)),
        ],
        out_shape=[
            shape_of((tokens, inner), F32),
            shape_of((tokens, inner), F32),
            shape_of((width, tokens), BF16),
            shape_of((8, tokens), F32),
        ],
        compiler_params=params(),
        cost_estimate=cost(16),
        name="gate_forward",
    )(rank, lengths, cotangent, cotangent_other, normed, mixed, w_second, w_second, rows)

    sums_other = exchange(sums)
    sum_block = pl.BlockSpec((8, GROUP), lambda i: (0, i))
    out_low, grad_first, grad_gate_low, gain_rows = pl.pallas_call(
        functools.partial(gate_grad_kernel, inner_all=inner_all),
        grid=(groups,),
        in_specs=[
            sum_block, sum_block, by_group(inner), by_group(inner), by_group(inner),
            whole(8, inner),
        ],
        out_specs=[by_group(inner), by_group(inner), by_group(inner), whole(8, inner)],
        out_shape=[
            shape_of((tokens, inner), BF16),
            shape_of((tokens, inner), BF16),
            shape_of((tokens, inner), BF16),
            shape_of((8, inner), F32),
        ],
        compiler_params=params(),
        cost_estimate=cost(13),
        name="gate_backward",
    )(sums, sums_other, gate_pre, grad_out_low, mixed, rows)

    first_grads = jnp.concatenate(
        [nn(live_t, out_low).astype(BF16), nn(normed_t, grad_gate_low).astype(BF16)], axis=1
    )
    def rows_of(value, which):
        return lax.dynamic_slice_in_dim(value, which * half_rows, half_rows)

    first_sum = lax.psum_scatter(first_grads, "dp", scatter_dimension=0, tiled=True)
    out_low = after(out_low, first_grads)
    mix_away = nt(rows_of(out_low, 1 - tensor_rank), w_out).astype(BF16)
    grad_first = after(grad_first, mix_away)
    mix_other = exchange(mix_away)
    last = groups - 1
    grad_inner_low, grad_kq, grad_step_low, conv_rows, head_sums = pl.pallas_call(
        backward_kernel,
        grid=(groups,),
        in_specs=[
            SMEM_SPEC,
            pl.BlockSpec((GROUP, inner), lambda i: (last - i, 0)),
            pl.BlockSpec(
                (8, inner), lambda i: (jnp.maximum((last - i) * (GROUP // 8) - 1, 0), 0)
            ),
            pl.BlockSpec((GROUP, 2 * size), lambda i: (last - i, 0)),
            pl.BlockSpec((GROUP, LANES), lambda i: (last - i, 0)),
            pl.BlockSpec((GROUP, inner), lambda i: (last - i, 0)),
            pl.BlockSpec((GROUP, inner), lambda i: (last - i, 0)),
            pl.BlockSpec((size, inner), lambda i: (last - i, 0)),
            whole(8, inner), whole(8, LANES),
        ],
        out_specs=[
            pl.BlockSpec((GROUP, inner), lambda i: (last - i, 0)),
            pl.BlockSpec((GROUP, 2 * size), lambda i: (last - i, 0)),
            pl.BlockSpec((GROUP, LANES), lambda i: (last - i, 0)),
            whole(8, inner), whole(8, LANES),
        ],
        out_shape=[
            shape_of((tokens, inner), BF16),
            shape_of((tokens, 2 * size), BF16),
            shape_of((tokens, LANES), BF16),
            shape_of((8, inner), F32),
            shape_of((8, LANES), F32),
        ],
        scratch_shapes=[
            pltpu.VMEM((GROUP + 8, inner), F32),
            pltpu.VMEM((GROUP + 8, inner), F32),
            pltpu.VMEM((size, inner), F32),
            pltpu.VMEM((LANES, inner), BF16),
            pltpu.VMEM((inner, LANES), BF16),
            pltpu.VMEM((GROUP, GROUP), BF16),
            pltpu.VMEM((GROUP, GROUP), BF16),
            pltpu.VMEM((3 * GROUP + 16, inner), F32),
            pltpu.VMEM((GROUP, inner), F32),
            pltpu.VMEM((GROUP, GROUP), F32),
            pltpu.VMEM((GROUP, GROUP), F32),
            pltpu.VMEM((GROUP, GROUP), F32),
            pltpu.VMEM((GROUP, inner), BF16),
            pltpu.VMEM((GROUP, inner), BF16),
            pltpu.VMEM((4 * GROUP, inner), BF16),
        ],
        compiler_params=params(),
        cost_estimate=cost(2),
        name="mixer_backward",
    )(
        lengths, inner_pre, inner_pre, state_act, step_in, mixed, grad_first, prev_states,
        rows, head_rows,
    )

    window = half_rows + HALO
    kq_own = lax.dynamic_slice_in_dim(grad_kq, tensor_rank * (half_rows - HALO), window)
    kq_away = lax.dynamic_slice_in_dim(grad_kq, (1 - tensor_rank) * (half_rows - HALO), window)
    kq_other = exchange(kq_away)

    grad_inner_low = after(grad_inner_low, mix_other)
    inner_grads = pl.pallas_call(
        product_kernel,
        grid=(inner // GROUP,),
        in_specs=[whole(width, tokens), pl.BlockSpec((tokens, GROUP), lambda i: (0, i))],
        out_specs=pl.BlockSpec((width, GROUP), lambda i: (0, i)),
        out_shape=shape_of((width, inner), BF16),
        compiler_params=params(),
        cost_estimate=cost(0),
        name="inner_weight_grads",
    )(normed_t, grad_inner_low)
    inner_sum = HalvingSum(inner_grads, shard_rank, shard_count, False)
    inner_sum.start()

    def normed_part(which, gip, dtype):
        def block(i, begin):
            return (begin[0] + i, 0)

        return pl.pallas_call(
            normed_grad_kernel,
            grid_spec=pltpu.PrefetchScalarGridSpec(
                num_scalar_prefetch=1,
                grid=(half_groups,),
                in_specs=[
                    pl.BlockSpec((GROUP, inner), block),
                    pl.BlockSpec((GROUP, inner), block),
                    pl.BlockSpec((GROUP, LANES), block),
                    pl.BlockSpec((width, inner), lambda i, begin: (0, 0)),
                    pl.BlockSpec((width, inner), lambda i, begin: (0, 0)),
                    pl.BlockSpec((width, LANES), lambda i, begin: (0, channels // LANES)),
                ],
                out_specs=pl.BlockSpec((GROUP, width), lambda i, begin: (i, 0)),
            ),
            out_shape=shape_of((half_rows, width), dtype),
            compiler_params=params(),
            cost_estimate=cost(0),
            name="normed_grads",
        )(
            (which * half_groups).astype(jnp.int32).reshape(1),
            grad_gate_low, gip, grad_step_low, w_second, w_first, w_first,
        )

    grad_inner_low, first_sum, _ = lax.optimization_barrier(
        (grad_inner_low, first_sum, inner_sum.away)
    )
    normed_away = normed_part(1 - tensor_rank, grad_inner_low, BF16)
    normed_other = exchange(normed_away)
    inner_sum.step()
    vmem = pl.BlockSpec(memory_space=pltpu.VMEM)
    kq_other = after(kq_other, normed_away, inner_sum.away)
    grad_state_low, rest_grads = pl.pallas_call(
        functools.partial(
            state_grad_kernel, shard=shard, state_shard=state_shard, heads=heads
        ),
        in_specs=[SMEM_SPEC, SMEM_SPEC] + [vmem] * 9,
        out_specs=[vmem] * 2,
        out_shape=[shape_of((tokens, 2 * size), BF16), shape_of((width, 2 * size + LANES), BF16)],
        scratch_shapes=[
            pltpu.VMEM((8, 2 * size), F32),
            pltpu.VMEM((window + 8, 2 * size), F32),
            pltpu.VMEM((window + 8, 2 * size), F32),
            pltpu.VMEM((LANES, width), F32),
        ],
        compiler_params=params(),
        cost_estimate=cost(0),
        name="state_backward",
    )(
        rank, lengths, kq_own, kq_other, state_pre, state_rows, normed_t, grad_step_low,
        conv_rows, gain_rows, head_sums,
    )
    rest_sum = HalvingSum(rest_grads, shard_rank, shard_count, True)
    rest_sum.start()
    inner_sum.step(rest_sum.away)
    normed_here = normed_part(
        tensor_rank, after(grad_inner_low, rest_sum.away, inner_sum.away), F32
    )
    rest_sum.step(inner_sum.away, normed_here)
    gap = rest_sum.away
    inner_sum.step(gap, normed_other)
    while inner_sum.left or rest_sum.left:
        rest_sum.step(inner_sum.away)
        inner_sum.step()
    inner_sum, rest_sum = inner_sum.value, rest_sum.value

    mix_here = nt(rows_of(after(out_low, gap), tensor_rank), w_out)
    mix = mix_here + after(mix_other, gap).astype(F32)
    slot = tensor_rank * half_rows + jnp.arange(half_rows, dtype=jnp.int32)
    valid_half = slot < jnp.sum(lengths[0])
    hidden_wide = hidden_in.astype(F32)
    block_out = (hidden_wide + jnp.where(valid_half[:, None], mix, 0.0)).astype(BF16)


    grad_normed = normed_here + normed_other.astype(F32)
    grad_normed = grad_normed + nt(
        rows_of(grad_state_low, tensor_rank), w_first[:, inner:channels]
    )
    gain = rows[ROW_NORM][None, :]
    inv_rms = lax.rsqrt(jnp.mean(hidden_wide * hidden_wide, axis=1, keepdims=True) + NORM_EPS)
    scaled_in = grad_normed * gain
    grad_hidden = (
        inv_rms * scaled_in
        - hidden_wide * inv_rms**3 * jnp.mean(scaled_in * hidden_wide, axis=1, keepdims=True)
        + cotangent.astype(F32)
    )

    grad_pgi, packed = pl.pallas_call(
        finish_kernel,
        in_specs=[vmem] * 6,
        out_specs=[vmem] * 2,
        out_shape=[shape_of((shard, 2, inner), F32), shape_of((shard, 2 * size + LANES), F32)],
        compiler_params=params(),
        cost_estimate=cost(1),
        name="finish",
    )(
        first_sum[:, inner:], inner_sum, rest_sum,
        projection_gate_inner.reshape(shard, 2 * inner), proj_state, proj_step,
    )
    (
        grad_state, grad_step, grad_gain, grad_conv, grad_bias, grad_taps, grad_taps_bias,
        grad_decay, grad_skip, grad_step_bias, grad_gate_gain,
    ) = pl.pallas_call(
        unpack_kernel,
        in_specs=[vmem] * 3,
        out_specs=[vmem] * 11,
        out_shape=[
            shape_of(dims, F32)
            for dims in (
                (shard, 2 * size), (shard, heads), (1, shard), (taps, shard), (1, shard),
                (taps, state_shard), (1, state_shard), (1, heads), (1, heads), (1, heads),
                (1, shard),
            )
        ],
        compiler_params=params(),
        cost_estimate=cost(1),
        name="unpack_small",
    )(packed, exchange(packed), norm_gain[None, :])
    return (
        block_out,
        grad_hidden,
        grad_gain[0],
        grad_pgi,
        grad_state,
        grad_step,
        grad_conv[:, None, :],
        grad_bias,
        grad_taps,
        grad_taps_bias[0],
        grad_decay[0],
        grad_skip[0],
        grad_step_bias[0],
        grad_gate_gain,
        first_sum[:, :inner].astype(F32).T,
    )


def solution(mesh):
    placed = (
        P(("dp", "tensor"), None),
        P("dp"),
        P("dp", None, "tensor"),
        P("dp", None),
        P("dp", "tensor"),
        P(None, "tensor", "dp"),
        P("tensor", "dp"),
        P(None, "dp"),
        P("dp"),
        P("tensor"),
        P("tensor"),
        P("tensor"),
        P("tensor", "dp"),
        P("tensor", "dp"),
        P("dp", None),
        P(("dp", "tensor"), None),
    )
    return jax.shard_map(
        on_device,
        mesh=mesh,
        in_specs=placed,
        out_specs=(
            P(("dp", "tensor"), None),
            P(("dp", "tensor"), None),
            P("dp"),
            P("dp", None, "tensor"),
            P("dp", None),
            P("dp", "tensor"),
            P(None, "tensor", "dp"),
            P("tensor", "dp"),
            P(None, "dp"),
            P("dp"),
            P("tensor"),
            P("tensor"),
            P("tensor"),
            P("tensor", "dp"),
            P("tensor", "dp"),
        ),
        check_vma=False,
    )
```
